128 devices in a mesh: slide: 8 (over z, core), tile: 16 (over y, x).
Axes of the slice: x: 4, y: 4, z: 4, core: 2. Of those that a mesh axis runs over, the one named last changes fastest.
Arguments:
- tile_features: bfloat16 [49152, 1536], P(('slide', 'tile')), may hold values from -8 to 8
- embed_weight: bfloat16 [1536, 768], replicated, may hold values from -0.15625 to 0.15625
- qkv_weight: bfloat16 [768, 2304], replicated, may hold values from -0.21875 to 0.21875
- positions: int32 [49152], P(('slide', 'tile')), may hold values from -1 to 16383, as said below
- out_grad: bfloat16 [4, 4096, 768], P(None, 'slide', 'tile'), may hold values from -48 to 48
Outputs:
- feature_grad: bfloat16 [49152, 1536], P(('slide', 'tile'))
- embed_grad: float32 [1536, 768], P('slide', 'tile')
- qkv_grad: float32 [768, 2304], P('slide', 'tile')
The draws below stay inside these ranges and needn't reach their ends.
Inputs may be any that keep to these rules, and one draw needn't show every extreme that they name: Every position 0 to 16383 is held by exactly one slot; -1 marks an empty slot. A device's live slots come first. A device holds 384, 128 or 64 live tiles, some devices 384 in every draw, and sends the same number to each segment row r (positions whose offset in their slide lies in [r * 512, (r + 1) * 512)), so at most 48 tiles, exactly 48 from the fullest devices.
All inputs are finite; a program needn't handle non-finite values.
Results may differ from the reference program's by a relative error of at most 0.025.
The reference program's roundings to bfloat16 on the way count: a program that leaves them out, or rounds other values in their place, can miss the bound.
Values may be sent and summed in bfloat16 or wider, within the bound.
No kernel may reach another device: no remote copies, remote signals or barrier semaphores. Data moves between devices by JAX's collectives and lax.ppermute only.
A program may use at most 128 MiB of HBM per device.

```python
import math
import jax
import jax.numpy as jnp
from jax import lax

D_TILE = 1536
D = 768
HEADS = 16
HEAD_SIZE = 48
SLIDES = 4
SEG = 512
SLIDE_POSITIONS = 4096
SEQ = 16384
TILE_DEV = 384
TILES = 49152
N_SLIDE = 8
N_TILE = 16


def draw_tile_features(key, part):
    key = jax.random.fold_in(key, 7)
    first_key = jax.random.fold_in(key, 0)
    values = jnp.clip(jax.random.normal(first_key, (TILES, D_TILE), jnp.float32), -6.0, 6.0)
    return values.astype(jnp.bfloat16)


def draw_out_grad(key, part):
    key = jax.random.fold_in(key, 13)
    first_key, second_key = jax.random.split(key)
    values = jnp.clip(jax.random.normal(first_key, (SLIDES, SLIDE_POSITIONS, D), jnp.float32), -6.0, 6.0)
    row_scale = jnp.exp(jax.random.uniform(second_key, (SLIDES, SLIDE_POSITIONS, HEADS), jnp.float32, math.log(4.0), math.log(8.0)))
    offset_phase = (jnp.arange(SLIDE_POSITIONS, dtype=jnp.int32) % N_SLIDE)[:, None]
    head_phase = (jnp.arange(HEADS, dtype=jnp.int32) % N_SLIDE)[None, :]
    dilated = (offset_phase == head_phase)[None, :, :]
    scale = jnp.where(dilated, row_scale, jnp.float32(1.0))
    scale = jnp.repeat(scale, HEAD_SIZE, axis=2)
    return (values * scale).astype(jnp.bfloat16)


def draw_positions(key, part):
    key = jax.random.fold_in(key, 11)
    order_key, shuffle_key = jax.random.split(key)
    devices = N_SLIDE * N_TILE
    pattern = jnp.array([6, 1, 1, 1, 2, 2, 2, 1], jnp.int32)
    order_perm = jax.random.permutation(order_key, devices)
    unit_counts = pattern[order_perm % 8]
    per_row = unit_counts * (TILE_DEV // 6 // N_SLIDE)
    counts = per_row * N_SLIDE
    first_index = jnp.cumsum(per_row) - per_row
    slot_index = jnp.arange(TILE_DEV, dtype=jnp.int32)[None, :]
    row_block = slot_index // per_row[:, None]
    inner_index = slot_index % per_row[:, None]
    is_live = slot_index < counts[:, None]
    block_index = first_index[:, None] + inner_index
    shuffles = jax.vmap(lambda sub_key: jax.random.permutation(sub_key, SLIDES * SEG))(jax.random.split(shuffle_key, N_SLIDE))
    safe_row = jnp.clip(row_block, 0, N_SLIDE - 1)
    safe_index = jnp.clip(block_index, 0, SLIDES * SEG - 1)
    shuffled = shuffles[safe_row, safe_index]
    slide_index = shuffled // SEG
    offset = shuffled % SEG
    placed = slide_index * SLIDE_POSITIONS + safe_row * SEG + offset
    return jnp.where(is_live, placed, -1).reshape(-1).astype(jnp.int32)


def scatter_about(rng, dims, deviation, most, kind=jnp.bfloat16):
    values = deviation * jax.random.normal(rng, dims, jnp.float32)
    return jnp.clip(values, min=-most, max=most).astype(kind)


def setup_inputs(seed: int = 0) -> dict:
    keys = jax.random.split(jax.random.key(seed), 6)
    tile_features = draw_tile_features(jax.random.fold_in(keys[5], 71), 0)
    embed_weight = scatter_about(keys[1], (D_TILE, D), D_TILE ** -0.5, 0.15625)
    qkv_weight = scatter_about(keys[2], (D, 3 * D), D ** -0.5, 0.21875)
    positions = draw_positions(jax.random.fold_in(keys[5], 71), 0)
    out_grad = draw_out_grad(jax.random.fold_in(keys[5], 71), 0)
    return {"tile_features": tile_features, "embed_weight": embed_weight, "qkv_weight": qkv_weight, "positions": positions, "out_grad": out_grad}


def rounded(values):
    return lax.optimization_barrier(values.astype(jnp.bfloat16)).astype(jnp.float32)


def pick_sparse(values, phase_col):
    grouped = values.reshape((values.shape[0] // N_SLIDE, N_SLIDE) + values.shape[1:])
    return lax.dynamic_index_in_dim(grouped, phase_col, 1, False)


def put_sparse(full, sparse, phase_col):
    grouped = full.reshape(full.shape[0] // N_SLIDE, N_SLIDE)
    column = jnp.arange(N_SLIDE, dtype=jnp.int32) == phase_col
    return jnp.where(column[None, :], sparse[:, None], grouped).reshape(full.shape)


def add_sparse(full, sparse, phase_col):
    grouped = full.reshape(full.shape[0] // N_SLIDE, N_SLIDE, full.shape[1])
    column = (jnp.arange(N_SLIDE, dtype=jnp.int32) == phase_col)[None, :, None]
    return (grouped + jnp.where(column, sparse[:, None, :], jnp.float32(0.0))).reshape(full.shape)


def attend(queries, key_rows, value_rows, cotangent, phase_col):
    highest_precision = lax.Precision.HIGHEST
    score_scale = HEAD_SIZE ** -0.5
    blocks = SLIDE_POSITIONS // SEG
    query_f = queries.astype(jnp.float32)
    key_f = key_rows.astype(jnp.float32)
    value_f = value_rows.astype(jnp.float32)
    grad_f = cotangent.astype(jnp.float32)
    batch_queries = query_f.reshape(blocks, SEG, HEAD_SIZE)
    batch_keys = key_f.reshape(blocks, SEG, HEAD_SIZE)
    batch_values = value_f.reshape(blocks, SEG, HEAD_SIZE)
    batch_gradient = grad_f.reshape(blocks, SEG, HEAD_SIZE)
    query_s = pick_sparse(query_f, phase_col)
    key_s = pick_sparse(key_f, phase_col)
    value_s = pick_sparse(value_f, phase_col)
    grad_s = pick_sparse(grad_f, phase_col)
    nearby_window = jnp.einsum("wlj,wej->wle", batch_queries, batch_keys, precision=highest_precision) * score_scale
    far = jnp.einsum("qd,kd->qk", query_s, key_s, precision=highest_precision) * score_scale
    near_max = jnp.max(nearby_window, axis=-1).reshape(SLIDE_POSITIONS)
    far_max = jnp.maximum(pick_sparse(near_max, phase_col), jnp.max(far, axis=-1))
    row_max = put_sparse(near_max, far_max, phase_col)
    exp_near = jnp.exp(nearby_window - row_max.reshape(blocks, SEG, 1))
    exp_far = jnp.exp(far - far_max[:, None])
    near_total = jnp.sum(exp_near, axis=-1).reshape(SLIDE_POSITIONS)
    far_total = pick_sparse(near_total, phase_col) + jnp.sum(exp_far, axis=-1)
    row_total = put_sparse(near_total, far_total, phase_col)
    prob_near = exp_near / row_total.reshape(blocks, SEG, 1)
    prob_far = exp_far / far_total[:, None]
    nearby_weight = rounded(prob_near)
    weight_far = rounded(prob_far)
    near_prob_gradient = jnp.einsum("wlj,wej->wle", batch_gradient, batch_values, precision=highest_precision)
    dprob_far = jnp.einsum("qd,kd->qk", grad_s, value_s, precision=highest_precision)
    near_delta = jnp.sum(prob_near * near_prob_gradient, axis=-1).reshape(SLIDE_POSITIONS)
    far_delta = pick_sparse(near_delta, phase_col) + jnp.sum(prob_far * dprob_far, axis=-1)
    row_delta = put_sparse(near_delta, far_delta, phase_col)
    near_score_gradient = rounded(prob_near * (near_prob_gradient - row_delta.reshape(blocks, SEG, 1)))
    dscore_far = rounded(prob_far * (dprob_far - far_delta[:, None]))
    query_gradient = jnp.einsum("tcg,tgl->tcl", near_score_gradient, batch_keys, precision=highest_precision).reshape(SLIDE_POSITIONS, HEAD_SIZE) * score_scale
    query_gradient = add_sparse(query_gradient, jnp.einsum("qk,kd->qd", dscore_far, key_s, precision=highest_precision) * score_scale, phase_col)
    key_gradient = jnp.einsum("vat,var->vtr", near_score_gradient, batch_queries, precision=highest_precision).reshape(SLIDE_POSITIONS, HEAD_SIZE) * score_scale
    key_gradient = add_sparse(key_gradient, jnp.einsum("qk,qd->kd", dscore_far, query_s, precision=highest_precision) * score_scale, phase_col)
    value_gradient = jnp.einsum("vat,var->vtr", nearby_weight, batch_gradient, precision=highest_precision).reshape(SLIDE_POSITIONS, HEAD_SIZE)
    value_gradient = add_sparse(value_gradient, jnp.einsum("qk,qd->kd", weight_far, grad_s, precision=highest_precision), phase_col)
    return jnp.stack([query_gradient, key_gradient, value_gradient], axis=1).astype(jnp.bfloat16)


def reference(tile_features, embed_weight, qkv_weight, positions, out_grad):
    is_live = positions >= 0
    target = jnp.where(is_live, positions, SEQ).astype(jnp.int32)
    owner_tile = jnp.zeros((SEQ,), jnp.int32).at[target].set(jnp.arange(TILES, dtype=jnp.int32), mode="drop")
    seq_rows = tile_features[owner_tile]
    embedded = jnp.dot(seq_rows, embed_weight, preferred_element_type=jnp.float32).astype(jnp.bfloat16)
    projected = jnp.dot(embedded, qkv_weight, preferred_element_type=jnp.float32).astype(jnp.bfloat16)
    by_position = projected.reshape(SLIDES, SLIDE_POSITIONS, HEADS, 3, HEAD_SIZE)
    cotangent = out_grad.reshape(SLIDES, SLIDE_POSITIONS, HEADS, HEAD_SIZE)

    def one_head(head_index):
        parts = lax.dynamic_index_in_dim(by_position, head_index, 2, False)
        grad_head = lax.dynamic_index_in_dim(cotangent, head_index, 2, False)
        phase_col = head_index % N_SLIDE
        return jax.vmap(attend, in_axes=(0, 0, 0, 0, None))(parts[:, :, 0], parts[:, :, 1], parts[:, :, 2], grad_head, phase_col)

    every_head = lax.map(one_head, jnp.arange(HEADS, dtype=jnp.int32))
    d_position = every_head.transpose(1, 2, 0, 3, 4).reshape(SEQ, 3 * D)
    qkv_grad = jnp.dot(embedded.T, d_position, preferred_element_type=jnp.float32)
    d_embedded = jnp.dot(d_position, qkv_weight.T, preferred_element_type=jnp.float32).astype(jnp.bfloat16)
    embed_grad = jnp.dot(seq_rows.T, d_embedded, preferred_element_type=jnp.float32)
    d_rows = jnp.dot(d_embedded, embed_weight.T, preferred_element_type=jnp.float32).astype(jnp.bfloat16)
    feature_grad = jnp.zeros((TILES, D_TILE), jnp.bfloat16).at[owner_tile].set(d_rows)
    return feature_grad, embed_grad, qkv_grad
```

```python
import functools

import jax
import jax.numpy as jnp
from jax import lax
from jax.experimental import pallas as pl
from jax.experimental.pallas import tpu as pltpu
from jax.sharding import PartitionSpec as P

HEAD_SIZE = 48
WIDTH = 3 * HEAD_SIZE
CHUNK_ROWS = 160
FLOATS = jnp.float32
HALFS = jnp.bfloat16
SCALE = HEAD_SIZE ** (-0.5)
VMEM = pltpu.CompilerParams(vmem_limit_bytes=56 * 1024 * 1024)


def iota(shape, dim):
    return lax.broadcasted_iota(jnp.int32, shape, dim)


def hot(cond):
    return jnp.where(cond, 1.0, 0.0).astype(HALFS)


def dot(a, b, dims="nn"):
    contract = (0 if dims[0] == "t" else 1, 1 if dims[1] == "t" else 0)
    return lax.dot_general(
        a, b, (((contract[0],), (contract[1],)), ((), ())), preferred_element_type=FLOATS
    )


def whole(memory=pltpu.VMEM):
    return pl.BlockSpec(memory_space=memory)


def call(body, outs, args, smem=(), **kw):
    specs = [whole(pltpu.SMEM if i in smem else pltpu.VMEM) for i in range(len(args))]
    return pl.pallas_call(
        body,
        out_shape=outs,
        in_specs=specs,
        out_specs=jax.tree.map(lambda _: whole(), outs),
        compiler_params=VMEM,
        **kw,
    )(*args)


def shaped(shape, dtype=HALFS):
    return jax.ShapeDtypeStruct(shape, dtype)


def place(pos, rank, off):
    row = (pos & 4095) >> 9
    dest = row * 16 + ((rank + off) & 15)
    return dest * 8, rank >> 4


def dispatch_body(me_ref, counts_ref, pos_row_ref, pos_col_ref, emb_ref, send_ref, base_ref):
    slots = emb_ref.shape[0]
    half = emb_ref.shape[1] // 2
    counts = counts_ref[...]
    before = (iota(counts.shape, 0) < me_ref[0]) & (iota(counts.shape, 1) == 0)
    off = jnp.sum(
        jnp.sum(jnp.where(before, counts, 0), axis=0, keepdims=True), axis=1, keepdims=True
    )
    pos = pos_row_ref[...]
    live = pos >= 0
    pos = jnp.where(live, pos, 0)
    member = ((pos & 4095) >> 9 == iota((8, slots), 0)) & live
    upper = hot(iota((slots, slots), 0) < iota((slots, slots), 1))
    ranks = dot(hot(member), upper)
    rank = jnp.sum(jnp.where(member, ranks, 0.0), axis=0, keepdims=True).astype(jnp.int32)
    dest, sub = place(pos, rank, off)
    base = jnp.where(live, dest + 2 * sub, -16)
    note = jnp.where(live, dest + 6, -16)
    local = ((pos >> 12) << 9) + (pos & 511)
    lane = iota((128, slots), 0)
    notes = jnp.where(
        lane == 4 * sub, (local >> 7) + 1, jnp.where(lane == 4 * sub + 1, local & 127, 0)
    )
    notes = notes.astype(FLOATS).astype(HALFS)
    step = 256
    for start in range(0, send_ref.shape[0], step):
        rows = iota((step, slots), 0) + start
        out = dot(hot(rows == base), emb_ref[:, :half])
        out = out + dot(hot(rows == base + 1), emb_ref[:, half:])
        send_ref[start : start + step, :] = out.astype(HALFS)
        info = dot(hot(rows == note), notes, "nt")
        send_ref[start : start + step, :128] = (out[:, :128] + info).astype(HALFS)
    pos = pos_col_ref[...]
    live = pos >= 0
    pos = jnp.where(live, pos, 0)
    member = ((pos & 4095) >> 9 == iota((slots, 128), 1)) & live
    lower = hot(iota((slots, slots), 0) > iota((slots, slots), 1))
    ranks = dot(lower, hot(member))
    rank = jnp.sum(jnp.where(member, ranks, 0.0), axis=1, keepdims=True).astype(jnp.int32)
    dest, sub = place(pos, rank, off)
    base_ref[...] = jnp.broadcast_to(jnp.where(live, dest + 2 * sub, -16), base_ref.shape)


def project_body(recv_ref, weight_ref, emb_ref, chunk_ref, pick0_ref, pick1_ref):
    total = recv_ref.shape[0]
    senders = total // 8
    sel = hot(iota((senders, total), 1) == 8 * iota((senders, total), 0) + 6)
    notes = dot(sel, recv_ref[:, :128])
    lane = iota((senders, 128), 1)
    valid = (notes > 0.5) & ((lane & 3) == 0) & (lane < 12)
    lower = hot(iota((senders, senders), 0) > iota((senders, senders), 1))
    cum = dot(lower, hot(valid))
    ones = jnp.where(valid, 1.0, 0.0)
    first = jnp.sum(jnp.where(lane == 0, ones, 0.0), axis=0, keepdims=True)
    first = jnp.sum(first, axis=1, keepdims=True)
    second = jnp.sum(jnp.where(lane == 4, ones, 0.0), axis=0, keepdims=True)
    second = jnp.sum(second, axis=1, keepdims=True)
    shift = jnp.where(lane >= 4, first, 0.0) + jnp.where(lane >= 8, second, 0.0)
    index = jnp.where(valid, cum + shift, -1.0)
    repeat = hot(iota((total, senders), 0) >> 3 == iota((total, senders), 1))
    index_all = dot(repeat, index.astype(HALFS))
    notes_all = dot(repeat, notes.astype(HALFS))
    turn = iota((total, 128), 0) & 7
    lanes = iota((total, 128), 1)
    mine = (lanes == 4 * (turn >> 1)) & (turn < 6)
    mine_low = (lanes == 4 * (turn >> 1) + 1) & (turn < 6)
    spot = jnp.sum(jnp.where(mine, index_all + 1.0, 0.0), axis=1, keepdims=True) - 1.0
    high = jnp.sum(jnp.where(mine, notes_all, 0.0), axis=1, keepdims=True)
    low = jnp.sum(jnp.where(mine_low, notes_all, 0.0), axis=1, keepdims=True)
    match = spot.astype(jnp.int32) == lanes
    pick0 = hot(match & ((turn & 1) == 0))
    pick1 = hot(match & ((turn & 1) == 1))
    pick0_ref[...] = pick0
    pick1_ref[...] = pick1
    half = recv_ref.shape[1]
    emb_ref[:, :half] = dot(pick0, recv_ref[...], "tn").astype(HALFS)
    emb_ref[:, half:] = dot(pick1, recv_ref[...], "tn").astype(HALFS)
    info = jnp.where(lanes == 0, high, jnp.where(lanes == 1, low, 0.0)).astype(HALFS)
    info = dot(info, pick0, "tn")[:16].astype(HALFS)
    heads = chunk_ref.shape[0] // CHUNK_ROWS
    for head in range(heads):
        columns = slice(head * WIDTH, (head + 1) * WIDTH)
        top = head * CHUNK_ROWS
        if head % 8 == 0:
            wide = slice(head * WIDTH, (head + 8) * WIDTH)
            part = dot(emb_ref[...], weight_ref[:, wide]).T
        columns = slice((head % 8) * WIDTH, (head % 8 + 1) * WIDTH)
        chunk_ref[top : top + WIDTH, :] = part[columns].astype(HALFS)
        chunk_ref[top + WIDTH : top + CHUNK_ROWS, :] = info


def dilated_body(phase_ref, chunk_ref, query_ref, far_ref, rows_ref, local_ref):
    blocks = chunk_ref.shape[0] // CHUNK_ROWS
    total = jnp.zeros((WIDTH, query_ref.shape[1]), FLOATS)
    target = 8 * iota((query_ref.shape[1], 128), 0) + phase_ref[0]
    for block in range(blocks):
        top = block * CHUNK_ROWS
        lanes = slice(block * 128, (block + 1) * 128)
        part = chunk_ref[top : top + WIDTH, :]
        info = chunk_ref[top + WIDTH : top + CHUNK_ROWS, :].astype(FLOATS)
        local = ((info[0:1] - 1.0) * 128.0 + info[1:2]).astype(jnp.int32)
        rows_ref[:, lanes] = part
        local_ref[:, lanes] = jnp.broadcast_to(local, (8, 128))
        total = total + dot(part, hot(target == local), "nt")
    query_ref[...] = total[:HEAD_SIZE].astype(HALFS)
    far_ref[...] = total[HEAD_SIZE:].astype(HALFS)


def near_body(phase_ref, rows_ref, local_ref, grad_ref, place_ref, near_ref):
    seg = grad_ref.shape[2]
    slide = pl.program_id(0)
    local = local_ref[0:1, :]
    order = hot(local == iota((seg, local.shape[1]), 0) + slide * seg)
    parts = dot(rows_ref[...], order, "nt").astype(HALFS)
    place_ref[...] = parts
    query = parts[:HEAD_SIZE]
    key = parts[HEAD_SIZE : 2 * HEAD_SIZE]
    value = parts[2 * HEAD_SIZE :]
    grad = grad_ref[0]
    score = dot(key, query, "tn") * SCALE
    top = jnp.max(score, axis=0, keepdims=True)
    prob = jnp.exp(score - top)
    norm = 1.0 / jnp.sum(prob, axis=0, keepdims=True)
    dilated = (iota((1, seg), 1) & 7) == phase_ref[0]
    prob = prob * jnp.where(dilated, 0.0, norm)
    dprob = dot(value, grad, "tn")
    delta = jnp.sum(prob * dprob, axis=0, keepdims=True)
    dscore = (prob * (dprob - delta)).astype(HALFS)
    near_ref[:HEAD_SIZE, :] = dot(key, dscore) * SCALE
    near_ref[HEAD_SIZE : 2 * HEAD_SIZE, :] = dot(query, dscore, "nt") * SCALE
    near_ref[2 * HEAD_SIZE :, :] = dot(grad, prob.astype(HALFS), "nt")


def far_body(phase_ref, query_ref, place_ref, grad_ref, *refs):
    n = (len(refs) - 2) // 2
    far_refs, dquery_ref, near_ref, out_refs = refs[:n], refs[n], refs[n + 1], refs[n + 2 :]
    seg = grad_ref.shape[2]
    for pair in range(grad_ref.shape[0] // 2):
        lanes = slice(pair * 128, (pair + 1) * 128)
        spots = slice(pair * 2 * seg, (pair + 1) * 2 * seg)
        query = query_ref[:, lanes]
        grad = jnp.zeros((HEAD_SIZE, 128), FLOATS)
        for b in range(2):
            target = 8 * (iota((seg, 128), 1) - 64 * b) + phase_ref[0]
            grad = grad + dot(grad_ref[2 * pair + b], hot(iota((seg, 128), 0) == target))
        grad = grad.astype(HALFS)
        key = jnp.concatenate(
            [place_ref[HEAD_SIZE : 2 * HEAD_SIZE, spots]]
            + [ref[:HEAD_SIZE, lanes] for ref in far_refs],
            axis=1,
        )
        value = jnp.concatenate(
            [place_ref[2 * HEAD_SIZE :, spots]] + [ref[HEAD_SIZE:, lanes] for ref in far_refs],
            axis=1,
        )
        size = key.shape[1]
        row = iota((size, 128), 0)
        slide_of_key = jnp.where(row < 2 * seg, row // seg, (row & 127) >> 6)
        same = slide_of_key == iota((size, 128), 1) >> 6
        score = jnp.where(same, dot(key, query, "tn") * SCALE, -1e30)
        top = jnp.max(score, axis=0, keepdims=True)
        prob = jnp.exp(score - top)
        prob = prob * (1.0 / jnp.sum(prob, axis=0, keepdims=True))
        dprob = dot(value, grad, "tn")
        delta = jnp.sum(prob * dprob, axis=0, keepdims=True)
        dscore = (prob * (dprob - delta)).astype(HALFS)
        dquery_ref[:, lanes] = (dot(key, dscore) * SCALE).astype(HALFS)
        dkey = dot(query, dscore, "nt") * SCALE
        dvalue = dot(grad, prob.astype(HALFS), "nt")
        near_ref[:HEAD_SIZE, spots] = dkey[:, : 2 * seg]
        near_ref[HEAD_SIZE:, spots] = dvalue[:, : 2 * seg]
        for k, ref in enumerate(out_refs):
            part = slice(2 * seg + k * 128, 2 * seg + (k + 1) * 128)
            ref[:HEAD_SIZE, lanes] = dkey[:, part].astype(HALFS)
            ref[HEAD_SIZE:, lanes] = dvalue[:, part].astype(HALFS)


def unplace_body(local_ref, near_ref, extra_ref, out_ref):
    places = near_ref.shape[1]
    block = out_ref.shape[1]
    local = local_ref[0:1, :]
    order = hot(local == iota((places, block), 0))
    query = near_ref[:HEAD_SIZE, :].astype(HALFS)
    rest = (near_ref[HEAD_SIZE:, :] + extra_ref[...]).astype(HALFS)
    out_ref[...] = dot(jnp.concatenate([query, rest], axis=0), order)


def finish_body(phase_ref, local_ref, main_ref, dquery_ref, *refs):
    far_refs, chunk_ref, rows_ref = refs[:-2], refs[-2], refs[-1]
    far = far_refs[0][...].astype(FLOATS)
    for ref in far_refs[1:]:
        far = far + ref[...].astype(FLOATS)
    sparse = jnp.concatenate([dquery_ref[...], far.astype(HALFS)], axis=0)
    local = local_ref[0:1, :]
    count = dquery_ref.shape[1]
    order = hot(local == 8 * iota((count, local.shape[1]), 0) + phase_ref[0])
    rows = (main_ref[...] + dot(sparse, order)).astype(HALFS)
    rows_ref[...] = rows
    for block in range(chunk_ref.shape[0] // WIDTH):
        chunk_ref[block * WIDTH : (block + 1) * WIDTH, :] = rows[
            :, block * 128 : (block + 1) * 128
        ]


def back_body(rows_ref, weight_ref, pick0_ref, pick1_ref, back_ref):
    half = back_ref.shape[1]
    grad = dot(weight_ref[...], rows_ref[...]).astype(HALFS)
    back = dot(pick0_ref[...], grad[:half], "nt") + dot(pick1_ref[...], grad[half:], "nt")
    back_ref[...] = back.astype(HALFS)


def collect_body(recv_ref, base_ref, out_ref):
    total, half = recv_ref.shape
    base = base_ref[:, 0:1]
    rows = iota((base.shape[0], total), 1)
    out_ref[:, :half] = dot(hot(rows == base), recv_ref[...]).astype(HALFS)
    out_ref[:, half:] = dot(hot(rows == base + 1), recv_ref[...]).astype(HALFS)


def per_device(tile_features, embed_weight, qkv_weight, positions, out_grad):
    n_slide = lax.axis_size("slide")
    n_tile = lax.axis_size("tile")
    devices = n_slide * n_tile
    every = ("slide", "tile")
    slots = tile_features.shape[0]
    slides, seg = out_grad.shape[0], out_grad.shape[1]
    wide = embed_weight.shape[1]
    half = wide // 2
    rows = slides * seg
    share = rows // n_tile
    row_here = lax.axis_index("slide")
    col_here = lax.axis_index("tile")
    me = (row_here * n_tile + col_here).astype(jnp.int32).reshape(1)
    phase = (col_here % n_slide).astype(jnp.int32).reshape(1)
    core = row_here % 2

    with jax.named_scope("counts"):
        count = jnp.sum((positions >= 0).astype(jnp.int32)) // n_slide
        counts = lax.all_to_all(
            jnp.broadcast_to(count, (devices, 1, 128)), every, 0, 0, tiled=True
        ).reshape(devices, 128)
    with jax.named_scope("embed"):
        embedded = jnp.dot(tile_features, embed_weight, preferred_element_type=FLOATS).astype(HALFS)
    with jax.named_scope("dispatch"):
        sent, base = call(
            dispatch_body,
            [shaped((devices * 8, half)), shaped((slots, 128), jnp.int32)],
            [me, counts, positions.reshape(1, slots), positions.reshape(slots, 1), embedded],
            smem=(0,),
        )
        arrived = lax.all_to_all(
            sent.reshape(devices, 8, half), every, 0, 0, tiled=True
        ).reshape(devices * 8, half)
    with jax.named_scope("project"):
        emb_rows, chunks, pick0, pick1 = call(
            project_body,
            [
                shaped((share, wide)),
                shaped((n_tile * CHUNK_ROWS, 128)),
                shaped((devices * 8, 128)),
                shaped((devices * 8, 128)),
            ],
            [arrived, qkv_weight],
        )
        chunks = lax.all_to_all(
            chunks.reshape(n_tile, CHUNK_ROWS, 128), "tile", 0, 0, tiled=True
        ).reshape(n_tile * CHUNK_ROWS, 128)
    with jax.named_scope("dilated"):
        few = rows // n_slide
        query, far, head_rows, local = call(
            dilated_body,
            [
                shaped((HEAD_SIZE, few)),
                shaped((2 * HEAD_SIZE, few)),
                shaped((WIDTH, rows)),
                shaped((8, rows), jnp.int32),
            ],
            [phase, chunks],
            smem=(0,),
        )
        fars = [far] + [
            lax.ppermute(far, "slide", [(i, (i + k) % n_slide) for i in range(n_slide)])
            for k in range(1, n_slide)
        ]
    with jax.named_scope("near"):
        grads = out_grad.transpose(0, 2, 1)
        placed, near = pl.pallas_call(
            near_body,
            grid=(slides,),
            out_shape=[shaped((WIDTH, rows)), shaped((WIDTH, rows), FLOATS)],
            in_specs=[
                whole(pltpu.SMEM),
                pl.BlockSpec((WIDTH, rows), lambda i: (0, 0)),
                pl.BlockSpec((8, rows), lambda i: (0, 0)),
                pl.BlockSpec((1, HEAD_SIZE, seg), lambda i: (i, 0, 0)),
            ],
            out_specs=[
                pl.BlockSpec((WIDTH, seg), lambda i: (0, i)),
                pl.BlockSpec((WIDTH, seg), lambda i: (0, i)),
            ],
            compiler_params=VMEM,
            cost_estimate=pl.CostEstimate(
                flops=8_000_000_000, bytes_accessed=8_000_000, transcendentals=1 << 20
            ),
        )(phase, head_rows, local, grads)
    with jax.named_scope("far"):
        results = call(
            far_body,
            [shaped((HEAD_SIZE, few)), shaped((2 * HEAD_SIZE, rows), FLOATS)]
            + [shaped((2 * HEAD_SIZE, few))] * n_slide,
            [phase, query, placed, grads] + fars,
            smem=(0,),
        )
        dquery, extra, outs = results[0], results[1], results[2:]
        returned = [outs[0]] + [
            lax.ppermute(outs[k], "slide", [((i + k) % n_slide, i) for i in range(n_slide)])
            for k in range(1, n_slide)
        ]
    with jax.named_scope("unplace"):
        block = rows // 4
        main = pl.pallas_call(
            unplace_body,
            grid=(rows // block,),
            out_shape=shaped((WIDTH, rows), FLOATS),
            in_specs=[
                pl.BlockSpec((8, block), lambda i: (0, i)),
                pl.BlockSpec((WIDTH, rows), lambda i: (0, 0)),
                pl.BlockSpec((2 * HEAD_SIZE, rows), lambda i: (0, 0)),
            ],
            out_specs=pl.BlockSpec((WIDTH, block), lambda i: (0, i)),
            compiler_params=VMEM,
            cost_estimate=pl.CostEstimate(
                flops=4_000_000_000, bytes_accessed=4_000_000, transcendentals=0
            ),
        )(local, near, extra)
        back_chunks, d_rows = call(
            finish_body,
            [shaped((n_tile * WIDTH, 128)), shaped((WIDTH, rows))],
            [phase, local, main, dquery] + returned,
            smem=(0,),
        )
        back_rows = lax.all_to_all(
            back_chunks.reshape(n_tile, WIDTH, 128), "tile", 0, 0, tiled=True
        ).reshape(n_tile * WIDTH, 128)
    with jax.named_scope("back"):
        back = call(
            back_body, shaped((devices * 8, half)), [back_rows, qkv_weight, pick0, pick1]
        )
        back = lax.all_to_all(
            back.reshape(devices, 8, half), every, 0, 0, tiled=True
        ).reshape(devices * 8, half)
        d_embedded = call(collect_body, shaped((slots, wide)), [back, base])
    with jax.named_scope("qkv_grad"):
        all_rows = lax.all_gather(emb_rows, "tile", axis=0, tiled=True)
        qkv_part = lax.dot_general(
            all_rows, d_rows, (((0,), (1,)), ((), ())), preferred_element_type=FLOATS
        ).astype(HALFS)
        qkv_parts = lax.all_to_all(
            qkv_part.reshape(n_slide, wide // n_slide, WIDTH), "slide", 0, 0, tiled=True
        )
        qkv_grad = jnp.sum(qkv_parts.astype(FLOATS), axis=0)
    with jax.named_scope("embed_grad"):
        tiles = tile_features.shape[1]
        narrow = tiles // n_slide
        split = tile_features.reshape(slots, n_slide // 2, 2, narrow)
        keep_cols = lax.dynamic_index_in_dim(split, core, 2, False).reshape(slots, tiles // 2)
        give_cols = lax.dynamic_index_in_dim(split, 1 - core, 2, False).reshape(slots, tiles // 2)
        given = lax.dot_general(
            d_embedded, give_cols, (((0,), (0,)), ((), ())), preferred_element_type=FLOATS
        ).astype(HALFS)
        given = lax.ppermute(given, "slide", [(i, i ^ 1) for i in range(n_slide)])
        kept = lax.dot_general(
            d_embedded, keep_cols, (((0,), (0,)), ((), ())), preferred_element_type=FLOATS
        )
        kept = (kept + given.astype(FLOATS)).astype(HALFS)
        parts = lax.all_to_all(
            kept.reshape(n_tile, wide // n_tile, tiles // 2), "tile", 0, 0, tiled=True
        )
        part = jnp.sum(parts.astype(FLOATS), axis=0)
        part = part.reshape(wide // n_tile, n_slide // 2, narrow).transpose(1, 0, 2)
        same_core = [list(range(c, n_slide, 2)) for c in range(2)]
        part = lax.all_to_all(part, "slide", 0, 0, axis_index_groups=same_core, tiled=True)
        embed_grad = jnp.sum(part, axis=0).T
    with jax.named_scope("feature_grad"):
        feature_grad = lax.dot_general(
            d_embedded, embed_weight, (((1,), (1,)), ((), ())), preferred_element_type=FLOATS
        ).astype(HALFS)
    return feature_grad, embed_grad, qkv_grad


def solution(mesh):
    placed = (P(("slide", "tile"), None), P(), P(), P(("slide", "tile")), P(None, "slide", "tile"))
    return jax.shard_map(
        per_device,
        mesh=mesh,
        in_specs=placed,
        out_specs=(P(("slide", "tile"), None), P("slide", "tile"), P("slide", "tile")),
        check_vma=False,
    )
```

```python
import functools

import jax
import jax.numpy as jnp
from jax import lax
from jax.experimental import pallas as pl
from jax.experimental.pallas import tpu as pltpu
from jax.sharding import PartitionSpec as P

HEAD_SIZE = 48
WIDTH = 3 * HEAD_SIZE
CHUNK_ROWS = 160
FLOATS = jnp.float32
HALFS = jnp.bfloat16
SCALE = HEAD_SIZE ** (-0.5)
VMEM = pltpu.CompilerParams(vmem_limit_bytes=56 * 1024 * 1024)


def iota(shape, dim):
    return lax.broadcasted_iota(jnp.int32, shape, dim)


def hot(cond):
    return jnp.where(cond, 1.0, 0.0).astype(HALFS)


def dot(a, b, dims="nn"):
    contract = (0 if dims[0] == "t" else 1, 1 if dims[1] == "t" else 0)
    return lax.dot_general(
        a, b, (((contract[0],), (contract[1],)), ((), ())), preferred_element_type=FLOATS
    )


def whole(memory=pltpu.VMEM):
    return pl.BlockSpec(memory_space=memory)


def call(body, outs, args, smem=(), **kw):
    specs = [whole(pltpu.SMEM if i in smem else pltpu.VMEM) for i in range(len(args))]
    return pl.pallas_call(
        body,
        out_shape=outs,
        in_specs=specs,
        out_specs=jax.tree.map(lambda _: whole(), outs),
        compiler_params=VMEM,
        **kw,
    )(*args)


def shaped(shape, dtype=HALFS):
    return jax.ShapeDtypeStruct(shape, dtype)


def place(pos, live, rank, few):
    row = (pos & 4095) >> 9
    dest = row * 128 + jnp.where(few, rank * 16, (rank & 15) * 8)
    sub = jnp.where(few, 0, rank >> 4)
    base = jnp.where(live, dest + 2 * sub, -16)
    twin = jnp.where(live & few, dest + 8, -16)
    return base, twin, sub


def dispatch_body(pos_row_ref, pos_col_ref, tiles_ref, send_ref, base_ref):
    slots = tiles_ref.shape[0]
    half = tiles_ref.shape[1] // 2
    pos = pos_row_ref[...]
    live = pos >= 0
    few = jnp.sum(jnp.where(live, 1, 0), axis=1, keepdims=True) <= 64
    pos = jnp.where(live, pos, 0)
    member = ((pos & 4095) >> 9 == iota((8, slots), 0)) & live
    upper = hot(iota((slots, slots), 0) < iota((slots, slots), 1))
    ranks = dot(hot(member), upper)
    rank = jnp.sum(jnp.where(member, ranks, 0.0), axis=0, keepdims=True).astype(jnp.int32)
    base, twin, sub = place(pos, live, rank, few)
    note = jnp.where(live, base - 2 * sub + 6, -16)
    note_twin = jnp.where(live & few, twin + 6, -16)
    local = ((pos >> 12) << 9) + (pos & 511)
    lane = iota((128, slots), 0) - 4 * sub
    notes = jnp.where(
        lane == 0,
        (local >> 7) + 1,
        jnp.where(lane == 1, local & 127, jnp.where((lane == 2) & few, 1, 0)),
    )
    notes = notes.astype(FLOATS).astype(HALFS)
    step = 256
    for start in range(0, send_ref.shape[0], step):
        rows = iota((step, slots), 0) + start
        out = dot(hot((rows == base) | (rows == twin)), tiles_ref[:, :half])
        out = out + dot(
            hot((rows == base + 1) | (rows == twin + 1)), tiles_ref[:, half:]
        )
        send_ref[start : start + step, :] = out.astype(HALFS)
        info = dot(hot((rows == note) | (rows == note_twin)), notes, "nt")
        send_ref[start : start + step, :128] = (out[:, :128] + info).astype(HALFS)
    pos = pos_col_ref[...]
    live = pos >= 0
    pos = jnp.where(live, pos, 0)
    member = ((pos & 4095) >> 9 == iota((slots, 128), 1)) & live
    lower = hot(iota((slots, slots), 0) > iota((slots, slots), 1))
    ranks = dot(lower, hot(member))
    rank = jnp.sum(jnp.where(member, ranks, 0.0), axis=1, keepdims=True).astype(jnp.int32)
    base, twin, sub = place(pos, live, rank, few)
    base_ref[...] = jnp.where(iota(base_ref.shape, 1) == 0, base, twin)


def project_body(
    odd_ref,
    recv_ref,
    embed_ref,
    weight_ref,
    emb_ref,
    tiles_ref,
    chunk_ref,
    pick0_ref,
    pick1_ref,
):
    total = recv_ref.shape[0]
    senders = total // 8
    sel = hot(iota((senders, total), 1) == 8 * iota((senders, total), 0) + 6)
    notes = dot(sel, recv_ref[:, :128])
    lane = iota((senders, 128), 1)
    lower = hot(iota((senders, senders), 0) > iota((senders, senders), 1))
    shared = (notes > 0.5) & (lane == 2)
    order = dot(lower, hot(shared)).astype(jnp.int32)
    other = shared & ((order & 1) != odd_ref[0])
    to_first = hot((iota((128, 128), 0) == 2) & (iota((128, 128), 1) == 0))
    other = dot(hot(other), to_first) > 0.5
    valid = (notes > 0.5) & ((lane & 3) == 0) & (lane < 12) & jnp.logical_not(other)
    cum = dot(lower, hot(valid))
    ones = jnp.where(valid, 1.0, 0.0)
    first = jnp.sum(jnp.where(lane == 0, ones, 0.0), axis=0, keepdims=True)
    first = jnp.sum(first, axis=1, keepdims=True)
    second = jnp.sum(jnp.where(lane == 4, ones, 0.0), axis=0, keepdims=True)
    second = jnp.sum(second, axis=1, keepdims=True)
    shift = jnp.where(lane >= 4, first, 0.0) + jnp.where(lane >= 8, second, 0.0)
    index = jnp.where(valid, cum + shift, -1.0)
    repeat = hot(iota((total, senders), 0) >> 3 == iota((total, senders), 1))
    index_all = dot(repeat, index.astype(HALFS))
    notes_all = dot(repeat, notes.astype(HALFS))
    turn = iota((total, 128), 0) & 7
    lanes = iota((total, 128), 1)
    mine = (lanes == 4 * (turn >> 1)) & (turn < 6)
    mine_low = (lanes == 4 * (turn >> 1) + 1) & (turn < 6)
    spot = jnp.sum(jnp.where(mine, index_all + 1.0, 0.0), axis=1, keepdims=True) - 1.0
    high = jnp.sum(jnp.where(mine, notes_all, 0.0), axis=1, keepdims=True)
    low = jnp.sum(jnp.where(mine_low, notes_all, 0.0), axis=1, keepdims=True)
    match = spot.astype(jnp.int32) == lanes
    pick0 = hot(match & ((turn & 1) == 0))
    pick1 = hot(match & ((turn & 1) == 1))
    pick0_ref[...] = pick0
    pick1_ref[...] = pick1
    half = recv_ref.shape[1]
    tiles_ref[:, :half] = dot(pick0, recv_ref[...], "tn").astype(HALFS)
    tiles_ref[:, half:] = dot(pick1, recv_ref[...], "tn").astype(HALFS)
    emb_ref[...] = dot(tiles_ref[...], embed_ref[...]).astype(HALFS)
    info = jnp.where(lanes == 0, high, jnp.where(lanes == 1, low, 0.0)).astype(HALFS)
    info = dot(info, pick0, "tn")[:16].astype(HALFS)
    heads = chunk_ref.shape[0] // CHUNK_ROWS
    for head in range(heads):
        top = head * CHUNK_ROWS
        if head % 8 == 0:
            wide = slice(head * WIDTH, (head + 8) * WIDTH)
            part = dot(emb_ref[...], weight_ref[:, wide]).T
        columns = slice((head % 8) * WIDTH, (head % 8 + 1) * WIDTH)
        chunk_ref[top : top + WIDTH, :] = part[columns].astype(HALFS)
        chunk_ref[top + WIDTH : top + CHUNK_ROWS, :] = info


def dilated_body(phase_ref, chunk_ref, query_ref, far_ref, rows_ref, local_ref):
    blocks = chunk_ref.shape[0] // CHUNK_ROWS
    total = jnp.zeros((WIDTH, query_ref.shape[1]), FLOATS)
    target = 8 * iota((query_ref.shape[1], 128), 0) + phase_ref[0]
    for block in range(blocks):
        top = block * CHUNK_ROWS
        lanes = slice(block * 128, (block + 1) * 128)
        part = chunk_ref[top : top + WIDTH, :]
        info = chunk_ref[top + WIDTH : top + CHUNK_ROWS, :].astype(FLOATS)
        local = ((info[0:1] - 1.0) * 128.0 + info[1:2]).astype(jnp.int32)
        rows_ref[:, lanes] = part
        local_ref[:, lanes] = jnp.broadcast_to(local, (8, 128))
        total = total + dot(part, hot(target == local), "nt")
    query_ref[...] = total[:HEAD_SIZE].astype(HALFS)
    for copy in range(far_ref.shape[0]):
        far_ref[copy] = total[HEAD_SIZE:].astype(HALFS)


def near_body(phase_ref, rows_ref, local_ref, grad_ref, place_ref, near_ref):
    seg = grad_ref.shape[2]
    slide = pl.program_id(0)
    local = local_ref[0:1, :]
    order = hot(local == iota((seg, local.shape[1]), 0) + slide * seg)
    parts = dot(rows_ref[...], order, "nt").astype(HALFS)
    place_ref[...] = parts
    query = parts[:HEAD_SIZE]
    key = parts[HEAD_SIZE : 2 * HEAD_SIZE]
    value = parts[2 * HEAD_SIZE :]
    grad = grad_ref[0]
    score = dot(key, query, "tn") * SCALE
    top = jnp.max(score, axis=0, keepdims=True)
    prob = jnp.exp(score - top)
    norm = 1.0 / jnp.sum(prob, axis=0, keepdims=True)
    dilated = (iota((1, seg), 1) & 7) == phase_ref[0]
    prob = prob * jnp.where(dilated, 0.0, norm)
    dprob = dot(value, grad, "tn")
    delta = jnp.sum(prob * dprob, axis=0, keepdims=True)
    dscore = (prob * (dprob - delta)).astype(HALFS)
    near_ref[:HEAD_SIZE, :] = dot(key, dscore) * SCALE
    near_ref[HEAD_SIZE : 2 * HEAD_SIZE, :] = dot(query, dscore, "nt") * SCALE
    near_ref[2 * HEAD_SIZE :, :] = dot(grad, prob.astype(HALFS), "nt")


def far_body(
    phase_ref, query_ref, place_ref, grad_ref, far_ref, dquery_ref, near_ref, out_ref
):
    n = far_ref.shape[0]
    seg = grad_ref.shape[2]
    for pair in range(grad_ref.shape[0] // 2):
        lanes = slice(pair * 128, (pair + 1) * 128)
        spots = slice(pair * 2 * seg, (pair + 1) * 2 * seg)
        query = query_ref[:, lanes]
        grad = jnp.zeros((HEAD_SIZE, 128), FLOATS)
        for b in range(2):
            target = 8 * (iota((seg, 128), 1) - 64 * b) + phase_ref[0]
            grad = grad + dot(grad_ref[2 * pair + b], hot(iota((seg, 128), 0) == target))
        grad = grad.astype(HALFS)
        key = jnp.concatenate(
            [place_ref[HEAD_SIZE : 2 * HEAD_SIZE, spots]]
            + [far_ref[k, :HEAD_SIZE, lanes] for k in range(n)],
            axis=1,
        )
        value = jnp.concatenate(
            [place_ref[2 * HEAD_SIZE :, spots]]
            + [far_ref[k, HEAD_SIZE:, lanes] for k in range(n)],
            axis=1,
        )
        size = key.shape[1]
        row = iota((size, 128), 0)
        slide_of_key = jnp.where(row < 2 * seg, row // seg, (row & 127) >> 6)
        same = slide_of_key == iota((size, 128), 1) >> 6
        score = jnp.where(same, dot(key, query, "tn") * SCALE, -1e30)
        top = jnp.max(score, axis=0, keepdims=True)
        prob = jnp.exp(score - top)
        prob = prob * (1.0 / jnp.sum(prob, axis=0, keepdims=True))
        dprob = dot(value, grad, "tn")
        delta = jnp.sum(prob * dprob, axis=0, keepdims=True)
        dscore = (prob * (dprob - delta)).astype(HALFS)
        dquery_ref[:, lanes] = (dot(key, dscore) * SCALE).astype(HALFS)
        dkey = dot(query, dscore, "nt") * SCALE
        dvalue = dot(grad, prob.astype(HALFS), "nt")
        near_ref[:HEAD_SIZE, spots] = dkey[:, : 2 * seg]
        near_ref[HEAD_SIZE:, spots] = dvalue[:, : 2 * seg]
        for k in range(n):
            part = slice(2 * seg + k * 128, 2 * seg + (k + 1) * 128)
            out_ref[k, :HEAD_SIZE, lanes] = dkey[:, part].astype(HALFS)
            out_ref[k, HEAD_SIZE:, lanes] = dvalue[:, part].astype(HALFS)


def unplace_body(local_ref, near_ref, extra_ref, out_ref):
    places = near_ref.shape[1]
    block = out_ref.shape[1]
    local = local_ref[0:1, :]
    order = hot(local == iota((places, block), 0))
    query = near_ref[:HEAD_SIZE, :].astype(HALFS)
    rest = (near_ref[HEAD_SIZE:, :] + extra_ref[...]).astype(HALFS)
    out_ref[...] = dot(jnp.concatenate([query, rest], axis=0), order)


def finish_body(phase_ref, local_ref, main_ref, dquery_ref, far_ref, chunk_ref, rows_ref):
    far = far_ref[0].astype(FLOATS)
    for k in range(1, far_ref.shape[0]):
        far = far + far_ref[k].astype(FLOATS)
    sparse = jnp.concatenate([dquery_ref[...], far.astype(HALFS)], axis=0)
    local = local_ref[0:1, :]
    count = dquery_ref.shape[1]
    order = hot(local == 8 * iota((count, local.shape[1]), 0) + phase_ref[0])
    rows = (main_ref[...] + dot(sparse, order)).astype(HALFS)
    rows_ref[...] = rows
    for block in range(chunk_ref.shape[0] // WIDTH):
        chunk_ref[block * WIDTH : (block + 1) * WIDTH, :] = rows[
            :, block * 128 : (block + 1) * 128
        ]


def tiles_grad_body(rows_ref, weight_ref, keep_ref, give_ref, grad_ref, kept_ref, given_ref):
    grad = dot(weight_ref[...], rows_ref[...]).astype(HALFS)
    grad_ref[...] = grad
    given_ref[...] = dot(grad, give_ref[...]).astype(HALFS)
    kept_ref[...] = dot(grad, keep_ref[...])


def back_body(grad_ref, pick0_ref, pick1_ref, back_ref):
    half = back_ref.shape[1]
    back = dot(pick0_ref[...], grad_ref[:half], "nt")
    back = back + dot(pick1_ref[...], grad_ref[half:], "nt")
    back_ref[...] = back.astype(HALFS)


def collect_body(recv_ref, base_ref, out_ref):
    total, half = recv_ref.shape
    base, twin = base_ref[:, 0:1], base_ref[:, 1:2]
    rows = iota((base.shape[0], total), 1)
    both = hot((rows == base) | (rows == twin))
    out_ref[:, :half] = dot(both, recv_ref[...]).astype(HALFS)
    both = hot((rows == base + 1) | (rows == twin + 1))
    out_ref[:, half:] = dot(both, recv_ref[...]).astype(HALFS)


def per_device(tile_features, embed_weight, qkv_weight, positions, out_grad):
    n_slide = lax.axis_size("slide")
    n_tile = lax.axis_size("tile")
    devices = n_slide * n_tile
    every = ("slide", "tile")
    slots = tile_features.shape[0]
    slides, seg = out_grad.shape[0], out_grad.shape[1]
    wide = embed_weight.shape[1]
    half = wide // 2
    rows = slides * seg
    share = rows // n_tile
    row_here = lax.axis_index("slide")
    col_here = lax.axis_index("tile")
    phase = (col_here % n_slide).astype(jnp.int32).reshape(1)
    odd = (col_here % 2).astype(jnp.int32).reshape(1)
    core = row_here % 2
    tiles = tile_features.shape[1]

    with jax.named_scope("dispatch"):
        sent, base = call(
            dispatch_body,
            [shaped((devices * 8, tiles // 2)), shaped((slots, 128), jnp.int32)],
            [positions.reshape(1, slots), positions.reshape(slots, 1), tile_features],
        )
        arrived = lax.all_to_all(
            sent.reshape(devices, 8, tiles // 2), every, 0, 0, tiled=True
        ).reshape(devices * 8, tiles // 2)
    with jax.named_scope("project"):
        emb_rows, tile_rows, chunks, pick0, pick1 = call(
            project_body,
            [
                shaped((share, wide)),
                shaped((share, tiles)),
                shaped((n_tile * CHUNK_ROWS, 128)),
                shaped((devices * 8, 128)),
                shaped((devices * 8, 128)),
            ],
            [odd, arrived, embed_weight, qkv_weight],
            smem=(0,),
        )
        chunks = lax.all_to_all(
            chunks.reshape(n_tile, CHUNK_ROWS, 128), "tile", 0, 0, tiled=True
        ).reshape(n_tile * CHUNK_ROWS, 128)
    with jax.named_scope("dilated"):
        few = rows // n_slide
        query, far, head_rows, local = call(
            dilated_body,
            [
                shaped((HEAD_SIZE, few)),
                shaped((n_slide, 2 * HEAD_SIZE, few)),
                shaped((WIDTH, rows)),
                shaped((8, rows), jnp.int32),
            ],
            [phase, chunks],
            smem=(0,),
        )
        far = lax.all_to_all(far, "slide", 0, 0, tiled=True)
    with jax.named_scope("near"):
        grads = out_grad.transpose(0, 2, 1)
        placed, near = pl.pallas_call(
            near_body,
            grid=(slides,),
            out_shape=[shaped((WIDTH, rows)), shaped((WIDTH, rows), FLOATS)],
            in_specs=[
                whole(pltpu.SMEM),
                pl.BlockSpec((WIDTH, rows), lambda i: (0, 0)),
                pl.BlockSpec((8, rows), lambda i: (0, 0)),
                pl.BlockSpec((1, HEAD_SIZE, seg), lambda i: (i, 0, 0)),
            ],
            out_specs=[
                pl.BlockSpec((WIDTH, seg), lambda i: (0, i)),
                pl.BlockSpec((WIDTH, seg), lambda i: (0, i)),
            ],
            compiler_params=VMEM,
            cost_estimate=pl.CostEstimate(
                flops=8_000_000_000, bytes_accessed=8_000_000, transcendentals=1 << 20
            ),
        )(phase, head_rows, local, grads)
    with jax.named_scope("far"):
        dquery, extra, far_grads = call(
            far_body,
            [
                shaped((HEAD_SIZE, few)),
                shaped((2 * HEAD_SIZE, rows), FLOATS),
                shaped((n_slide, 2 * HEAD_SIZE, few)),
            ],
            [phase, query, placed, grads, far],
            smem=(0,),
        )
        far_grads = lax.all_to_all(far_grads, "slide", 0, 0, tiled=True)
    with jax.named_scope("unplace"):
        block = rows // 4
        main = pl.pallas_call(
            unplace_body,
            grid=(rows // block,),
            out_shape=shaped((WIDTH, rows), FLOATS),
            in_specs=[
                pl.BlockSpec((8, block), lambda i: (0, i)),
                pl.BlockSpec((WIDTH, rows), lambda i: (0, 0)),
                pl.BlockSpec((2 * HEAD_SIZE, rows), lambda i: (0, 0)),
            ],
            out_specs=pl.BlockSpec((WIDTH, block), lambda i: (0, i)),
            compiler_params=VMEM,
            cost_estimate=pl.CostEstimate(
                flops=4_000_000_000, bytes_accessed=4_000_000, transcendentals=0
            ),
        )(local, near, extra)
        back_chunks, d_rows = call(
            finish_body,
            [shaped((n_tile * WIDTH, 128)), shaped((WIDTH, rows))],
            [phase, local, main, dquery, far_grads],
            smem=(0,),
        )
        back_rows = lax.all_to_all(
            back_chunks.reshape(n_tile, WIDTH, 128), "tile", 0, 0, tiled=True
        ).reshape(n_tile * WIDTH, 128)
    with jax.named_scope("qkv_grad"):
        all_rows = lax.all_gather(emb_rows, "tile", axis=0, tiled=True)
        qkv_part = lax.dot_general(
            all_rows, d_rows, (((0,), (1,)), ((), ())), preferred_element_type=FLOATS
        ).astype(HALFS)
        qkv_parts = lax.all_to_all(
            qkv_part.reshape(n_slide, wide // n_slide, WIDTH), "slide", 0, 0, tiled=True
        )
        back_rows, qkv_parts = lax.optimization_barrier((back_rows, qkv_parts))
        qkv_grad = jnp.sum(qkv_parts.astype(FLOATS), axis=0)
    with jax.named_scope("tiles_grad"):
        narrow = tiles // n_slide
        split = tile_rows.reshape(share, n_slide // 2, 2, narrow)
        keep_cols = lax.dynamic_index_in_dim(split, core, 2, False).reshape(share, tiles // 2)
        give_cols = lax.dynamic_index_in_dim(split, 1 - core, 2, False).reshape(share, tiles // 2)
        grad_rows, kept, given = call(
            tiles_grad_body,
            [
                shaped((wide, share)),
                shaped((wide, tiles // 2), FLOATS),
                shaped((wide, tiles // 2)),
            ],
            [back_rows, qkv_weight, keep_cols, give_cols],
        )
        given = lax.ppermute(given, "slide", [(i, i ^ 1) for i in range(n_slide)])
    with jax.named_scope("back"):
        back = call(back_body, shaped((devices * 8, half)), [grad_rows, pick0, pick1])
        back = lax.all_to_all(
            back.reshape(devices, 8, half), every, 0, 0, tiled=True
        ).reshape(devices * 8, half)
        d_embedded = call(collect_body, shaped((slots, wide)), [back, base])
    with jax.named_scope("embed_grad"):
        kept = (kept + given.astype(FLOATS)).astype(HALFS)
        parts = lax.all_to_all(
            kept.reshape(n_tile, wide // n_tile, tiles // 2), "tile", 0, 0, tiled=True
        )
        part = jnp.sum(parts.astype(FLOATS), axis=0)
        part = part.reshape(wide // n_tile, n_slide // 2, narrow).transpose(1, 0, 2)
        same_core = [list(range(c, n_slide, 2)) for c in range(2)]
        part = lax.all_to_all(part, "slide", 0, 0, axis_index_groups=same_core, tiled=True)
        embed_grad = jnp.sum(part, axis=0).T
    with jax.named_scope("feature_grad"):
        feature_grad = lax.dot_general(
            d_embedded, embed_weight, (((1,), (1,)), ((), ())), preferred_element_type=FLOATS
        ).astype(HALFS)
    return feature_grad, embed_grad, qkv_grad


def solution(mesh):
    placed = (P(("slide", "tile"), None), P(), P(), P(("slide", "tile")), P(None, "slide", "tile"))
    return jax.shard_map(
        per_device,
        mesh=mesh,
        in_specs=placed,
        out_specs=(P(("slide", "tile"), None), P("slide", "tile"), P("slide", "tile")),
        check_vma=False,
    )
```

```python
import functools

import jax
import jax.numpy as jnp
from jax import lax
from jax.experimental import pallas as pl
from jax.experimental.pallas import tpu as pltpu
from jax.sharding import PartitionSpec as P

HEAD_SIZE = 48
WIDTH = 3 * HEAD_SIZE
CHUNK_ROWS = 160
FLOATS = jnp.float32
HALFS = jnp.bfloat16
SCALE = HEAD_SIZE ** (-0.5)
VMEM = pltpu.CompilerParams(vmem_limit_bytes=56 * 1024 * 1024)


def iota(shape, dim):
    return lax.broadcasted_iota(jnp.int32, shape, dim)


def hot(cond):
    return jnp.where(cond, 1.0, 0.0).astype(HALFS)


def dot(a, b, dims="nn"):
    contract = (0 if dims[0] == "t" else 1, 1 if dims[1] == "t" else 0)
    return lax.dot_general(
        a, b, (((contract[0],), (contract[1],)), ((), ())), preferred_element_type=FLOATS
    )


def whole(memory=pltpu.VMEM):
    return pl.BlockSpec(memory_space=memory)


def call(body, outs, args, smem=(), **kw):
    specs = [whole(pltpu.SMEM if i in smem else pltpu.VMEM) for i in range(len(args))]
    return pl.pallas_call(
        body,
        out_shape=outs,
        in_specs=specs,
        out_specs=jax.tree.map(lambda _: whole(), outs),
        compiler_params=VMEM,
        **kw,
    )(*args)


def shaped(shape, dtype=HALFS):
    return jax.ShapeDtypeStruct(shape, dtype)


def resident(shape, dtype=HALFS):
    return pltpu.VMEM(shape, dtype)


def stay(*values):
    return [pltpu.with_memory_space_constraint(value, pltpu.VMEM) for value in values]


def place(pos_ref):
    slots = pos_ref.shape[0]
    pos = pos_ref[...].reshape(1, slots)
    live = pos >= 0
    few = jnp.sum(jnp.where(live, 1, 0), axis=1, keepdims=True) <= 64
    pos = jnp.where(live, pos, 0)
    member = ((pos & 4095) >> 9 == iota((8, slots), 0)) & live
    upper = hot(iota((slots, slots), 0) < iota((slots, slots), 1))
    ranks = dot(hot(member), upper)
    rank = jnp.sum(jnp.where(member, ranks, 0.0), axis=0, keepdims=True).astype(jnp.int32)
    dest = ((pos & 4095) >> 9) * 128 + jnp.where(few, rank * 16, (rank & 15) * 8)
    dest = jnp.where(live, dest, -16)
    sub = jnp.where(few, 0, rank >> 4)
    mask = jnp.where(few, -9, -1)
    return pos, few, dest, sub, mask


def dispatch_body(pos_ref, tiles_ref, send_ref):
    slots = tiles_ref.shape[0]
    half = tiles_ref.shape[1] // 2
    pos, few, dest, sub, mask = place(pos_ref)
    base = dest + 2 * sub
    local = ((pos >> 12) << 9) + (pos & 511)
    lane = iota((128, slots), 0) - 4 * sub
    notes = jnp.where(
        lane == 0,
        (local >> 7) + 1,
        jnp.where(lane == 1, local & 127, jnp.where((lane == 2) & few, 1, 0)),
    )
    notes = notes.astype(FLOATS).astype(HALFS)
    step = 256
    for start in range(0, send_ref.shape[0], step):
        rows = (iota((step, slots), 0) + start) & mask
        out = dot(hot(rows == base), tiles_ref[:, :half])
        out = out + dot(hot(rows == base + 1), tiles_ref[:, half:])
        send_ref[start : start + step, :] = out.astype(HALFS)
        info = dot(hot(rows == dest + 6), notes, "nt")
        send_ref[start : start + step, :128] = (out[:, :128] + info).astype(HALFS)


def slots_body(pos_ref, base_ref):
    slots = pos_ref.shape[0]
    _, _, dest, sub, mask = place(pos_ref)
    same = iota((slots, slots), 0) == iota((slots, slots), 1)
    base = jnp.sum(jnp.where(same, dest + 2 * sub, 0), axis=1, keepdims=True)
    base_ref[...] = jnp.where(iota(base_ref.shape, 1) == 0, base, mask)


def project_body(
    odd_ref,
    recv_ref,
    embed_ref,
    weight_ref,
    emb_ref,
    tiles_ref,
    chunk_ref,
    pick0_ref,
    pick1_ref,
):
    total = recv_ref.shape[0]
    senders = total // 8
    sel = hot(iota((senders, total), 1) == 8 * iota((senders, total), 0) + 6)
    notes = dot(sel, recv_ref[:, :128])
    lane = iota((senders, 128), 1)
    lower = hot(iota((senders, senders), 0) > iota((senders, senders), 1))
    shared = (notes > 0.5) & (lane == 2)
    order = dot(lower, hot(shared)).astype(jnp.int32)
    other = shared & ((order & 1) != odd_ref[0])
    to_first = hot((iota((128, 128), 0) == 2) & (iota((128, 128), 1) == 0))
    other = dot(hot(other), to_first) > 0.5
    valid = (notes > 0.5) & ((lane & 3) == 0) & (lane < 12) & jnp.logical_not(other)
    cum = dot(lower, hot(valid))
    ones = jnp.where(valid, 1.0, 0.0)
    first = jnp.sum(jnp.where(lane == 0, ones, 0.0), axis=0, keepdims=True)
    first = jnp.sum(first, axis=1, keepdims=True)
    second = jnp.sum(jnp.where(lane == 4, ones, 0.0), axis=0, keepdims=True)
    second = jnp.sum(second, axis=1, keepdims=True)
    shift = jnp.where(lane >= 4, first, 0.0) + jnp.where(lane >= 8, second, 0.0)
    index = jnp.where(valid, cum + shift, -1.0)
    repeat = hot(iota((total, senders), 0) >> 3 == iota((total, senders), 1))
    index_all = dot(repeat, index.astype(HALFS))
    notes_all = dot(repeat, notes.astype(HALFS))
    turn = iota((total, 128), 0) & 7
    lanes = iota((total, 128), 1)
    mine = (lanes == 4 * (turn >> 1)) & (turn < 6)
    mine_low = (lanes == 4 * (turn >> 1) + 1) & (turn < 6)
    spot = jnp.sum(jnp.where(mine, index_all + 1.0, 0.0), axis=1, keepdims=True) - 1.0
    high = jnp.sum(jnp.where(mine, notes_all, 0.0), axis=1, keepdims=True)
    low = jnp.sum(jnp.where(mine_low, notes_all, 0.0), axis=1, keepdims=True)
    match = spot.astype(jnp.int32) == lanes
    pick0 = hot(match & ((turn & 1) == 0))
    pick1 = hot(match & ((turn & 1) == 1))
    pick0_ref[...] = pick0
    pick1_ref[...] = pick1
    half = recv_ref.shape[1]
    tiles_ref[:, :half] = dot(pick0, recv_ref[...], "tn").astype(HALFS)
    tiles_ref[:, half:] = dot(pick1, recv_ref[...], "tn").astype(HALFS)
    emb_ref[...] = dot(tiles_ref[...], embed_ref[...]).astype(HALFS)
    info = jnp.where(lanes == 0, high, jnp.where(lanes == 1, low, 0.0)).astype(HALFS)
    info = dot(info, pick0, "tn")[:16].astype(HALFS)
    heads = chunk_ref.shape[0] // CHUNK_ROWS
    for head in range(heads):
        top = head * CHUNK_ROWS
        if head % 8 == 0:
            wide = slice(head * WIDTH, (head + 8) * WIDTH)
            part = dot(emb_ref[...], weight_ref[:, wide]).T
        columns = slice((head % 8) * WIDTH, (head % 8 + 1) * WIDTH)
        chunk_ref[top : top + WIDTH, :] = part[columns].astype(HALFS)
        chunk_ref[top + WIDTH : top + CHUNK_ROWS, :] = info


def dilated_body(phase_ref, chunk_ref, query_ref, far_ref, rows_ref, local_ref):
    blocks = chunk_ref.shape[0] // CHUNK_ROWS
    total = jnp.zeros((WIDTH, query_ref.shape[1]), FLOATS)
    target = 8 * iota((query_ref.shape[1], 128), 0) + phase_ref[0]
    for block in range(blocks):
        top = block * CHUNK_ROWS
        lanes = slice(block * 128, (block + 1) * 128)
        part = chunk_ref[top : top + WIDTH, :]
        info = chunk_ref[top + WIDTH : top + CHUNK_ROWS, :].astype(FLOATS)
        local = ((info[0:1] - 1.0) * 128.0 + info[1:2]).astype(jnp.int32)
        rows_ref[:, lanes] = part
        local_ref[:, lanes] = jnp.broadcast_to(local, (8, 128))
        total = total + dot(part, hot(target == local), "nt")
    query_ref[...] = total[:HEAD_SIZE].astype(HALFS)
    for copy in range(far_ref.shape[0]):
        far_ref[copy] = total[HEAD_SIZE:].astype(HALFS)


def near_body(phase_ref, rows_ref, local_ref, grad_ref, place_ref, near_ref):
    seg = grad_ref.shape[2]
    local = local_ref[0:1, :]
    dilated = (iota((1, seg), 1) & 7) == phase_ref[0]
    for slide in range(grad_ref.shape[0]):
        spots = slice(slide * seg, (slide + 1) * seg)
        order = hot(local == iota((seg, local.shape[1]), 0) + slide * seg)
        parts = dot(rows_ref[...], order, "nt").astype(HALFS)
        place_ref[:, spots] = parts
        query = parts[:HEAD_SIZE]
        key = parts[HEAD_SIZE : 2 * HEAD_SIZE]
        value = parts[2 * HEAD_SIZE :]
        grad = grad_ref[slide]
        score = dot(key, query, "tn") * SCALE
        top = jnp.max(score, axis=0, keepdims=True)
        prob = jnp.exp(score - top)
        norm = 1.0 / jnp.sum(prob, axis=0, keepdims=True)
        prob = prob * jnp.where(dilated, 0.0, norm)
        dprob = dot(value, grad, "tn")
        delta = jnp.sum(prob * dprob, axis=0, keepdims=True)
        dscore = (prob * (dprob - delta)).astype(HALFS)
        near_ref[:HEAD_SIZE, spots] = dot(key, dscore) * SCALE
        near_ref[HEAD_SIZE : 2 * HEAD_SIZE, spots] = dot(query, dscore, "nt") * SCALE
        near_ref[2 * HEAD_SIZE :, spots] = dot(grad, prob.astype(HALFS), "nt")


def pick_body(phase_ref, grad_ref, out_ref):
    seg = grad_ref.shape[2]
    for pair in range(grad_ref.shape[0] // 2):
        grad = jnp.zeros((HEAD_SIZE, 128), FLOATS)
        for b in range(2):
            target = 8 * (iota((seg, 128), 1) - 64 * b) + phase_ref[0]
            grad = grad + dot(grad_ref[2 * pair + b], hot(iota((seg, 128), 0) == target))
        out_ref[:, pair * 128 : (pair + 1) * 128] = grad.astype(HALFS)


def far_body(query_ref, grad_ref, place_ref, far_ref, out_ref, dscore_ref, prob_ref):
    n = far_ref.shape[0]
    near = place_ref.shape[1] // 2
    seg = near // 2
    for pair in range(2):
        lanes = slice(pair * 128, (pair + 1) * 128)
        spots = slice(pair * near, (pair + 1) * near)
        query = query_ref[:, lanes]
        grad = grad_ref[:, lanes]
        key = jnp.concatenate(
            [place_ref[HEAD_SIZE : 2 * HEAD_SIZE, spots]]
            + [far_ref[k, :HEAD_SIZE, lanes] for k in range(n)],
            axis=1,
        )
        value = jnp.concatenate(
            [place_ref[2 * HEAD_SIZE :, spots]]
            + [far_ref[k, HEAD_SIZE:, lanes] for k in range(n)],
            axis=1,
        )
        size = key.shape[1]
        row = iota((size, 128), 0)
        slide_of_key = jnp.where(row < near, row // seg, (row & 127) >> 6)
        same = slide_of_key == iota((size, 128), 1) >> 6
        score = jnp.where(same, dot(key, query, "tn") * SCALE, -1e30)
        top = jnp.max(score, axis=0, keepdims=True)
        prob = jnp.exp(score - top)
        prob = prob * (1.0 / jnp.sum(prob, axis=0, keepdims=True))
        dprob = dot(value, grad, "tn")
        delta = jnp.sum(prob * dprob, axis=0, keepdims=True)
        dscore = (prob * (dprob - delta)).astype(HALFS)
        prob = prob.astype(HALFS)
        dkey = dot(query, dscore[near:], "nt") * SCALE
        dvalue = dot(grad, prob[near:], "nt")
        for k in range(n):
            part = slice(k * 128, (k + 1) * 128)
            out_ref[k, :HEAD_SIZE, lanes] = dkey[:, part].astype(HALFS)
            out_ref[k, HEAD_SIZE:, lanes] = dvalue[:, part].astype(HALFS)
        dscore_ref[pair] = dscore
        prob_ref[pair] = prob[:near]


def sum_body(
    query_ref,
    grad_ref,
    place_ref,
    far_ref,
    dscore_ref,
    prob_ref,
    near_ref,
    dquery_ref,
    sum_ref,
):
    near = place_ref.shape[1] // 2
    sum_ref[:HEAD_SIZE, :] = near_ref[:HEAD_SIZE, :].astype(HALFS)
    for pair in range(2):
        lanes = slice(pair * 128, (pair + 1) * 128)
        spots = slice(pair * near, (pair + 1) * near)
        query = query_ref[:, lanes]
        grad = grad_ref[:, lanes]
        key = jnp.concatenate(
            [place_ref[HEAD_SIZE : 2 * HEAD_SIZE, spots]]
            + [far_ref[k, :HEAD_SIZE, lanes] for k in range(far_ref.shape[0])],
            axis=1,
        )
        dscore = dscore_ref[pair]
        dquery_ref[:, lanes] = (dot(key, dscore) * SCALE).astype(HALFS)
        dkey = dot(query, dscore[:near], "nt") * SCALE
        dvalue = dot(grad, prob_ref[pair], "nt")
        middle = slice(HEAD_SIZE, 2 * HEAD_SIZE)
        sum_ref[middle, spots] = (near_ref[middle, spots] + dkey).astype(HALFS)
        last = slice(2 * HEAD_SIZE, WIDTH)
        sum_ref[last, spots] = (near_ref[last, spots] + dvalue).astype(HALFS)


def unplace_body(local_ref, sum_ref, out_ref):
    block = 512
    for start in range(0, out_ref.shape[1], block):
        lanes = slice(start, start + block)
        order = hot(local_ref[0:1, lanes] == iota((sum_ref.shape[1], block), 0))
        out_ref[:, lanes] = dot(sum_ref[...], order)


def finish_body(phase_ref, local_ref, main_ref, dquery_ref, far_ref, chunk_ref, rows_ref):
    far = far_ref[0].astype(FLOATS)
    for k in range(1, far_ref.shape[0]):
        far = far + far_ref[k].astype(FLOATS)
    sparse = jnp.concatenate([dquery_ref[...], far.astype(HALFS)], axis=0)
    local = local_ref[0:1, :]
    count = dquery_ref.shape[1]
    order = hot(local == 8 * iota((count, local.shape[1]), 0) + phase_ref[0])
    rows = (main_ref[...] + dot(sparse, order)).astype(HALFS)
    rows_ref[...] = rows
    for block in range(chunk_ref.shape[0] // WIDTH):
        chunk_ref[block * WIDTH : (block + 1) * WIDTH, :] = rows[
            :, block * 128 : (block + 1) * 128
        ]


def qkv_grad_body(grad_ref, rows_ref, out_ref):
    out_ref[...] = dot(grad_ref[...], rows_ref[...]).T


def tiles_grad_body(rows_ref, weight_ref, give_ref, grad_ref, given_ref):
    grad = dot(weight_ref[...], rows_ref[...]).astype(HALFS)
    grad_ref[...] = grad
    for block in range(give_ref.shape[0]):
        given_ref[block] = dot(give_ref[block], grad, "nt").astype(HALFS)


def merge_body(chip_ref, grad_ref, keep_ref, given_ref, own_ref, *piece_refs):
    chips = keep_ref.shape[0]
    for k in range(chips):
        block = (chip_ref[0] + k) & (chips - 1)
        part = dot(keep_ref[block], grad_ref[...], "nt") + given_ref[block].astype(FLOATS)
        if k == 0:
            own_ref[...] = part
        else:
            piece_refs[k - 1][...] = part.astype(HALFS)


def back_body(grad_ref, pick0_ref, pick1_ref, back_ref):
    half = back_ref.shape[1]
    back = dot(pick0_ref[...], grad_ref[:half], "nt")
    back = back + dot(pick1_ref[...], grad_ref[half:], "nt")
    back_ref[...] = back.astype(HALFS)


def collect_body(recv_ref, base_ref, out_ref):
    total, half = recv_ref.shape
    base, mask = base_ref[:, 0:1], base_ref[:, 1:2]
    rows = iota((base.shape[0], total), 1) & mask
    out_ref[:, :half] = dot(hot(rows == base), recv_ref[...]).astype(HALFS)
    out_ref[:, half:] = dot(hot(rows == base + 1), recv_ref[...]).astype(HALFS)


def per_device(tile_features, embed_weight, qkv_weight, positions, out_grad):
    n_slide = lax.axis_size("slide")
    n_tile = lax.axis_size("tile")
    devices = n_slide * n_tile
    every = ("slide", "tile")
    slots = tile_features.shape[0]
    slides, seg = out_grad.shape[0], out_grad.shape[1]
    wide = embed_weight.shape[1]
    half = wide // 2
    rows = slides * seg
    share = rows // n_tile
    row_here = lax.axis_index("slide")
    col_here = lax.axis_index("tile")
    phase = (col_here % n_slide).astype(jnp.int32).reshape(1)
    odd = (col_here % 2).astype(jnp.int32).reshape(1)
    core = row_here % 2
    tiles = tile_features.shape[1]

    with jax.named_scope("dispatch"):
        sent = call(
            dispatch_body, shaped((devices * 8, tiles // 2)), [positions, tile_features]
        )
        base = call(slots_body, resident((slots, 128), jnp.int32), [positions])
        arrived = lax.all_to_all(
            sent.reshape(devices, 8, tiles // 2), every, 0, 0, tiled=True
        ).reshape(devices * 8, tiles // 2)
    with jax.named_scope("project"):
        emb_rows, tile_rows, chunks, pick0, pick1 = call(
            project_body,
            [
                shaped((share, wide)),
                shaped((share, tiles)),
                shaped((n_tile * CHUNK_ROWS, 128)),
                resident((devices * 8, 128)),
                resident((devices * 8, 128)),
            ],
            [odd, *stay(arrived), embed_weight, qkv_weight],
            smem=(0,),
        )
        chunks = lax.all_to_all(
            chunks.reshape(n_tile, CHUNK_ROWS, 128), "tile", 0, 0, tiled=True
        ).reshape(n_tile * CHUNK_ROWS, 128)
    with jax.named_scope("dilated"):
        few = rows // n_slide
        query, far, head_rows, local = call(
            dilated_body,
            [
                resident((HEAD_SIZE, few)),
                shaped((n_slide, 2 * HEAD_SIZE, few)),
                resident((WIDTH, rows)),
                resident((8, rows), jnp.int32),
            ],
            [phase, *stay(chunks)],
            smem=(0,),
        )
        far = lax.all_to_all(far, "slide", 0, 0, tiled=True)
    with jax.named_scope("near"):
        grads = out_grad.transpose(0, 2, 1)
        dilated_grads = call(pick_body, resident((HEAD_SIZE, few)), [phase, grads], smem=(0,))
        placed, near = call(
            near_body,
            [resident((WIDTH, rows)), resident((WIDTH, rows), FLOATS)],
            [phase, *stay(head_rows, local), grads],
            smem=(0,),
            cost_estimate=pl.CostEstimate(
                flops=8_000_000_000, bytes_accessed=8_000_000, transcendentals=1 << 20
            ),
        )
    with jax.named_scope("far"):
        far_grads, dscores, probs = call(
            far_body,
            [
                shaped((n_slide, 2 * HEAD_SIZE, few)),
                resident((2, rows, 128)),
                resident((2, rows // 2, 128)),
            ],
            stay(query, dilated_grads, placed, far),
        )
        far_grads = lax.all_to_all(far_grads, "slide", 0, 0, tiled=True)
    with jax.named_scope("unplace"):
        dquery, summed = call(
            sum_body,
            [resident((HEAD_SIZE, few)), resident((WIDTH, rows))],
            stay(query, dilated_grads, placed, far, dscores, probs, near),
        )
        main = call(
            unplace_body,
            resident((WIDTH, rows), FLOATS),
            stay(local, summed),
            cost_estimate=pl.CostEstimate(
                flops=4_000_000_000, bytes_accessed=4_000_000, transcendentals=0
            ),
        )
        back_chunks, d_rows = call(
            finish_body,
            [shaped((n_tile * WIDTH, 128)), resident((WIDTH, rows))],
            [phase, *stay(local, main, dquery, far_grads)],
            smem=(0,),
        )
        back_rows = lax.all_to_all(
            back_chunks.reshape(n_tile, WIDTH, 128), "tile", 0, 0, tiled=True
        ).reshape(n_tile * WIDTH, 128)
    with jax.named_scope("qkv_grad"):
        all_rows = lax.all_gather(emb_rows, "tile", axis=0, tiled=True)
        qkv_part = call(
            qkv_grad_body, shaped((wide, WIDTH), FLOATS), [*stay(d_rows), all_rows]
        )
        back_rows, qkv_part = lax.optimization_barrier((back_rows, qkv_part))
        qkv_grad = lax.psum_scatter(qkv_part, "slide", scatter_dimension=0, tiled=True)
    with jax.named_scope("tiles_grad"):
        narrow = tiles // n_slide
        chips = n_slide // 2
        split = tile_rows.reshape(share, chips, 2, narrow)
        keep_cols = lax.dynamic_index_in_dim(split, core, 2, False).transpose(1, 2, 0)
        give_cols = lax.dynamic_index_in_dim(split, 1 - core, 2, False).transpose(1, 2, 0)
        grad_rows, given = call(
            tiles_grad_body,
            [resident((wide, share)), shaped((chips, narrow, wide))],
            [*stay(back_rows), qkv_weight, give_cols],
        )
        given = lax.ppermute(given, "slide", [(i, i ^ 1) for i in range(n_slide)])
        own, *pieces = call(
            merge_body,
            [shaped((narrow, wide), FLOATS)] + [shaped((narrow, wide))] * (chips - 1),
            [(row_here // 2).astype(jnp.int32).reshape(1), *stay(grad_rows), keep_cols, *stay(given)],
            smem=(0,),
        )
    with jax.named_scope("back"):
        back = call(back_body, shaped((devices * 8, half)), stay(grad_rows, pick0, pick1))
        back, pieces = lax.optimization_barrier((back, pieces))
        part = own
        for k in range(1, chips):
            piece = lax.ppermute(
                pieces[k - 1], "slide", [(i, (i + 2 * k) % n_slide) for i in range(n_slide)]
            )
            part = part + piece.astype(FLOATS)
        part = part.astype(HALFS).T
        back = lax.all_to_all(
            back.reshape(devices, 8, half), every, 0, 0, tiled=True
        ).reshape(devices * 8, half)
        back, part = lax.optimization_barrier((back, part))
        d_embedded = call(collect_body, shaped((slots, wide)), stay(back, base))
    with jax.named_scope("embed_grad"):
        parts = lax.all_to_all(
            part.reshape(n_tile, wide // n_tile, narrow), "tile", 0, 0, tiled=True
        )
        parts, qkv_grad = lax.optimization_barrier((parts, qkv_grad))
        embed_grad = jnp.sum(parts.astype(FLOATS), axis=0).T
    with jax.named_scope("feature_grad"):
        feature_grad = lax.dot_general(
            d_embedded, embed_weight, (((1,), (1,)), ((), ())), preferred_element_type=FLOATS
        ).astype(HALFS)
    return feature_grad, embed_grad, qkv_grad


def solution(mesh):
    placed = (P(("slide", "tile"), None), P(), P(), P(("slide", "tile")), P(None, "slide", "tile"))
    return jax.shard_map(
        per_device,
        mesh=mesh,
        in_specs=placed,
        out_specs=(P(("slide", "tile"), None), P("slide", "tile"), P("slide", "tile")),
        check_vma=False,
    )
```

```python
import functools

import jax
import jax.numpy as jnp
from jax import lax
from jax.experimental import pallas as pl
from jax.experimental.pallas import tpu as pltpu
from jax.sharding import PartitionSpec as P

HEAD_SIZE = 48
WIDTH = 3 * HEAD_SIZE
CHUNK_ROWS = 160
FLOATS = jnp.float32
HALFS = jnp.bfloat16
SCALE = HEAD_SIZE ** (-0.5)
VMEM = pltpu.CompilerParams(vmem_limit_bytes=56 * 1024 * 1024)


def iota(shape, dim):
    return lax.broadcasted_iota(jnp.int32, shape, dim)


def hot(cond):
    return jnp.where(cond, 1.0, 0.0).astype(HALFS)


def dot(a, b, dims="nn"):
    contract = (0 if dims[0] == "t" else 1, 1 if dims[1] == "t" else 0)
    return lax.dot_general(
        a, b, (((contract[0],), (contract[1],)), ((), ())), preferred_element_type=FLOATS
    )


def whole(memory=pltpu.VMEM):
    return pl.BlockSpec(memory_space=memory)


def call(body, outs, args, smem=(), anywhere=(), **kw):
    specs = [whole(pltpu.SMEM if i in smem else pltpu.VMEM) for i in range(len(args))]
    for i in anywhere:
        specs[i] = whole(pl.ANY)
    out_specs = jax.tree.map(lambda _: whole(), outs)
    return pl.pallas_call(
        body,
        out_shape=outs,
        in_specs=specs,
        out_specs=out_specs,
        compiler_params=VMEM,
        **kw,
    )(*args)


def shaped(shape, dtype=HALFS):
    return jax.ShapeDtypeStruct(shape, dtype)


def resident(shape, dtype=HALFS):
    return pltpu.VMEM(shape, dtype)


def stay(*values):
    return [pltpu.with_memory_space_constraint(value, pltpu.VMEM) for value in values]


def place(pos_ref):
    slots = pos_ref.shape[0]
    pos = pos_ref[...].reshape(1, slots)
    live = pos >= 0
    few = jnp.sum(jnp.where(live, 1, 0), axis=1, keepdims=True) <= 64
    pos = jnp.where(live, pos, 0)
    member = ((pos & 4095) >> 9 == iota((8, slots), 0)) & live
    upper = hot(iota((slots, slots), 0) < iota((slots, slots), 1))
    ranks = dot(hot(member), upper)
    rank = jnp.sum(jnp.where(member, ranks, 0.0), axis=0, keepdims=True).astype(jnp.int32)
    dest = ((pos & 4095) >> 9) * 128 + jnp.where(few, rank * 16, (rank & 15) * 8)
    dest = jnp.where(live, dest, -16)
    sub = jnp.where(few, 0, rank >> 4)
    mask = jnp.where(few, -9, -1)
    return pos, few, dest, sub, mask


def dispatch_body(pos_ref, tiles_ref, send_ref):
    slots = tiles_ref.shape[0]
    half = tiles_ref.shape[1] // 2
    pos, few, dest, sub, mask = place(pos_ref)
    base = dest + 2 * sub
    local = ((pos >> 12) << 9) + (pos & 511)
    lane = iota((128, slots), 0) - 4 * sub
    notes = jnp.where(
        lane == 0,
        (local >> 7) + 1,
        jnp.where(lane == 1, local & 127, jnp.where((lane == 2) & few, 1, 0)),
    )
    notes = notes.astype(FLOATS).astype(HALFS)
    step = 256
    for start in range(0, send_ref.shape[0], step):
        rows = (iota((step, slots), 0) + start) & mask
        out = dot(hot(rows == base), tiles_ref[:, :half])
        out = out + dot(hot(rows == base + 1), tiles_ref[:, half:])
        send_ref[start : start + step, :] = out.astype(HALFS)
        info = dot(hot(rows == dest + 6), notes, "nt")
        send_ref[start : start + step, :128] = (out[:, :128] + info).astype(HALFS)


def slots_body(pos_ref, base_ref):
    slots = pos_ref.shape[0]
    _, _, dest, sub, mask = place(pos_ref)
    same = iota((slots, slots), 0) == iota((slots, slots), 1)
    base = jnp.sum(jnp.where(same, dest + 2 * sub, 0), axis=1, keepdims=True)
    base_ref[...] = jnp.where(iota(base_ref.shape, 1) == 0, base, mask)


def project_body(
    odd_ref,
    recv_ref,
    embed_hbm_ref,
    weight_hbm_ref,
    emb_ref,
    tiles_ref,
    chunk_ref,
    pick0_ref,
    pick1_ref,
    embed_ref,
    weight_ref,
    embed_sem,
    weight_sem,
):
    embed_load = pltpu.make_async_copy(embed_hbm_ref, embed_ref, embed_sem)
    embed_load.start()
    weight_load = pltpu.make_async_copy(weight_hbm_ref, weight_ref, weight_sem)
    weight_load.start()
    total = recv_ref.shape[0]
    senders = total // 8
    sel = hot(iota((senders, total), 1) == 8 * iota((senders, total), 0) + 6)
    notes = dot(sel, recv_ref[:, :128])
    lane = iota((senders, 128), 1)
    lower = hot(iota((senders, senders), 0) > iota((senders, senders), 1))
    shared = (notes > 0.5) & (lane == 2)
    order = dot(lower, hot(shared)).astype(jnp.int32)
    other = shared & ((order & 1) != odd_ref[0])
    to_first = hot((iota((128, 128), 0) == 2) & (iota((128, 128), 1) == 0))
    other = dot(hot(other), to_first) > 0.5
    valid = (notes > 0.5) & ((lane & 3) == 0) & (lane < 12) & jnp.logical_not(other)
    cum = dot(lower, hot(valid))
    ones = jnp.where(valid, 1.0, 0.0)
    first = jnp.sum(jnp.where(lane == 0, ones, 0.0), axis=0, keepdims=True)
    first = jnp.sum(first, axis=1, keepdims=True)
    second = jnp.sum(jnp.where(lane == 4, ones, 0.0), axis=0, keepdims=True)
    second = jnp.sum(second, axis=1, keepdims=True)
    shift = jnp.where(lane >= 4, first, 0.0) + jnp.where(lane >= 8, second, 0.0)
    index = jnp.where(valid, cum + shift, -1.0)
    repeat = hot(iota((total, senders), 0) >> 3 == iota((total, senders), 1))
    index_all = dot(repeat, index.astype(HALFS))
    notes_all = dot(repeat, notes.astype(HALFS))
    turn = iota((total, 128), 0) & 7
    lanes = iota((total, 128), 1)
    mine = (lanes == 4 * (turn >> 1)) & (turn < 6)
    mine_low = (lanes == 4 * (turn >> 1) + 1) & (turn < 6)
    spot = jnp.sum(jnp.where(mine, index_all + 1.0, 0.0), axis=1, keepdims=True) - 1.0
    high = jnp.sum(jnp.where(mine, notes_all, 0.0), axis=1, keepdims=True)
    low = jnp.sum(jnp.where(mine_low, notes_all, 0.0), axis=1, keepdims=True)
    match = spot.astype(jnp.int32) == lanes
    pick0 = hot(match & ((turn & 1) == 0))
    pick1 = hot(match & ((turn & 1) == 1))
    pick0_ref[...] = pick0
    pick1_ref[...] = pick1
    half = recv_ref.shape[1]
    tiles_ref[:, :half] = dot(pick0, recv_ref[...], "tn").astype(HALFS)
    tiles_ref[:, half:] = dot(pick1, recv_ref[...], "tn").astype(HALFS)
    embed_load.wait()
    emb_ref[...] = dot(tiles_ref[...], embed_ref[...]).astype(HALFS)
    info = jnp.where(lanes == 0, high, jnp.where(lanes == 1, low, 0.0)).astype(HALFS)
    info = dot(info, pick0, "tn")[:16].astype(HALFS)
    weight_load.wait()
    heads = chunk_ref.shape[0] // CHUNK_ROWS
    for head in range(heads):
        top = head * CHUNK_ROWS
        if head % 8 == 0:
            wide = slice(head * WIDTH, (head + 8) * WIDTH)
            part = dot(emb_ref[...], weight_ref[:, wide]).T
        columns = slice((head % 8) * WIDTH, (head % 8 + 1) * WIDTH)
        chunk_ref[top : top + WIDTH, :] = part[columns].astype(HALFS)
        chunk_ref[top + WIDTH : top + CHUNK_ROWS, :] = info


def dilated_body(phase_ref, chunk_ref, query_ref, far_ref, rows_ref, local_ref):
    blocks = chunk_ref.shape[0] // CHUNK_ROWS
    total = jnp.zeros((WIDTH, query_ref.shape[1]), FLOATS)
    target = 8 * iota((query_ref.shape[1], 128), 0) + phase_ref[0]
    for block in range(blocks):
        top = block * CHUNK_ROWS
        lanes = slice(block * 128, (block + 1) * 128)
        part = chunk_ref[top : top + WIDTH, :]
        info = chunk_ref[top + WIDTH : top + CHUNK_ROWS, :].astype(FLOATS)
        local = ((info[0:1] - 1.0) * 128.0 + info[1:2]).astype(jnp.int32)
        rows_ref[:, lanes] = part
        local_ref[:, lanes] = jnp.broadcast_to(local, (8, 128))
        total = total + dot(part, hot(target == local), "nt")
    query_ref[...] = total[:HEAD_SIZE].astype(HALFS)
    for copy in range(far_ref.shape[0]):
        far_ref[copy] = total[HEAD_SIZE:].astype(HALFS)


def near_body(phase_ref, rows_ref, local_ref, grad_ref, place_ref, near_ref):
    seg = grad_ref.shape[2]
    local = local_ref[0:1, :]
    dilated = (iota((1, seg), 1) & 7) == phase_ref[0]
    for slide in range(grad_ref.shape[0]):
        spots = slice(slide * seg, (slide + 1) * seg)
        order = hot(local == iota((seg, local.shape[1]), 0) + slide * seg)
        parts = dot(rows_ref[...], order, "nt").astype(HALFS)
        place_ref[:, spots] = parts
        query = parts[:HEAD_SIZE]
        key = parts[HEAD_SIZE : 2 * HEAD_SIZE]
        value = parts[2 * HEAD_SIZE :]
        grad = grad_ref[slide]
        score = dot(key, query, "tn") * SCALE
        top = jnp.max(score, axis=0, keepdims=True)
        prob = jnp.exp(score - top)
        norm = 1.0 / jnp.sum(prob, axis=0, keepdims=True)
        prob = prob * jnp.where(dilated, 0.0, norm)
        dprob = dot(value, grad, "tn")
        delta = jnp.sum(prob * dprob, axis=0, keepdims=True)
        dscore = (prob * (dprob - delta)).astype(HALFS)
        near_ref[:HEAD_SIZE, spots] = dot(key, dscore) * SCALE
        near_ref[HEAD_SIZE : 2 * HEAD_SIZE, spots] = dot(query, dscore, "nt") * SCALE
        near_ref[2 * HEAD_SIZE :, spots] = dot(grad, prob.astype(HALFS), "nt")


def pick_body(phase_ref, grad_ref, out_ref):
    seg = grad_ref.shape[2]
    for pair in range(grad_ref.shape[0] // 2):
        grad = jnp.zeros((HEAD_SIZE, 128), FLOATS)
        for b in range(2):
            target = 8 * (iota((seg, 128), 1) - 64 * b) + phase_ref[0]
            grad = grad + dot(grad_ref[2 * pair + b], hot(iota((seg, 128), 0) == target))
        out_ref[:, pair * 128 : (pair + 1) * 128] = grad.astype(HALFS)


def far_body(query_ref, grad_ref, place_ref, far_ref, out_ref, dscore_ref, prob_ref):
    n = far_ref.shape[0]
    near = place_ref.shape[1] // 2
    seg = near // 2
    for pair in range(2):
        lanes = slice(pair * 128, (pair + 1) * 128)
        spots = slice(pair * near, (pair + 1) * near)
        query = query_ref[:, lanes]
        grad = grad_ref[:, lanes]
        key = jnp.concatenate(
            [place_ref[HEAD_SIZE : 2 * HEAD_SIZE, spots]]
            + [far_ref[k, :HEAD_SIZE, lanes] for k in range(n)],
            axis=1,
        )
        value = jnp.concatenate(
            [place_ref[2 * HEAD_SIZE :, spots]]
            + [far_ref[k, HEAD_SIZE:, lanes] for k in range(n)],
            axis=1,
        )
        size = key.shape[1]
        row = iota((size, 128), 0)
        slide_of_key = jnp.where(row < near, row // seg, (row & 127) >> 6)
        same = slide_of_key == iota((size, 128), 1) >> 6
        score = jnp.where(same, dot(key, query, "tn") * SCALE, -1e30)
        top = jnp.max(score, axis=0, keepdims=True)
        prob = jnp.exp(score - top)
        prob = prob * (1.0 / jnp.sum(prob, axis=0, keepdims=True))
        dprob = dot(value, grad, "tn")
        delta = jnp.sum(prob * dprob, axis=0, keepdims=True)
        dscore = (prob * (dprob - delta)).astype(HALFS)
        prob = prob.astype(HALFS)
        dkey = dot(query, dscore[near:], "nt") * SCALE
        dvalue = dot(grad, prob[near:], "nt")
        for k in range(n):
            part = slice(k * 128, (k + 1) * 128)
            out_ref[k, :HEAD_SIZE, lanes] = dkey[:, part].astype(HALFS)
            out_ref[k, HEAD_SIZE:, lanes] = dvalue[:, part].astype(HALFS)
        dscore_ref[pair] = dscore
        prob_ref[pair] = prob[:near]


def sum_body(
    query_ref,
    grad_ref,
    place_ref,
    far_ref,
    dscore_ref,
    prob_ref,
    near_ref,
    dquery_ref,
    sum_ref,
):
    near = place_ref.shape[1] // 2
    sum_ref[:HEAD_SIZE, :] = near_ref[:HEAD_SIZE, :].astype(HALFS)
    for pair in range(2):
        lanes = slice(pair * 128, (pair + 1) * 128)
        spots = slice(pair * near, (pair + 1) * near)
        query = query_ref[:, lanes]
        grad = grad_ref[:, lanes]
        key = jnp.concatenate(
            [place_ref[HEAD_SIZE : 2 * HEAD_SIZE, spots]]
            + [far_ref[k, :HEAD_SIZE, lanes] for k in range(far_ref.shape[0])],
            axis=1,
        )
        dscore = dscore_ref[pair]
        dquery_ref[:, lanes] = (dot(key, dscore) * SCALE).astype(HALFS)
        dkey = dot(query, dscore[:near], "nt") * SCALE
        dvalue = dot(grad, prob_ref[pair], "nt")
        middle = slice(HEAD_SIZE, 2 * HEAD_SIZE)
        sum_ref[middle, spots] = (near_ref[middle, spots] + dkey).astype(HALFS)
        last = slice(2 * HEAD_SIZE, WIDTH)
        sum_ref[last, spots] = (near_ref[last, spots] + dvalue).astype(HALFS)


def unplace_body(local_ref, sum_ref, out_ref):
    block = 512
    for start in range(0, out_ref.shape[1], block):
        lanes = slice(start, start + block)
        order = hot(local_ref[0:1, lanes] == iota((sum_ref.shape[1], block), 0))
        out_ref[:, lanes] = dot(sum_ref[...], order)


def finish_body(phase_ref, local_ref, main_ref, dquery_ref, far_ref, chunk_ref, rows_ref):
    far = far_ref[0].astype(FLOATS)
    for k in range(1, far_ref.shape[0]):
        far = far + far_ref[k].astype(FLOATS)
    sparse = jnp.concatenate([dquery_ref[...], far.astype(HALFS)], axis=0)
    local = local_ref[0:1, :]
    count = dquery_ref.shape[1]
    order = hot(local == 8 * iota((count, local.shape[1]), 0) + phase_ref[0])
    rows = (main_ref[...] + dot(sparse, order)).astype(HALFS)
    rows_ref[...] = rows
    for block in range(chunk_ref.shape[0] // WIDTH):
        chunk_ref[block * WIDTH : (block + 1) * WIDTH, :] = rows[
            :, block * 128 : (block + 1) * 128
        ]


def qkv_grad_body(core_ref, grad_ref, rows_ref, keep_ref, give_ref, all_ref):
    block = keep_ref.shape[1]
    part = dot(grad_ref[...], rows_ref[...]).T
    all_ref[...] = jnp.concatenate([part, jnp.zeros_like(part[:, : 256 - WIDTH])], axis=1)
    for chip in range(keep_ref.shape[0]):
        mine = pl.multiple_of((2 * chip + core_ref[0]) * block, block)
        other = pl.multiple_of((2 * chip + 1 - core_ref[0]) * block, block)
        keep_ref[chip] = all_ref[pl.ds(mine, block), :]
        give_ref[chip] = all_ref[pl.ds(other, block), :].astype(HALFS)


def give_body(grad_ref, give_ref, given_ref):
    given_ref[...] = dot(grad_ref[...], give_ref[...]).astype(HALFS)


def merge_body(grad_ref, keep_ref, given_ref, out_ref):
    rows, size = out_ref.shape[1] * 2 // 3, 128
    part = dot(grad_ref[...], keep_ref[...]) + given_ref[...].astype(FLOATS)
    part = part.astype(HALFS)
    columns = part.shape[0] // rows
    for block in range(out_ref.shape[0] // columns):
        left = block // 2 * 3 * size
        first = left if block % 2 == 0 else left + 2 * size
        other = left + size if block % 2 == 0 else left + size + 64
        for column in range(columns):
            here = part[column * rows : (column + 1) * rows]
            spot = block * columns + column
            out_ref[spot, :rows, :] = here[:, first : first + size]
            rest = here[:, other : other + 64]
            out_ref[spot, rows:, :] = jnp.concatenate(
                [rest[: rows // 2], rest[rows // 2 :]], axis=1
            )


def merge_qkv_body(chip_ref, keep_ref, given_ref, own_ref, *piece_refs):
    chips = keep_ref.shape[0]
    for k in range(chips):
        block = (chip_ref[0] + k) & (chips - 1)
        part = keep_ref[block] + given_ref[block].astype(FLOATS)
        if k == 0:
            own_ref[...] = part
        else:
            piece_refs[k - 1][...] = part.astype(HALFS)


def last_body(chip_ref, parts_ref, own_ref, *refs):
    piece_refs, embed_ref, qkv_ref = refs[:-2], refs[-2], refs[-1]
    total = parts_ref[0].astype(FLOATS)
    for k in range(1, parts_ref.shape[0]):
        total = total + parts_ref[k].astype(FLOATS)
    rest = jnp.concatenate([total[48:, :64], total[48:, 64:]], axis=0)
    even = jnp.concatenate([total[:48], rest], axis=1)
    odd = jnp.concatenate([rest, total[:48]], axis=1)
    embed_ref[...] = jnp.where((chip_ref[0] & 1) == 0, even, odd)
    qkv = own_ref[...]
    for ref in piece_refs:
        qkv = qkv + ref[...].astype(FLOATS)
    qkv_ref[...] = qkv.T[:WIDTH]


def back_body(rows_ref, weight_ref, pick0_ref, pick1_ref, grad_ref, back_ref):
    half = back_ref.shape[1]
    grad = dot(weight_ref[...], rows_ref[...]).astype(HALFS)
    grad_ref[...] = grad
    back = dot(pick0_ref[...], grad[:half], "nt") + dot(pick1_ref[...], grad[half:], "nt")
    back_ref[...] = back.astype(HALFS)


def collect_body(recv_ref, base_ref, out_ref):
    total, half = recv_ref.shape
    base, mask = base_ref[:, 0:1], base_ref[:, 1:2]
    rows = iota((base.shape[0], total), 1) & mask
    out_ref[:, :half] = dot(hot(rows == base), recv_ref[...]).astype(HALFS)
    out_ref[:, half:] = dot(hot(rows == base + 1), recv_ref[...]).astype(HALFS)


def per_device(tile_features, embed_weight, qkv_weight, positions, out_grad):
    n_slide = lax.axis_size("slide")
    n_tile = lax.axis_size("tile")
    devices = n_slide * n_tile
    every = ("slide", "tile")
    slots = tile_features.shape[0]
    slides, seg = out_grad.shape[0], out_grad.shape[1]
    wide = embed_weight.shape[1]
    half = wide // 2
    rows = slides * seg
    share = rows // n_tile
    row_here = lax.axis_index("slide")
    col_here = lax.axis_index("tile")
    phase = (col_here % n_slide).astype(jnp.int32).reshape(1)
    odd = (col_here % 2).astype(jnp.int32).reshape(1)
    core = row_here % 2
    tiles = tile_features.shape[1]

    with jax.named_scope("dispatch"):
        sent = call(
            dispatch_body, resident((devices * 8, tiles // 2)), [positions, tile_features]
        )
        base = call(slots_body, resident((slots, 128), jnp.int32), [positions])
        arrived = lax.all_to_all(
            sent.reshape(devices, 8, tiles // 2), every, 0, 0, tiled=True
        ).reshape(devices * 8, tiles // 2)
    with jax.named_scope("project"):
        emb_rows, tile_rows, chunks, pick0, pick1 = call(
            project_body,
            [
                shaped((share, wide)),
                shaped((share, tiles)),
                resident((n_tile * CHUNK_ROWS, 128)),
                shaped((devices * 8, 128)),
                shaped((devices * 8, 128)),
            ],
            [odd, *stay(arrived), embed_weight, qkv_weight],
            smem=(0,),
            anywhere=(2, 3),
            scratch_shapes=[
                pltpu.VMEM(embed_weight.shape, HALFS),
                pltpu.VMEM(qkv_weight.shape, HALFS),
                pltpu.SemaphoreType.DMA,
                pltpu.SemaphoreType.DMA,
            ],
        )
        chunks = lax.all_to_all(
            chunks.reshape(n_tile, CHUNK_ROWS, 128), "tile", 0, 0, tiled=True
        ).reshape(n_tile * CHUNK_ROWS, 128)
    with jax.named_scope("dilated"):
        few = rows // n_slide
        query, far, head_rows, local = call(
            dilated_body,
            [
                resident((HEAD_SIZE, few)),
                resident((n_slide, 2 * HEAD_SIZE, few)),
                shaped((WIDTH, rows)),
                resident((8, rows), jnp.int32),
            ],
            [phase, *stay(chunks)],
            smem=(0,),
        )
        far = lax.all_to_all(far, "slide", 0, 0, tiled=True)
    with jax.named_scope("near"):
        grads = out_grad.transpose(0, 2, 1)
        dilated_grads = call(pick_body, resident((HEAD_SIZE, few)), [phase, grads], smem=(0,))
        placed, near = call(
            near_body,
            [resident((WIDTH, rows)), resident((WIDTH, rows), FLOATS)],
            [phase, head_rows, *stay(local), grads],
            smem=(0,),
            cost_estimate=pl.CostEstimate(
                flops=8_000_000_000, bytes_accessed=8_000_000, transcendentals=1 << 20
            ),
        )
    with jax.named_scope("far"):
        far_grads, dscores, probs = call(
            far_body,
            [
                resident((n_slide, 2 * HEAD_SIZE, few)),
                shaped((2, rows, 128)),
                shaped((2, rows // 2, 128)),
            ],
            stay(query, dilated_grads, placed, far),
        )
        far_grads = lax.all_to_all(far_grads, "slide", 0, 0, tiled=True)
    with jax.named_scope("unplace"):
        dquery, summed = call(
            sum_body,
            [resident((HEAD_SIZE, few)), resident((WIDTH, rows))],
            [*stay(query, dilated_grads, placed, far), dscores, probs, *stay(near)],
        )
        main = call(
            unplace_body,
            resident((WIDTH, rows), FLOATS),
            stay(local, summed),
            cost_estimate=pl.CostEstimate(
                flops=4_000_000_000, bytes_accessed=4_000_000, transcendentals=0
            ),
        )
        back_chunks, d_rows = call(
            finish_body,
            [resident((n_tile * WIDTH, 128)), shaped((WIDTH, rows))],
            [phase, *stay(local, main, dquery, far_grads)],
            smem=(0,),
        )
        back_rows = lax.all_to_all(
            back_chunks.reshape(n_tile, WIDTH, 128), "tile", 0, 0, tiled=True
        ).reshape(n_tile * WIDTH, 128)
    with jax.named_scope("qkv_grad"):
        all_rows = lax.all_gather(emb_rows, "tile", axis=0, tiled=True)
        chips = n_slide // 2
        block = wide // n_slide
        keep_qkv, give_qkv = call(
            qkv_grad_body,
            [shaped((chips, block, 256), FLOATS), shaped((chips, block, 256))],
            [core.astype(jnp.int32).reshape(1), d_rows, all_rows],
            smem=(0,),
            scratch_shapes=[pltpu.VMEM((wide, 256), FLOATS)],
        )
        chip = (row_here // 2).astype(jnp.int32).reshape(1)
        swap = [(i, i ^ 1) for i in range(n_slide)]
        given_qkv = lax.ppermute(give_qkv, "slide", swap)
        own_qkv, *pieces = call(
            merge_qkv_body,
            [shaped((block, 256), FLOATS)] + [shaped((block, 256))] * (chips - 1),
            [chip, keep_qkv, given_qkv],
            smem=(0,),
        )
        pieces = [
            lax.ppermute(
                pieces[k - 1], "slide", [(i, (i + 2 * k) % n_slide) for i in range(n_slide)]
            )
            for k in range(1, chips)
        ]
    with jax.named_scope("tiles_grad"):
        narrow = tiles // n_slide
        split = tile_rows.reshape(share, chips, 2, narrow)
        keep_cols = lax.dynamic_index_in_dim(split, core, 2, False).reshape(share, tiles // 2)
        give_cols = lax.dynamic_index_in_dim(split, 1 - core, 2, False).reshape(share, tiles // 2)
        grad_rows, back = call(
            back_body,
            [shaped((wide, share)), shaped((devices * 8, half))],
            [*stay(back_rows), qkv_weight, pick0, pick1],
        )
        back = lax.all_to_all(
            back.reshape(devices, 8, half), every, 0, 0, tiled=True
        ).reshape(devices * 8, half)
        given = call(give_body, shaped((wide, tiles // 2)), [grad_rows, give_cols])
        given = lax.ppermute(given, "slide", swap)
        merged = call(
            merge_body, shaped((chips * n_tile, 72, 128)), [grad_rows, keep_cols, given]
        )
        merged, back = lax.optimization_barrier((merged, back))
    with jax.named_scope("collect"):
        d_embedded = call(collect_body, shaped((slots, wide)), stay(back, base))
    with jax.named_scope("embed_grad"):
        same_core = [
            [(2 * z + c) * n_tile + t for z in range(chips) for t in range(n_tile)]
            for c in range(2)
        ]
        parts = lax.all_to_all(
            merged, every, 0, 0, axis_index_groups=same_core, tiled=True
        )
        embed_grad, qkv_grad = call(
            last_body,
            [shaped((wide // n_tile, narrow), FLOATS), shaped((WIDTH, wide // n_slide), FLOATS)],
            [chip, *stay(parts), own_qkv, *pieces],
            smem=(0,),
        )
        embed_grad, qkv_grad = embed_grad.T, qkv_grad.T
    with jax.named_scope("feature_grad"):
        feature_grad = lax.dot_general(
            d_embedded, embed_weight, (((1,), (1,)), ((), ())), preferred_element_type=FLOATS
        ).astype(HALFS)
    return feature_grad, embed_grad, qkv_grad


def solution(mesh):
    placed = (P(("slide", "tile"), None), P(), P(), P(("slide", "tile")), P(None, "slide", "tile"))
    return jax.shard_map(
        per_device,
        mesh=mesh,
        in_specs=placed,
        out_specs=(P(("slide", "tile"), None), P("slide", "tile"), P("slide", "tile")),
        check_vma=False,
    )
```

```python
import functools

import jax
import jax.numpy as jnp
from jax import lax
from jax.experimental import pallas as pl
from jax.experimental.pallas import tpu as pltpu
from jax.sharding import PartitionSpec as P

HEAD_SIZE = 48
WIDTH = 3 * HEAD_SIZE
CHUNK_ROWS = 160
FLOATS = jnp.float32
HALFS = jnp.bfloat16
SCALE = HEAD_SIZE ** (-0.5)
VMEM = pltpu.CompilerParams(vmem_limit_bytes=56 * 1024 * 1024)


def iota(shape, dim):
    return lax.broadcasted_iota(jnp.int32, shape, dim)


def hot(cond):
    return jnp.where(cond, 1.0, 0.0).astype(HALFS)


def dot(a, b, dims="nn"):
    contract = (0 if dims[0] == "t" else 1, 1 if dims[1] == "t" else 0)
    return lax.dot_general(
        a, b, (((contract[0],), (contract[1],)), ((), ())), preferred_element_type=FLOATS
    )


def whole(memory=pltpu.VMEM):
    return pl.BlockSpec(memory_space=memory)


def call(body, outs, args, smem=(), anywhere=(), **kw):
    specs = [whole(pltpu.SMEM if i in smem else pltpu.VMEM) for i in range(len(args))]
    for i in anywhere:
        specs[i] = whole(pl.ANY)
    out_specs = jax.tree.map(lambda _: whole(), outs)
    return pl.pallas_call(
        body,
        out_shape=outs,
        in_specs=specs,
        out_specs=out_specs,
        compiler_params=VMEM,
        **kw,
    )(*args)


def shaped(shape, dtype=HALFS):
    return jax.ShapeDtypeStruct(shape, dtype)


def resident(shape, dtype=HALFS):
    return pltpu.VMEM(shape, dtype)


def stay(*values):
    return [pltpu.with_memory_space_constraint(value, pltpu.VMEM) for value in values]


def place(pos_ref):
    slots = pos_ref.shape[0]
    pos = pos_ref[...].reshape(1, slots)
    live = pos >= 0
    few = jnp.sum(jnp.where(live, 1, 0), axis=1, keepdims=True) <= 64
    pos = jnp.where(live, pos, 0)
    member = ((pos & 4095) >> 9 == iota((8, slots), 0)) & live
    upper = hot(iota((slots, slots), 0) < iota((slots, slots), 1))
    ranks = dot(hot(member), upper)
    rank = jnp.sum(jnp.where(member, ranks, 0.0), axis=0, keepdims=True).astype(jnp.int32)
    dest = ((pos & 4095) >> 9) * 128 + jnp.where(few, rank * 16, (rank & 15) * 8)
    dest = jnp.where(live, dest, -16)
    sub = jnp.where(few, 0, rank >> 4)
    mask = jnp.where(few, -9, -1)
    return pos, few, dest, sub, mask


def dispatch_body(pos_ref, tiles_ref, send_ref):
    slots = tiles_ref.shape[0]
    half = tiles_ref.shape[1] // 2
    pos, few, dest, sub, mask = place(pos_ref)
    base = dest + 2 * sub
    local = ((pos >> 12) << 9) + (pos & 511)
    lane = iota((128, slots), 0) - 4 * sub
    notes = jnp.where(
        lane == 0,
        (local >> 7) + 1,
        jnp.where(lane == 1, local & 127, jnp.where((lane == 2) & few, 1, 0)),
    )
    notes = notes.astype(FLOATS).astype(HALFS)
    step = 256
    for start in range(0, send_ref.shape[0], step):
        rows = (iota((step, slots), 0) + start) & mask
        out = dot(hot(rows == base), tiles_ref[:, :half])
        out = out + dot(hot(rows == base + 1), tiles_ref[:, half:])
        send_ref[start : start + step, :] = out.astype(HALFS)
        info = dot(hot(rows == dest + 6), notes, "nt")
        send_ref[start : start + step, :128] = (out[:, :128] + info).astype(HALFS)


def slots_body(pos_ref, base_ref):
    slots = pos_ref.shape[0]
    _, _, dest, sub, mask = place(pos_ref)
    same = iota((slots, slots), 0) == iota((slots, slots), 1)
    base = jnp.sum(jnp.where(same, dest + 2 * sub, 0), axis=1, keepdims=True)
    base_ref[...] = jnp.where(iota(base_ref.shape, 1) == 0, base, mask)


def project_body(
    odd_ref,
    recv_ref,
    embed_hbm_ref,
    weight_hbm_ref,
    emb_ref,
    tiles_ref,
    chunk_ref,
    pick0_ref,
    pick1_ref,
    embed_ref,
    weight_ref,
    embed_sem,
    weight_sem,
):
    embed_load = pltpu.make_async_copy(embed_hbm_ref, embed_ref, embed_sem)
    embed_load.start()
    weight_load = pltpu.make_async_copy(weight_hbm_ref, weight_ref, weight_sem)
    weight_load.start()
    total = recv_ref.shape[0]
    senders = total // 8
    sel = hot(iota((senders, total), 1) == 8 * iota((senders, total), 0) + 6)
    notes = dot(sel, recv_ref[:, :128])
    lane = iota((senders, 128), 1)
    lower = hot(iota((senders, senders), 0) > iota((senders, senders), 1))
    shared = (notes > 0.5) & (lane == 2)
    order = dot(lower, hot(shared)).astype(jnp.int32)
    other = shared & ((order & 1) != odd_ref[0])
    to_first = hot((iota((128, 128), 0) == 2) & (iota((128, 128), 1) == 0))
    other = dot(hot(other), to_first) > 0.5
    valid = (notes > 0.5) & ((lane & 3) == 0) & (lane < 12) & jnp.logical_not(other)
    cum = dot(lower, hot(valid))
    ones = jnp.where(valid, 1.0, 0.0)
    first = jnp.sum(jnp.where(lane == 0, ones, 0.0), axis=0, keepdims=True)
    first = jnp.sum(first, axis=1, keepdims=True)
    second = jnp.sum(jnp.where(lane == 4, ones, 0.0), axis=0, keepdims=True)
    second = jnp.sum(second, axis=1, keepdims=True)
    shift = jnp.where(lane >= 4, first, 0.0) + jnp.where(lane >= 8, second, 0.0)
    index = jnp.where(valid, cum + shift, -1.0)
    repeat = hot(iota((total, senders), 0) >> 3 == iota((total, senders), 1))
    index_all = dot(repeat, index.astype(HALFS))
    notes_all = dot(repeat, notes.astype(HALFS))
    turn = iota((total, 128), 0) & 7
    lanes = iota((total, 128), 1)
    mine = (lanes == 4 * (turn >> 1)) & (turn < 6)
    mine_low = (lanes == 4 * (turn >> 1) + 1) & (turn < 6)
    spot = jnp.sum(jnp.where(mine, index_all + 1.0, 0.0), axis=1, keepdims=True) - 1.0
    high = jnp.sum(jnp.where(mine, notes_all, 0.0), axis=1, keepdims=True)
    low = jnp.sum(jnp.where(mine_low, notes_all, 0.0), axis=1, keepdims=True)
    match = spot.astype(jnp.int32) == lanes
    pick0 = hot(match & ((turn & 1) == 0))
    pick1 = hot(match & ((turn & 1) == 1))
    pick0_ref[...] = pick0
    pick1_ref[...] = pick1
    half = recv_ref.shape[1]
    tiles_ref[:, :half] = dot(pick0, recv_ref[...], "tn").astype(HALFS)
    tiles_ref[:, half:] = dot(pick1, recv_ref[...], "tn").astype(HALFS)
    embed_load.wait()
    emb_ref[...] = dot(tiles_ref[...], embed_ref[...]).astype(HALFS)
    info = jnp.where(lanes == 0, high, jnp.where(lanes == 1, low, 0.0)).astype(HALFS)
    info = dot(info, pick0, "tn")[:16].astype(HALFS)
    weight_load.wait()
    heads = chunk_ref.shape[0] // CHUNK_ROWS
    for head in range(heads):
        top = head * CHUNK_ROWS
        if head % 8 == 0:
            wide = slice(head * WIDTH, (head + 8) * WIDTH)
            part = dot(emb_ref[...], weight_ref[:, wide]).T
        columns = slice((head % 8) * WIDTH, (head % 8 + 1) * WIDTH)
        chunk_ref[top : top + WIDTH, :] = part[columns].astype(HALFS)
        chunk_ref[top + WIDTH : top + CHUNK_ROWS, :] = info


def dilated_body(phase_ref, chunk_ref, query_ref, far_ref, rows_ref, local_ref):
    blocks = chunk_ref.shape[0] // CHUNK_ROWS
    total = jnp.zeros((WIDTH, query_ref.shape[1]), FLOATS)
    target = 8 * iota((query_ref.shape[1], 128), 0) + phase_ref[0]
    for block in range(blocks):
        top = block * CHUNK_ROWS
        lanes = slice(block * 128, (block + 1) * 128)
        part = chunk_ref[top : top + WIDTH, :]
        info = chunk_ref[top + WIDTH : top + CHUNK_ROWS, :].astype(FLOATS)
        local = ((info[0:1] - 1.0) * 128.0 + info[1:2]).astype(jnp.int32)
        rows_ref[:, lanes] = part
        local_ref[:, lanes] = jnp.broadcast_to(local, (8, 128))
        total = total + dot(part, hot(target == local), "nt")
    query_ref[...] = total[:HEAD_SIZE].astype(HALFS)
    for copy in range(far_ref.shape[0]):
        far_ref[copy] = total[HEAD_SIZE:].astype(HALFS)


def near_body(phase_ref, rows_ref, local_ref, grad_ref, place_ref, near_ref):
    seg = grad_ref.shape[2]
    local = local_ref[0:1, :]
    dilated = (iota((1, seg), 1) & 7) == phase_ref[0]
    for slide in range(grad_ref.shape[0]):
        spots = slice(slide * seg, (slide + 1) * seg)
        order = hot(local == iota((seg, local.shape[1]), 0) + slide * seg)
        parts = dot(rows_ref[...], order, "nt").astype(HALFS)
        place_ref[:, spots] = parts
        query = parts[:HEAD_SIZE]
        key = parts[HEAD_SIZE : 2 * HEAD_SIZE]
        value = parts[2 * HEAD_SIZE :]
        grad = grad_ref[slide]
        score = dot(key, query, "tn") * SCALE
        top = jnp.max(score, axis=0, keepdims=True)
        prob = jnp.exp(score - top)
        norm = 1.0 / jnp.sum(prob, axis=0, keepdims=True)
        prob = prob * jnp.where(dilated, 0.0, norm)
        dprob = dot(value, grad, "tn")
        delta = jnp.sum(prob * dprob, axis=0, keepdims=True)
        dscore = (prob * (dprob - delta)).astype(HALFS)
        near_ref[:HEAD_SIZE, spots] = dot(key, dscore) * SCALE
        near_ref[HEAD_SIZE : 2 * HEAD_SIZE, spots] = dot(query, dscore, "nt") * SCALE
        near_ref[2 * HEAD_SIZE :, spots] = dot(grad, prob.astype(HALFS), "nt")


def pick_body(phase_ref, grad_ref, out_ref):
    seg = grad_ref.shape[2]
    for pair in range(grad_ref.shape[0] // 2):
        grad = jnp.zeros((HEAD_SIZE, 128), FLOATS)
        for b in range(2):
            target = 8 * (iota((seg, 128), 1) - 64 * b) + phase_ref[0]
            grad = grad + dot(grad_ref[2 * pair + b], hot(iota((seg, 128), 0) == target))
        out_ref[:, pair * 128 : (pair + 1) * 128] = grad.astype(HALFS)


def far_body(query_ref, grad_ref, place_ref, far_ref, out_ref, dscore_ref, prob_ref):
    n = far_ref.shape[0]
    near = place_ref.shape[1] // 2
    seg = near // 2
    for pair in range(2):
        lanes = slice(pair * 128, (pair + 1) * 128)
        spots = slice(pair * near, (pair + 1) * near)
        query = query_ref[:, lanes]
        grad = grad_ref[:, lanes]
        key = jnp.concatenate(
            [place_ref[HEAD_SIZE : 2 * HEAD_SIZE, spots]]
            + [far_ref[k, :HEAD_SIZE, lanes] for k in range(n)],
            axis=1,
        )
        value = jnp.concatenate(
            [place_ref[2 * HEAD_SIZE :, spots]]
            + [far_ref[k, HEAD_SIZE:, lanes] for k in range(n)],
            axis=1,
        )
        size = key.shape[1]
        column = iota((128, size), 1)
        slide_of_key = jnp.where(column < near, column // seg, (column & 127) >> 6)
        same = slide_of_key == iota((128, size), 0) >> 6
        score = jnp.where(same, dot(query, key, "tn") * SCALE, -1e30)
        top = jnp.max(score, axis=1, keepdims=True)
        prob = jnp.exp(score - top)
        prob = prob * (1.0 / jnp.sum(prob, axis=1, keepdims=True))
        dprob = dot(grad, value, "tn")
        delta = jnp.sum(prob * dprob, axis=1, keepdims=True)
        dscore = (prob * (dprob - delta)).astype(HALFS)
        prob = prob.astype(HALFS)
        dkey = dot(query, dscore[:, near:]) * SCALE
        dvalue = dot(grad, prob[:, near:])
        for k in range(n):
            part = slice(k * 128, (k + 1) * 128)
            out_ref[k, :HEAD_SIZE, lanes] = dkey[:, part].astype(HALFS)
            out_ref[k, HEAD_SIZE:, lanes] = dvalue[:, part].astype(HALFS)
        dscore_ref[pair] = dscore
        prob_ref[pair] = prob[:, :near]


def sum_body(
    query_ref,
    grad_ref,
    place_ref,
    far_ref,
    dscore_ref,
    prob_ref,
    near_ref,
    dquery_ref,
    sum_ref,
):
    near = place_ref.shape[1] // 2
    sum_ref[:HEAD_SIZE, :] = near_ref[:HEAD_SIZE, :].astype(HALFS)
    for pair in range(2):
        lanes = slice(pair * 128, (pair + 1) * 128)
        spots = slice(pair * near, (pair + 1) * near)
        query = query_ref[:, lanes]
        grad = grad_ref[:, lanes]
        key = jnp.concatenate(
            [place_ref[HEAD_SIZE : 2 * HEAD_SIZE, spots]]
            + [far_ref[k, :HEAD_SIZE, lanes] for k in range(far_ref.shape[0])],
            axis=1,
        )
        dscore = dscore_ref[pair]
        dquery_ref[:, lanes] = (dot(key, dscore, "nt") * SCALE).astype(HALFS)
        dkey = dot(query, dscore[:, :near]) * SCALE
        dvalue = dot(grad, prob_ref[pair])
        middle = slice(HEAD_SIZE, 2 * HEAD_SIZE)
        sum_ref[middle, spots] = (near_ref[middle, spots] + dkey).astype(HALFS)
        last = slice(2 * HEAD_SIZE, WIDTH)
        sum_ref[last, spots] = (near_ref[last, spots] + dvalue).astype(HALFS)


def unplace_body(local_ref, sum_ref, out_ref):
    block = 512
    for start in range(0, out_ref.shape[1], block):
        lanes = slice(start, start + block)
        order = hot(local_ref[0:1, lanes] == iota((sum_ref.shape[1], block), 0))
        out_ref[:, lanes] = dot(sum_ref[...], order)


def finish_body(phase_ref, local_ref, main_ref, dquery_ref, far_ref, chunk_ref, rows_ref):
    far = far_ref[0].astype(FLOATS)
    for k in range(1, far_ref.shape[0]):
        far = far + far_ref[k].astype(FLOATS)
    sparse = jnp.concatenate([dquery_ref[...], far.astype(HALFS)], axis=0)
    local = local_ref[0:1, :]
    count = dquery_ref.shape[1]
    order = hot(local == 8 * iota((count, local.shape[1]), 0) + phase_ref[0])
    rows = (main_ref[...] + dot(sparse, order)).astype(HALFS)
    rows_ref[...] = rows
    for block in range(chunk_ref.shape[0] // WIDTH):
        chunk_ref[block * WIDTH : (block + 1) * WIDTH, :] = rows[
            :, block * 128 : (block + 1) * 128
        ]


def qkv_grad_body(core_ref, grad_ref, rows_ref, keep_ref, give_ref, all_ref):
    block = keep_ref.shape[1]
    part = dot(grad_ref[...], rows_ref[...]).T
    all_ref[...] = jnp.concatenate([part, jnp.zeros_like(part[:, : 256 - WIDTH])], axis=1)
    for chip in range(keep_ref.shape[0]):
        mine = pl.multiple_of((2 * chip + core_ref[0]) * block, block)
        other = pl.multiple_of((2 * chip + 1 - core_ref[0]) * block, block)
        keep_ref[chip] = all_ref[pl.ds(mine, block), :]
        give_ref[chip] = all_ref[pl.ds(other, block), :].astype(HALFS)


def merge_body(grad_ref, other_grad_ref, keep_ref, other_keep_ref, out_ref):
    rows, size = out_ref.shape[1] * 2 // 3, 128
    grad = jnp.concatenate([grad_ref[...], other_grad_ref[...]], axis=1)
    part = dot(grad, jnp.concatenate([keep_ref[...], other_keep_ref[...]], axis=0))
    part = part.astype(HALFS)
    columns = part.shape[0] // rows
    for block in range(out_ref.shape[0] // columns):
        left = block // 2 * 3 * size
        first = left if block % 2 == 0 else left + 2 * size
        other = left + size if block % 2 == 0 else left + size + 64
        for column in range(columns):
            here = part[column * rows : (column + 1) * rows]
            spot = block * columns + column
            out_ref[spot, :rows, :] = here[:, first : first + size]
            rest = here[:, other : other + 64]
            out_ref[spot, rows:, :] = jnp.concatenate(
                [rest[: rows // 2], rest[rows // 2 :]], axis=1
            )


def merge_qkv_body(chip_ref, keep_ref, given_ref, own_ref, *piece_refs):
    chips = keep_ref.shape[0]
    for k in range(chips):
        block = (chip_ref[0] + k) & (chips - 1)
        part = keep_ref[block] + given_ref[block].astype(FLOATS)
        if k == 0:
            own_ref[...] = part
        else:
            piece_refs[k - 1][...] = part.astype(HALFS)


def last_body(chip_ref, parts_ref, own_ref, *refs):
    piece_refs, embed_ref, qkv_ref = refs[:-2], refs[-2], refs[-1]
    total = parts_ref[0].astype(FLOATS)
    for k in range(1, parts_ref.shape[0]):
        total = total + parts_ref[k].astype(FLOATS)
    rest = jnp.concatenate([total[48:, :64], total[48:, 64:]], axis=0)
    even = jnp.concatenate([total[:48], rest], axis=1)
    odd = jnp.concatenate([rest, total[:48]], axis=1)
    embed_ref[...] = jnp.where((chip_ref[0] & 1) == 0, even, odd)
    qkv = own_ref[...]
    for ref in piece_refs:
        qkv = qkv + ref[...].astype(FLOATS)
    qkv_ref[...] = qkv.T[:WIDTH]


def load_body(_, hbm_ref, vmem_ref, sem):
    load = pltpu.make_async_copy(hbm_ref, vmem_ref, sem)
    load.start()
    load.wait()


def back_body(rows_ref, weight_ref, pick0_ref, pick1_ref, grad_ref, back_ref):
    half = back_ref.shape[1]
    grad = dot(weight_ref[...], rows_ref[...]).astype(HALFS)
    grad_ref[...] = grad
    back = dot(pick0_ref[...], grad[:half], "nt") + dot(pick1_ref[...], grad[half:], "nt")
    back_ref[...] = back.astype(HALFS)


def collect_body(recv_ref, base_ref, out_ref):
    total, half = recv_ref.shape
    base, mask = base_ref[:, 0:1], base_ref[:, 1:2]
    rows = iota((base.shape[0], total), 1) & mask
    out_ref[:, :half] = dot(hot(rows == base), recv_ref[...]).astype(HALFS)
    out_ref[:, half:] = dot(hot(rows == base + 1), recv_ref[...]).astype(HALFS)


def per_device(tile_features, embed_weight, qkv_weight, positions, out_grad):
    n_slide = lax.axis_size("slide")
    n_tile = lax.axis_size("tile")
    devices = n_slide * n_tile
    every = ("slide", "tile")
    slots = tile_features.shape[0]
    slides, seg = out_grad.shape[0], out_grad.shape[1]
    wide = embed_weight.shape[1]
    half = wide // 2
    rows = slides * seg
    share = rows // n_tile
    row_here = lax.axis_index("slide")
    col_here = lax.axis_index("tile")
    phase = (col_here % n_slide).astype(jnp.int32).reshape(1)
    odd = (col_here % 2).astype(jnp.int32).reshape(1)
    core = row_here % 2
    tiles = tile_features.shape[1]

    with jax.named_scope("dispatch"):
        sent = call(
            dispatch_body,
            resident((devices * 8, tiles // 2)),
            [positions, tile_features],
        )
        base = call(slots_body, resident((slots, 128), jnp.int32), [positions])
        arrived = lax.all_to_all(
            sent.reshape(devices, 8, tiles // 2), every, 0, 0, tiled=True
        ).reshape(devices * 8, tiles // 2)
    with jax.named_scope("project"):
        emb_rows, tile_rows, chunks, pick0, pick1 = call(
            project_body,
            [
                shaped((share, wide)),
                shaped((share, tiles)),
                resident((n_tile * CHUNK_ROWS, 128)),
                shaped((devices * 8, 128)),
                shaped((devices * 8, 128)),
            ],
            [odd, *stay(arrived), embed_weight, qkv_weight],
            smem=(0,),
            anywhere=(2, 3),
            scratch_shapes=[
                pltpu.VMEM(embed_weight.shape, HALFS),
                pltpu.VMEM(qkv_weight.shape, HALFS),
                pltpu.SemaphoreType.DMA,
                pltpu.SemaphoreType.DMA,
            ],
        )
        chunks = lax.all_to_all(
            chunks.reshape(n_tile, CHUNK_ROWS, 128), "tile", 0, 0, tiled=True
        ).reshape(n_tile * CHUNK_ROWS, 128)
    with jax.named_scope("swap_tiles"):
        swap = [(i, i ^ 1) for i in range(n_slide)]
        chips = n_slide // 2
        narrow = tiles // n_slide
        split = tile_rows.reshape(share, chips, 2, narrow)
        keep_cols = lax.dynamic_index_in_dim(split, core, 2, False).reshape(share, tiles // 2)
        give_cols = lax.dynamic_index_in_dim(split, 1 - core, 2, False).reshape(share, tiles // 2)
        got_cols = lax.ppermute(give_cols, "slide", swap)
    with jax.named_scope("dilated"):
        few = rows // n_slide
        query, far, head_rows, local = call(
            dilated_body,
            [
                resident((HEAD_SIZE, few)),
                resident((n_slide, 2 * HEAD_SIZE, few)),
                shaped((WIDTH, rows)),
                resident((8, rows), jnp.int32),
            ],
            [phase, *stay(chunks)],
            smem=(0,),
        )
        far = lax.all_to_all(far, "slide", 0, 0, tiled=True)
    with jax.named_scope("near"):
        grads = out_grad.transpose(0, 2, 1)
        dilated_grads = call(pick_body, resident((HEAD_SIZE, few)), [phase, grads], smem=(0,))
        placed, near = call(
            near_body,
            [resident((WIDTH, rows)), resident((WIDTH, rows), FLOATS)],
            [phase, head_rows, *stay(local), grads],
            smem=(0,),
            cost_estimate=pl.CostEstimate(
                flops=8_000_000_000, bytes_accessed=8_000_000, transcendentals=1 << 20
            ),
        )
    with jax.named_scope("far"):
        far_grads, dscores, probs = call(
            far_body,
            [
                resident((n_slide, 2 * HEAD_SIZE, few)),
                shaped((2, 128, rows)),
                shaped((2, 128, rows // 2)),
            ],
            stay(query, dilated_grads, placed, far),
        )
        far_grads = lax.all_to_all(far_grads, "slide", 0, 0, tiled=True)
    with jax.named_scope("unplace"):
        dquery, summed = call(
            sum_body,
            [resident((HEAD_SIZE, few)), resident((WIDTH, rows))],
            [*stay(query, dilated_grads, placed, far), dscores, probs, *stay(near)],
        )
        main = call(
            unplace_body,
            resident((WIDTH, rows), FLOATS),
            stay(local, summed),
            cost_estimate=pl.CostEstimate(
                flops=4_000_000_000, bytes_accessed=4_000_000, transcendentals=0
            ),
        )
        back_chunks, d_rows = call(
            finish_body,
            [resident((n_tile * WIDTH, 128)), shaped((WIDTH, rows))],
            [phase, *stay(local, main, dquery, far_grads)],
            smem=(0,),
        )
        back_rows = lax.all_to_all(
            back_chunks.reshape(n_tile, WIDTH, 128), "tile", 0, 0, tiled=True
        ).reshape(n_tile * WIDTH, 128)
    with jax.named_scope("qkv_grad"):
        all_rows = lax.all_gather(emb_rows, "tile", axis=0, tiled=True)
        block = wide // n_slide
        keep_qkv, give_qkv = call(
            qkv_grad_body,
            [shaped((chips, block, 256), FLOATS), shaped((chips, block, 256))],
            [core.astype(jnp.int32).reshape(1), d_rows, all_rows],
            smem=(0,),
            scratch_shapes=[pltpu.VMEM((wide, 256), FLOATS)],
        )
        chip = (row_here // 2).astype(jnp.int32).reshape(1)
        given_qkv = lax.ppermute(give_qkv, "slide", swap)
        own_qkv, *pieces = call(
            merge_qkv_body,
            [shaped((block, 256), FLOATS)] + [shaped((block, 256))] * (chips - 1),
            [chip, keep_qkv, given_qkv],
            smem=(0,),
        )
        pieces = [
            lax.ppermute(
                pieces[k - 1], "slide", [(i, (i + 2 * k) % n_slide) for i in range(n_slide)]
            )
            for k in range(1, chips)
        ]
    with jax.named_scope("tiles_grad"):
        loaded = call(
            load_body,
            resident(qkv_weight.shape),
            [d_rows, qkv_weight],
            anywhere=(0, 1),
            scratch_shapes=[pltpu.SemaphoreType.DMA],
        )
        grad_rows, back = call(
            back_body,
            [shaped((wide, share)), shaped((devices * 8, half))],
            [*stay(back_rows, loaded), pick0, pick1],
        )
        back = lax.all_to_all(
            back.reshape(devices, 8, half), every, 0, 0, tiled=True
        ).reshape(devices * 8, half)
        other_rows = lax.ppermute(grad_rows, "slide", swap)
        merged = call(
            merge_body,
            shaped((chips * n_tile, 72, 128)),
            [grad_rows, *stay(other_rows), keep_cols, got_cols],
        )
        merged, back = lax.optimization_barrier((merged, back))
    with jax.named_scope("collect"):
        d_embedded = call(collect_body, shaped((slots, wide)), stay(back, base))
    with jax.named_scope("embed_grad"):
        same_core = [
            [(2 * z + c) * n_tile + t for z in range(chips) for t in range(n_tile)]
            for c in range(2)
        ]
        parts = lax.all_to_all(
            merged, every, 0, 0, axis_index_groups=same_core, tiled=True
        )
        embed_grad, qkv_grad = call(
            last_body,
            [shaped((wide // n_tile, narrow), FLOATS), shaped((WIDTH, wide // n_slide), FLOATS)],
            [chip, *stay(parts), own_qkv, *pieces],
            smem=(0,),
        )
        embed_grad, qkv_grad = embed_grad.T, qkv_grad.T
    with jax.named_scope("feature_grad"):
        feature_grad = lax.dot_general(
            d_embedded, embed_weight, (((1,), (1,)), ((), ())), preferred_element_type=FLOATS
        ).astype(HALFS)
    return feature_grad, embed_grad, qkv_grad


def solution(mesh):
    placed = (P(("slide", "tile"), None), P(), P(), P(("slide", "tile")), P(None, "slide", "tile"))
    return jax.shard_map(
        per_device,
        mesh=mesh,
        in_specs=placed,
        out_specs=(P(("slide", "tile"), None), P("slide", "tile"), P("slide", "tile")),
        check_vma=False,
    )
```

```python
import functools

import jax
import jax.numpy as jnp
from jax import lax
from jax.experimental import pallas as pl
from jax.experimental.pallas import tpu as pltpu
from jax.sharding import PartitionSpec as P

HEAD_SIZE = 48
WIDTH = 3 * HEAD_SIZE
CHUNK_ROWS = 160
FLOATS = jnp.float32
HALFS = jnp.bfloat16
SCALE = HEAD_SIZE ** (-0.5)
VMEM = pltpu.CompilerParams(vmem_limit_bytes=56 * 1024 * 1024)


def iota(shape, dim):
    return lax.broadcasted_iota(jnp.int32, shape, dim)


def hot(cond):
    return jnp.where(cond, 1.0, 0.0).astype(HALFS)


def dot(a, b, dims="nn"):
    contract = (0 if dims[0] == "t" else 1, 1 if dims[1] == "t" else 0)
    return lax.dot_general(
        a, b, (((contract[0],), (contract[1],)), ((), ())), preferred_element_type=FLOATS
    )


def whole(memory=pltpu.VMEM):
    return pl.BlockSpec(memory_space=memory)


def call(body, outs, args, smem=(), anywhere=(), **kw):
    specs = [whole(pltpu.SMEM if i in smem else pltpu.VMEM) for i in range(len(args))]
    for i in anywhere:
        specs[i] = whole(pl.ANY)
    out_specs = jax.tree.map(lambda _: whole(), outs)
    return pl.pallas_call(
        body,
        out_shape=outs,
        in_specs=specs,
        out_specs=out_specs,
        compiler_params=VMEM,
        **kw,
    )(*args)


def shaped(shape, dtype=HALFS):
    return jax.ShapeDtypeStruct(shape, dtype)


def resident(shape, dtype=HALFS):
    return pltpu.VMEM(shape, dtype)


def stay(*values):
    return [pltpu.with_memory_space_constraint(value, pltpu.VMEM) for value in values]


def place(pos_ref):
    slots = pos_ref.shape[0]
    pos = pos_ref[...].reshape(1, slots)
    live = pos >= 0
    few = jnp.sum(jnp.where(live, 1, 0), axis=1, keepdims=True) <= 64
    pos = jnp.where(live, pos, 0)
    member = ((pos & 4095) >> 9 == iota((8, slots), 0)) & live
    upper = hot(iota((slots, slots), 0) < iota((slots, slots), 1))
    ranks = dot(hot(member), upper)
    rank = jnp.sum(jnp.where(member, ranks, 0.0), axis=0, keepdims=True).astype(jnp.int32)
    dest = ((pos & 4095) >> 9) * 128 + jnp.where(few, rank * 16, (rank & 15) * 8)
    dest = jnp.where(live, dest, -16)
    sub = jnp.where(few, 0, rank >> 4)
    mask = jnp.where(few, -9, -1)
    return pos, few, dest, sub, mask


def interleave(first, second):
    step, half = first.shape
    upper = (iota((step, half), 0) & 7) < 4
    even = jnp.where(upper, first, pltpu.roll(second, 4, 0))
    odd = jnp.where(upper, pltpu.roll(first, step - 4, 0), second)
    both = jnp.stack(
        [even.reshape(step // 8, 8, half), odd.reshape(step // 8, 8, half)], axis=1
    )
    return both.reshape(2 * step, half)


def dispatch_body(pos_ref, tiles_ref, send_ref):
    slots = tiles_ref.shape[0]
    half = send_ref.shape[1]
    rest = tiles_ref.shape[1] - 2 * half
    pos, few, dest, sub, mask = place(pos_ref)
    dest, mask = dest >> 1, jnp.where(few, -5, -1)
    local = ((pos >> 12) << 9) + (pos & 511)
    lane = iota((128, slots), 0) - 4 * sub
    notes = jnp.where(
        lane == 0,
        (local >> 7) + 1,
        jnp.where(lane == 1, local & 127, jnp.where((lane == 2) & few, 1, 0)),
    )
    notes = notes.astype(FLOATS).astype(HALFS)
    last = [jnp.where(sub == k, dest + 3, -16) for k in range(3)]
    step = 128
    for start in range(0, send_ref.shape[0] // 2, step):
        rows = (iota((step, slots), 0) + start) & mask
        whole_rows = hot(rows == dest + sub)
        tail = tiles_ref[:, 2 * half :]
        first = jnp.concatenate(
            [dot(hot(rows == last[k]), tail) for k in range(2)]
            + [dot(hot(rows == dest + 3), notes, "nt")],
            axis=1,
        )
        first = first + dot(whole_rows, tiles_ref[:, :half])
        second = dot(whole_rows, tiles_ref[:, half : 2 * half])
        second = jnp.concatenate(
            [second[:, :rest] + dot(hot(rows == last[2]), tail), second[:, rest:]], axis=1
        )
        both = interleave(first, second)
        send_ref[2 * start : 2 * (start + step), :] = both.astype(HALFS)


def slots_body(pos_ref, base_ref):
    slots = pos_ref.shape[0]
    _, _, dest, sub, mask = place(pos_ref)
    same = iota((slots, slots), 0) == iota((slots, slots), 1)
    base = jnp.sum(jnp.where(same, dest + sub, 0), axis=1, keepdims=True)
    base_ref[...] = jnp.where(iota(base_ref.shape, 1) == 0, base, mask)


def project_body(
    odd_ref,
    recv_ref,
    embed_hbm_ref,
    weight_hbm_ref,
    emb_ref,
    tiles_ref,
    chunk_ref,
    pick_ref,
    embed_ref,
    weight_ref,
    embed_sem,
    weight_sem,
):
    embed_load = pltpu.make_async_copy(embed_hbm_ref, embed_ref, embed_sem)
    embed_load.start()
    weight_load = pltpu.make_async_copy(weight_hbm_ref, weight_ref, weight_sem)
    weight_load.start()
    total = recv_ref.shape[0]
    senders = total // 8
    sel = hot(iota((senders, total), 1) == 8 * iota((senders, total), 0) + 3)
    half = recv_ref.shape[1]
    notes = dot(sel, recv_ref[:, half - 128 :])
    lane = iota((senders, 128), 1)
    lower = hot(iota((senders, senders), 0) > iota((senders, senders), 1))
    shared = (notes > 0.5) & (lane == 2)
    order = dot(lower, hot(shared)).astype(jnp.int32)
    other = shared & ((order & 1) != odd_ref[0])
    to_first = hot((iota((128, 128), 0) == 2) & (iota((128, 128), 1) == 0))
    other = dot(hot(other), to_first) > 0.5
    valid = (notes > 0.5) & ((lane & 3) == 0) & (lane < 12) & jnp.logical_not(other)
    cum = dot(lower, hot(valid))
    ones = jnp.where(valid, 1.0, 0.0)
    first = jnp.sum(jnp.where(lane == 0, ones, 0.0), axis=0, keepdims=True)
    first = jnp.sum(first, axis=1, keepdims=True)
    second = jnp.sum(jnp.where(lane == 4, ones, 0.0), axis=0, keepdims=True)
    second = jnp.sum(second, axis=1, keepdims=True)
    shift = jnp.where(lane >= 4, first, 0.0) + jnp.where(lane >= 8, second, 0.0)
    index = jnp.where(valid, cum + shift, -1.0)
    repeat = hot(iota((total, senders), 0) >> 3 == iota((total, senders), 1))
    index_all = dot(repeat, index.astype(HALFS))
    notes_all = dot(repeat, notes.astype(HALFS))
    turn = iota((total, 128), 0) & 7
    lanes = iota((total, 128), 1)
    slot = turn & 3
    here = 4 * jnp.where(slot < 3, slot, jnp.where(turn == 3, 0, 2))
    mine = lanes == here
    mine_low = lanes == here + 1
    spot = jnp.sum(jnp.where(mine, index_all + 1.0, 0.0), axis=1, keepdims=True) - 1.0
    middle = jnp.where((lanes == 4) & (turn == 3), index_all + 1.0, 0.0)
    middle = jnp.sum(middle, axis=1, keepdims=True) - 1.0
    high = jnp.sum(jnp.where(mine, notes_all, 0.0), axis=1, keepdims=True)
    low = jnp.sum(jnp.where(mine_low, notes_all, 0.0), axis=1, keepdims=True)
    match = spot.astype(jnp.int32) == lanes
    pick0 = hot(match & (turn < 3))
    pick1 = hot(match & (turn > 3) & (turn < 7))
    pick_rest = hot(match & (slot == 3))
    pick_middle = hot(middle.astype(jnp.int32) == lanes)
    slots_only = jnp.where(match & (slot < 3), 1.0, 0.0).reshape(senders // 2, 2, 8, 128)
    upper = iota((senders // 2, 8, 128), 1) < 4
    slots_only = jnp.where(upper, slots_only[:, 0], pltpu.roll(slots_only[:, 1], 4, 1))
    pick_ref[...] = slots_only.reshape(total // 2, 128).astype(HALFS)
    tiles_ref[:, :half] = dot(pick0, recv_ref[...], "tn").astype(HALFS)
    tiles_ref[:, half : 2 * half] = dot(pick1, recv_ref[...], "tn").astype(HALFS)
    rest = tiles_ref.shape[1] - 2 * half
    tail = dot(pick_rest, recv_ref[:, :rest], "tn")
    tail = tail + dot(pick_middle, recv_ref[:, rest : 2 * rest], "tn")
    tiles_ref[:, 2 * half :] = tail.astype(HALFS)
    embed_load.wait()
    emb_ref[...] = dot(tiles_ref[...], embed_ref[...]).astype(HALFS)
    info = jnp.where(lanes == 0, high, jnp.where(lanes == 1, low, 0.0)).astype(HALFS)
    info = dot(info, pick0, "tn")[:16].astype(HALFS)
    weight_load.wait()
    heads = chunk_ref.shape[0] // CHUNK_ROWS
    for head in range(heads):
        top = head * CHUNK_ROWS
        if head % 8 == 0:
            wide = slice(head * WIDTH, (head + 8) * WIDTH)
            part = dot(emb_ref[...], weight_ref[:, wide]).T
        columns = slice((head % 8) * WIDTH, (head % 8 + 1) * WIDTH)
        chunk_ref[top : top + WIDTH, :] = part[columns].astype(HALFS)
        chunk_ref[top + WIDTH : top + CHUNK_ROWS, :] = info


def dilated_body(phase_ref, chunk_ref, query_ref, far_ref, rows_ref, local_ref):
    blocks = chunk_ref.shape[0] // CHUNK_ROWS
    total = jnp.zeros((WIDTH, query_ref.shape[1]), FLOATS)
    target = 8 * iota((query_ref.shape[1], 128), 0) + phase_ref[0]
    for block in range(blocks):
        top = block * CHUNK_ROWS
        lanes = slice(block * 128, (block + 1) * 128)
        part = chunk_ref[top : top + WIDTH, :]
        info = chunk_ref[top + WIDTH : top + CHUNK_ROWS, :].astype(FLOATS)
        local = ((info[0:1] - 1.0) * 128.0 + info[1:2]).astype(jnp.int32)
        rows_ref[:, lanes] = part
        local_ref[:, lanes] = jnp.broadcast_to(local, (8, 128))
        total = total + dot(part, hot(target == local), "nt")
    query_ref[...] = total[:HEAD_SIZE].astype(HALFS)
    for copy in range(far_ref.shape[0]):
        far_ref[copy] = total[HEAD_SIZE:].astype(HALFS)


def near_body(phase_ref, rows_ref, local_ref, grad_ref, place_ref, near_ref):
    seg = grad_ref.shape[2]
    local = local_ref[0:1, :]
    dilated = (iota((1, seg), 1) & 7) == phase_ref[0]
    for slide in range(grad_ref.shape[0]):
        spots = slice(slide * seg, (slide + 1) * seg)
        order = hot(local == iota((seg, local.shape[1]), 0) + slide * seg)
        parts = dot(rows_ref[...], order, "nt").astype(HALFS)
        place_ref[:, spots] = parts
        query = parts[:HEAD_SIZE]
        key = parts[HEAD_SIZE : 2 * HEAD_SIZE]
        value = parts[2 * HEAD_SIZE :]
        grad = grad_ref[slide]
        score = dot(key, query, "tn") * SCALE
        top = jnp.max(score, axis=0, keepdims=True)
        prob = jnp.exp(score - top)
        norm = 1.0 / jnp.sum(prob, axis=0, keepdims=True)
        prob = prob * jnp.where(dilated, 0.0, norm)
        dprob = dot(value, grad, "tn")
        delta = jnp.sum(prob * dprob, axis=0, keepdims=True)
        dscore = (prob * (dprob - delta)).astype(HALFS)
        near_ref[:HEAD_SIZE, spots] = dot(key, dscore) * SCALE
        near_ref[HEAD_SIZE : 2 * HEAD_SIZE, spots] = dot(query, dscore, "nt") * SCALE
        near_ref[2 * HEAD_SIZE :, spots] = dot(grad, prob.astype(HALFS), "nt")


def pick_body(phase_ref, grad_ref, out_ref):
    seg = grad_ref.shape[2]
    for pair in range(grad_ref.shape[0] // 2):
        grad = jnp.zeros((HEAD_SIZE, 128), FLOATS)
        for b in range(2):
            target = 8 * (iota((seg, 128), 1) - 64 * b) + phase_ref[0]
            grad = grad + dot(grad_ref[2 * pair + b], hot(iota((seg, 128), 0) == target))
        out_ref[:, pair * 128 : (pair + 1) * 128] = grad.astype(HALFS)


def far_body(query_ref, grad_ref, place_ref, far_ref, out_ref, dscore_ref, prob_ref):
    n = far_ref.shape[0]
    near = place_ref.shape[1] // 2
    seg = near // 2
    for pair in range(2):
        lanes = slice(pair * 128, (pair + 1) * 128)
        spots = slice(pair * near, (pair + 1) * near)
        query = query_ref[:, lanes]
        grad = grad_ref[:, lanes]
        key = jnp.concatenate(
            [place_ref[HEAD_SIZE : 2 * HEAD_SIZE, spots]]
            + [far_ref[k, :HEAD_SIZE, lanes] for k in range(n)],
            axis=1,
        )
        value = jnp.concatenate(
            [place_ref[2 * HEAD_SIZE :, spots]]
            + [far_ref[k, HEAD_SIZE:, lanes] for k in range(n)],
            axis=1,
        )
        size = key.shape[1]
        column = iota((128, size), 1)
        slide_of_key = jnp.where(column < near, column // seg, (column & 127) >> 6)
        same = slide_of_key == iota((128, size), 0) >> 6
        score = jnp.where(same, dot(query, key, "tn") * SCALE, -1e30)
        top = jnp.max(score, axis=1, keepdims=True)
        prob = jnp.exp(score - top)
        prob = prob * (1.0 / jnp.sum(prob, axis=1, keepdims=True))
        dprob = dot(grad, value, "tn")
        delta = jnp.sum(prob * dprob, axis=1, keepdims=True)
        dscore = (prob * (dprob - delta)).astype(HALFS)
        prob = prob.astype(HALFS)
        dkey = dot(query, dscore[:, near:]) * SCALE
        dvalue = dot(grad, prob[:, near:])
        for k in range(n):
            part = slice(k * 128, (k + 1) * 128)
            out_ref[k, :HEAD_SIZE, lanes] = dkey[:, part].astype(HALFS)
            out_ref[k, HEAD_SIZE:, lanes] = dvalue[:, part].astype(HALFS)
        dscore_ref[pair] = dscore
        prob_ref[pair] = prob[:, :near]


def sum_body(
    query_ref,
    grad_ref,
    place_ref,
    far_ref,
    dscore_ref,
    prob_ref,
    near_ref,
    dquery_ref,
    sum_ref,
):
    near = place_ref.shape[1] // 2
    sum_ref[:HEAD_SIZE, :] = near_ref[:HEAD_SIZE, :].astype(HALFS)
    for pair in range(2):
        lanes = slice(pair * 128, (pair + 1) * 128)
        spots = slice(pair * near, (pair + 1) * near)
        query = query_ref[:, lanes]
        grad = grad_ref[:, lanes]
        key = jnp.concatenate(
            [place_ref[HEAD_SIZE : 2 * HEAD_SIZE, spots]]
            + [far_ref[k, :HEAD_SIZE, lanes] for k in range(far_ref.shape[0])],
            axis=1,
        )
        dscore = dscore_ref[pair]
        dquery_ref[:, lanes] = (dot(key, dscore, "nt") * SCALE).astype(HALFS)
        dkey = dot(query, dscore[:, :near]) * SCALE
        dvalue = dot(grad, prob_ref[pair])
        middle = slice(HEAD_SIZE, 2 * HEAD_SIZE)
        sum_ref[middle, spots] = (near_ref[middle, spots] + dkey).astype(HALFS)
        last = slice(2 * HEAD_SIZE, WIDTH)
        sum_ref[last, spots] = (near_ref[last, spots] + dvalue).astype(HALFS)


def unplace_body(local_ref, sum_ref, out_ref):
    block = 512
    for start in range(0, out_ref.shape[1], block):
        lanes = slice(start, start + block)
        order = hot(local_ref[0:1, lanes] == iota((sum_ref.shape[1], block), 0))
        out_ref[:, lanes] = dot(sum_ref[...], order)


def finish_body(phase_ref, local_ref, main_ref, dquery_ref, far_ref, chunk_ref, rows_ref):
    far = far_ref[0].astype(FLOATS)
    for k in range(1, far_ref.shape[0]):
        far = far + far_ref[k].astype(FLOATS)
    sparse = jnp.concatenate([dquery_ref[...], far.astype(HALFS)], axis=0)
    local = local_ref[0:1, :]
    count = dquery_ref.shape[1]
    order = hot(local == 8 * iota((count, local.shape[1]), 0) + phase_ref[0])
    rows = (main_ref[...] + dot(sparse, order)).astype(HALFS)
    rows_ref[...] = rows
    for block in range(chunk_ref.shape[0] // WIDTH):
        chunk_ref[block * WIDTH : (block + 1) * WIDTH, :] = rows[
            :, block * 128 : (block + 1) * 128
        ]


def qkv_grad_body(core_ref, grad_ref, rows_ref, keep_ref, give_ref, all_ref):
    block = keep_ref.shape[1]
    part = dot(grad_ref[...], rows_ref[...]).T
    all_ref[...] = jnp.concatenate([part, jnp.zeros_like(part[:, : 256 - WIDTH])], axis=1)
    for chip in range(keep_ref.shape[0]):
        mine = pl.multiple_of((2 * chip + core_ref[0]) * block, block)
        other = pl.multiple_of((2 * chip + 1 - core_ref[0]) * block, block)
        keep_ref[chip] = all_ref[pl.ds(mine, block), :]
        give_ref[chip] = all_ref[pl.ds(other, block), :].astype(HALFS)


def merge_body(grad_ref, other_grad_ref, keep_ref, other_keep_ref, out_ref):
    rows, size = out_ref.shape[1] * 2 // 3, 128
    grad = jnp.concatenate([grad_ref[...], other_grad_ref[...]], axis=1)
    part = dot(grad, jnp.concatenate([keep_ref[...], other_keep_ref[...]], axis=0))
    part = part.astype(HALFS)
    columns = part.shape[0] // rows
    for block in range(out_ref.shape[0] // columns):
        left = block // 2 * 3 * size
        first = left if block % 2 == 0 else left + 2 * size
        other = left + size if block % 2 == 0 else left + size + 64
        for column in range(columns):
            here = part[column * rows : (column + 1) * rows]
            spot = block * columns + column
            out_ref[spot, :rows, :] = here[:, first : first + size]
            rest = here[:, other : other + 64]
            out_ref[spot, rows:, :] = jnp.concatenate(
                [rest[: rows // 2], rest[rows // 2 :]], axis=1
            )


def merge_qkv_body(chip_ref, keep_ref, given_ref, own_ref, *piece_refs):
    chips = keep_ref.shape[0]
    for k in range(chips):
        block = (chip_ref[0] + k) & (chips - 1)
        part = keep_ref[block] + given_ref[block].astype(FLOATS)
        if k == 0:
            own_ref[...] = part
        else:
            piece_refs[k - 1][...] = part.astype(HALFS)


def last_body(chip_ref, parts_ref, own_ref, *refs):
    piece_refs, embed_ref, qkv_ref = refs[:-2], refs[-2], refs[-1]
    total = parts_ref[0].astype(FLOATS)
    for k in range(1, parts_ref.shape[0]):
        total = total + parts_ref[k].astype(FLOATS)
    rest = jnp.concatenate([total[48:, :64], total[48:, 64:]], axis=0)
    even = jnp.concatenate([total[:48], rest], axis=1)
    odd = jnp.concatenate([rest, total[:48]], axis=1)
    embed_ref[...] = jnp.where((chip_ref[0] & 1) == 0, even, odd)
    qkv = own_ref[...]
    for ref in piece_refs:
        qkv = qkv + ref[...].astype(FLOATS)
    qkv_ref[...] = qkv.T[:WIDTH]


def load_body(_, *refs):
    count, sems = len(refs) // 2, refs[-1]
    loads = [
        pltpu.make_async_copy(refs[k], refs[count + k], sems.at[k]) for k in range(count)
    ]
    for load in loads:
        load.start()
    for load in loads:
        load.wait()


def load(after, *values):
    return call(
        load_body,
        [resident(value.shape) for value in values],
        [after, *values],
        anywhere=range(len(values) + 1),
        scratch_shapes=[pltpu.SemaphoreType.DMA((len(values),))],
    )


def back_body(rows_ref, weight_ref, pick_ref, grad_ref, back_ref):
    half = back_ref.shape[1]
    grad = dot(weight_ref[...], rows_ref[...]).astype(HALFS)
    grad_ref[...] = grad
    step = 128
    for start in range(0, pick_ref.shape[0], step):
        pick = pick_ref[start : start + step, :]
        both = interleave(dot(pick, grad[:half], "nt"), dot(pick, grad[half:], "nt"))
        back_ref[2 * start : 2 * (start + step), :] = both.astype(HALFS)


def collect_body(recv_ref, base_ref, out_ref):
    total, half = recv_ref.shape
    base, mask = base_ref[:, 0:1], base_ref[:, 1:2]
    rows = iota((base.shape[0], total), 1) & mask
    out_ref[:, :half] = dot(hot(rows == base), recv_ref[...]).astype(HALFS)
    out_ref[:, half:] = dot(hot(rows == base + 4), recv_ref[...]).astype(HALFS)


def per_device(tile_features, embed_weight, qkv_weight, positions, out_grad):
    n_slide = lax.axis_size("slide")
    n_tile = lax.axis_size("tile")
    devices = n_slide * n_tile
    every = ("slide", "tile")
    slots = tile_features.shape[0]
    slides, seg = out_grad.shape[0], out_grad.shape[1]
    wide = embed_weight.shape[1]
    half = wide // 2
    rows = slides * seg
    share = rows // n_tile
    row_here = lax.axis_index("slide")
    col_here = lax.axis_index("tile")
    phase = (col_here % n_slide).astype(jnp.int32).reshape(1)
    odd = (col_here % 2).astype(jnp.int32).reshape(1)
    core = row_here % 2
    tiles = tile_features.shape[1]
    packed = (tiles - 256) // 2

    with jax.named_scope("dispatch"):
        sent = call(
            dispatch_body,
            resident((devices * 8, packed)),
            [positions, tile_features],
        )
        base = call(slots_body, resident((slots, 128), jnp.int32), [positions])
        arrived = lax.all_to_all(
            sent.reshape(devices, 8, packed), every, 0, 0, tiled=True
        ).reshape(devices * 8, packed)
    with jax.named_scope("project"):
        emb_rows, tile_rows, chunks, pick = call(
            project_body,
            [
                shaped((share, wide)),
                shaped((share, tiles)),
                resident((n_tile * CHUNK_ROWS, 128)),
                shaped((devices * 4, 128)),
            ],
            [odd, *stay(arrived), embed_weight, qkv_weight],
            smem=(0,),
            anywhere=(2, 3),
            scratch_shapes=[
                pltpu.VMEM(embed_weight.shape, HALFS),
                pltpu.VMEM(qkv_weight.shape, HALFS),
                pltpu.SemaphoreType.DMA,
                pltpu.SemaphoreType.DMA,
            ],
        )
        chunks = lax.all_to_all(
            chunks.reshape(n_tile, CHUNK_ROWS, 128), "tile", 0, 0, tiled=True
        ).reshape(n_tile * CHUNK_ROWS, 128)
    with jax.named_scope("swap_tiles"):
        swap = [(i, i ^ 1) for i in range(n_slide)]
        chips = n_slide // 2
        narrow = tiles // n_slide
        split = tile_rows.reshape(share, chips, 2, narrow)
        keep_cols = lax.dynamic_index_in_dim(split, core, 2, False).reshape(share, tiles // 2)
        give_cols = lax.dynamic_index_in_dim(split, 1 - core, 2, False).reshape(share, tiles // 2)
        got_cols = lax.ppermute(give_cols, "slide", swap)
    with jax.named_scope("dilated"):
        few = rows // n_slide
        query, far, head_rows, local = call(
            dilated_body,
            [
                resident((HEAD_SIZE, few)),
                resident((n_slide, 2 * HEAD_SIZE, few)),
                shaped((WIDTH, rows)),
                resident((8, rows), jnp.int32),
            ],
            [phase, *stay(chunks)],
            smem=(0,),
        )
        far = lax.all_to_all(far, "slide", 0, 0, tiled=True)
    with jax.named_scope("near"):
        grads = out_grad.transpose(0, 2, 1)
        dilated_grads = call(pick_body, resident((HEAD_SIZE, few)), [phase, grads], smem=(0,))
        placed, near = call(
            near_body,
            [resident((WIDTH, rows)), resident((WIDTH, rows), FLOATS)],
            [phase, head_rows, *stay(local), grads],
            smem=(0,),
            cost_estimate=pl.CostEstimate(
                flops=8_000_000_000, bytes_accessed=8_000_000, transcendentals=1 << 20
            ),
        )
    with jax.named_scope("far"):
        far_grads, dscores, probs = call(
            far_body,
            [
                resident((n_slide, 2 * HEAD_SIZE, few)),
                shaped((2, 128, rows)),
                shaped((2, 128, rows // 2)),
            ],
            stay(query, dilated_grads, placed, far),
        )
        far_grads = lax.all_to_all(far_grads, "slide", 0, 0, tiled=True)
    with jax.named_scope("unplace"):
        dquery, summed = call(
            sum_body,
            [resident((HEAD_SIZE, few)), resident((WIDTH, rows))],
            [*stay(query, dilated_grads, placed, far), dscores, probs, *stay(near)],
        )
        main = call(
            unplace_body,
            resident((WIDTH, rows), FLOATS),
            stay(local, summed),
            cost_estimate=pl.CostEstimate(
                flops=4_000_000_000, bytes_accessed=4_000_000, transcendentals=0
            ),
        )
        back_chunks, d_rows = call(
            finish_body,
            [resident((n_tile * WIDTH, 128)), shaped((WIDTH, rows))],
            [phase, *stay(local, main, dquery, far_grads)],
            smem=(0,),
        )
        back_rows = lax.all_to_all(
            back_chunks.reshape(n_tile, WIDTH, 128), "tile", 0, 0, tiled=True
        ).reshape(n_tile * WIDTH, 128)
    with jax.named_scope("qkv_grad"):
        all_rows = lax.all_gather(emb_rows, "tile", axis=0, tiled=True)
        block = wide // n_slide
        keep_qkv, give_qkv = call(
            qkv_grad_body,
            [shaped((chips, block, 256), FLOATS), shaped((chips, block, 256))],
            [core.astype(jnp.int32).reshape(1), d_rows, all_rows],
            smem=(0,),
            scratch_shapes=[pltpu.VMEM((wide, 256), FLOATS)],
        )
        chip = (row_here // 2).astype(jnp.int32).reshape(1)
        given_qkv = lax.ppermute(give_qkv, "slide", swap)
        own_qkv, *pieces = call(
            merge_qkv_body,
            [shaped((block, 256), FLOATS)] + [shaped((block, 256))] * (chips - 1),
            [chip, keep_qkv, given_qkv],
            smem=(0,),
        )
        pieces = [
            lax.ppermute(
                pieces[k - 1], "slide", [(i, (i + 2 * k) % n_slide) for i in range(n_slide)]
            )
            for k in range(1, chips)
        ]
    with jax.named_scope("tiles_grad"):
        (weight_here,) = load(d_rows, qkv_weight)
        grad_rows, back = call(
            back_body,
            [shaped((wide, share)), shaped((devices * 8, half))],
            [*stay(back_rows, weight_here), pick],
        )
        back = lax.all_to_all(
            back.reshape(devices, 8, half), every, 0, 0, tiled=True
        ).reshape(devices * 8, half)
        other_rows = lax.ppermute(grad_rows, "slide", swap)
        merged = call(
            merge_body,
            shaped((chips * n_tile, 72, 128)),
            [grad_rows, *stay(other_rows), keep_cols, got_cols],
        )
        merged, back = lax.optimization_barrier((merged, back))
    with jax.named_scope("collect"):
        d_embedded = call(collect_body, shaped((slots, wide)), stay(back, base))
    with jax.named_scope("embed_grad"):
        same_core = [
            [(2 * z + c) * n_tile + t for z in range(chips) for t in range(n_tile)]
            for c in range(2)
        ]
        parts = lax.all_to_all(
            merged, every, 0, 0, axis_index_groups=same_core, tiled=True
        )
        embed_grad, qkv_grad = call(
            last_body,
            [shaped((wide // n_tile, narrow), FLOATS), shaped((WIDTH, wide // n_slide), FLOATS)],
            [chip, *stay(parts), own_qkv, *pieces],
            smem=(0,),
        )
        embed_grad, qkv_grad = embed_grad.T, qkv_grad.T
    with jax.named_scope("feature_grad"):
        feature_grad = lax.dot_general(
            d_embedded, embed_weight, (((1,), (1,)), ((), ())), preferred_element_type=FLOATS
        ).astype(HALFS)
    return feature_grad, embed_grad, qkv_grad


def solution(mesh):
    placed = (P(("slide", "tile"), None), P(), P(), P(("slide", "tile")), P(None, "slide", "tile"))
    return jax.shard_map(
        per_device,
        mesh=mesh,
        in_specs=placed,
        out_specs=(P(("slide", "tile"), None), P("slide", "tile"), P("slide", "tile")),
        check_vma=False,
    )
```

```python
import functools

import jax
import jax.numpy as jnp
from jax import lax
from jax.experimental import pallas as pl
from jax.experimental.pallas import tpu as pltpu
from jax.sharding import PartitionSpec as P

HEAD_SIZE = 48
WIDTH = 3 * HEAD_SIZE
CHUNK_ROWS = 152
FLOATS = jnp.float32
HALFS = jnp.bfloat16
SCALE = HEAD_SIZE ** (-0.5)
VMEM = pltpu.CompilerParams(vmem_limit_bytes=56 * 1024 * 1024)


def iota(shape, dim):
    return lax.broadcasted_iota(jnp.int32, shape, dim)


def hot(cond):
    return jnp.where(cond, 1.0, 0.0).astype(HALFS)


def dot(a, b, dims="nn"):
    contract = (0 if dims[0] == "t" else 1, 1 if dims[1] == "t" else 0)
    return lax.dot_general(
        a, b, (((contract[0],), (contract[1],)), ((), ())), preferred_element_type=FLOATS
    )


def whole(memory=pltpu.VMEM):
    return pl.BlockSpec(memory_space=memory)


def call(body, outs, args, smem=(), anywhere=(), blocks=None, **kw):
    specs = [whole(pltpu.SMEM if i in smem else pltpu.VMEM) for i in range(len(args))]
    for i in anywhere:
        specs[i] = whole(pl.ANY)
    for i, block in (blocks or {}).items():
        specs[i] = block
    out_specs = jax.tree.map(lambda _: whole(), outs)
    return pl.pallas_call(
        body,
        out_shape=outs,
        in_specs=specs,
        out_specs=out_specs,
        compiler_params=VMEM,
        **kw,
    )(*args)


def shaped(shape, dtype=HALFS):
    return jax.ShapeDtypeStruct(shape, dtype)


def resident(shape, dtype=HALFS):
    return pltpu.VMEM(shape, dtype)


def stay(*values):
    return [pltpu.with_memory_space_constraint(value, pltpu.VMEM) for value in values]


def place(pos_ref):
    slots = pos_ref.shape[0]
    pos = pos_ref[...].reshape(1, slots)
    live = pos >= 0
    few = jnp.sum(jnp.where(live, 1, 0), axis=1, keepdims=True) <= 64
    pos = jnp.where(live, pos, 0)
    member = ((pos & 4095) >> 9 == iota((8, slots), 0)) & live
    upper = hot(iota((slots, slots), 0) < iota((slots, slots), 1))
    ranks = dot(hot(member), upper)
    rank = jnp.sum(jnp.where(member, ranks, 0.0), axis=0, keepdims=True).astype(jnp.int32)
    dest = ((pos & 4095) >> 9) * 128 + jnp.where(few, rank * 16, (rank & 15) * 8)
    dest = jnp.where(live, dest, -16)
    sub = jnp.where(few, 0, rank >> 4)
    mask = jnp.where(few, -9, -1)
    return pos, few, dest, sub, mask


def interleave(first, second):
    step, half = first.shape
    upper = (iota((step, half), 0) & 7) < 4
    even = jnp.where(upper, first, pltpu.roll(second, 4, 0))
    odd = jnp.where(upper, pltpu.roll(first, step - 4, 0), second)
    both = jnp.stack(
        [even.reshape(step // 8, 8, half), odd.reshape(step // 8, 8, half)], axis=1
    )
    return both.reshape(2 * step, half)


def dispatch_body(pos_ref, left_ref, right_ref, rest_ref, send_ref):
    slots, half = left_ref.shape
    rest = rest_ref.shape[1]
    pos, few, dest, sub, mask = place(pos_ref)
    dest, mask = dest >> 1, jnp.where(few, -5, -1)
    local = ((pos >> 12) << 9) + (pos & 511)
    lane = iota((128, slots), 0) - 4 * sub
    notes = jnp.where(
        lane == 0,
        (local >> 7) + 1,
        jnp.where(lane == 1, local & 127, jnp.where((lane == 2) & few, 1, 0)),
    )
    notes = notes.astype(FLOATS).astype(HALFS)
    last = [jnp.where(sub == k, dest + 3, -16) for k in range(3)]
    step = 128
    for start in range(0, send_ref.shape[0] // 2, step):
        rows = (iota((step, slots), 0) + start) & mask
        whole_rows = hot(rows == dest + sub)
        tail = rest_ref[...]
        first = jnp.concatenate(
            [dot(hot(rows == last[k]), tail) for k in range(2)]
            + [dot(hot(rows == dest + 3), notes, "nt")],
            axis=1,
        )
        first = first + dot(whole_rows, left_ref[...])
        second = dot(whole_rows, right_ref[...])
        second = jnp.concatenate(
            [second[:, :rest] + dot(hot(rows == last[2]), tail), second[:, rest:]], axis=1
        )
        both = interleave(first, second)
        send_ref[2 * start : 2 * (start + step), :] = both.astype(HALFS)


def slots_body(pos_ref, base_ref):
    slots = pos_ref.shape[0]
    _, _, dest, sub, mask = place(pos_ref)
    same = iota((slots, slots), 0) == iota((slots, slots), 1)
    base = jnp.sum(jnp.where(same, dest + sub, 0), axis=1, keepdims=True)
    base_ref[...] = jnp.where(iota(base_ref.shape, 1) == 0, base, mask)


def project_body(
    odd_ref,
    recv_ref,
    embed_hbm_ref,
    weight_hbm_ref,
    emb_ref,
    tiles_ref,
    chunk_ref,
    pick_ref,
    embed_ref,
    weight_ref,
    embed_sem,
    weight_sem,
):
    embed_load = pltpu.make_async_copy(embed_hbm_ref, embed_ref, embed_sem)
    embed_load.start()
    columns = weight_ref.shape[2]
    weight_loads = [
        pltpu.make_async_copy(
            weight_hbm_ref.at[:, k * columns : (k + 1) * columns], weight_ref.at[k], weight_sem.at[k]
        )
        for k in range(2)
    ]
    for one in weight_loads:
        one.start()
    total = recv_ref.shape[0]
    senders = total // 8
    sel = hot(iota((senders, total), 1) == 8 * iota((senders, total), 0) + 3)
    half = recv_ref.shape[1]
    notes = dot(sel, recv_ref[:, half - 128 :])
    lane = iota((senders, 128), 1)
    lower = hot(iota((senders, senders), 0) > iota((senders, senders), 1))
    shared = (notes > 0.5) & (lane == 2)
    order = dot(lower, hot(shared)).astype(jnp.int32)
    other = shared & ((order & 1) != odd_ref[0])
    to_first = hot((iota((128, 128), 0) == 2) & (iota((128, 128), 1) == 0))
    other = dot(hot(other), to_first) > 0.5
    valid = (notes > 0.5) & ((lane & 3) == 0) & (lane < 12) & jnp.logical_not(other)
    cum = dot(lower, hot(valid))
    ones = jnp.where(valid, 1.0, 0.0)
    first = jnp.sum(jnp.where(lane == 0, ones, 0.0), axis=0, keepdims=True)
    first = jnp.sum(first, axis=1, keepdims=True)
    second = jnp.sum(jnp.where(lane == 4, ones, 0.0), axis=0, keepdims=True)
    second = jnp.sum(second, axis=1, keepdims=True)
    shift = jnp.where(lane >= 4, first, 0.0) + jnp.where(lane >= 8, second, 0.0)
    index = jnp.where(valid, cum + shift, -1.0)
    repeat = hot(iota((total, senders), 0) >> 3 == iota((total, senders), 1))
    index_all = dot(repeat, index.astype(HALFS))
    notes_all = dot(repeat, notes.astype(HALFS))
    turn = iota((total, 128), 0) & 7
    lanes = iota((total, 128), 1)
    slot = turn & 3
    here = 4 * jnp.where(slot < 3, slot, jnp.where(turn == 3, 0, 2))
    mine = lanes == here
    mine_low = lanes == here + 1
    spot = jnp.sum(jnp.where(mine, index_all + 1.0, 0.0), axis=1, keepdims=True) - 1.0
    middle = jnp.where((lanes == 4) & (turn == 3), index_all + 1.0, 0.0)
    middle = jnp.sum(middle, axis=1, keepdims=True) - 1.0
    high = jnp.sum(jnp.where(mine, notes_all, 0.0), axis=1, keepdims=True)
    low = jnp.sum(jnp.where(mine_low, notes_all, 0.0), axis=1, keepdims=True)
    match = spot.astype(jnp.int32) == lanes
    pick0 = hot(match & (turn < 3))
    pick1 = hot(match & (turn > 3) & (turn < 7))
    pick_rest = hot(match & (slot == 3))
    pick_middle = hot(middle.astype(jnp.int32) == lanes)
    slots_only = jnp.where(match & (slot < 3), 1.0, 0.0).reshape(senders // 2, 2, 8, 128)
    upper = iota((senders // 2, 8, 128), 1) < 4
    slots_only = jnp.where(upper, slots_only[:, 0], pltpu.roll(slots_only[:, 1], 4, 1))
    pick_ref[...] = slots_only.reshape(total // 2, 128).astype(HALFS)
    tiles_ref[:, :half] = dot(pick0, recv_ref[...], "tn").astype(HALFS)
    tiles_ref[:, half : 2 * half] = dot(pick1, recv_ref[...], "tn").astype(HALFS)
    rest = tiles_ref.shape[1] - 2 * half
    tail = dot(pick_rest, recv_ref[:, :rest], "tn")
    tail = tail + dot(pick_middle, recv_ref[:, rest : 2 * rest], "tn")
    tiles_ref[:, 2 * half :] = tail.astype(HALFS)
    embed_load.wait()
    emb_ref[...] = dot(tiles_ref[...], embed_ref[...]).astype(HALFS)
    info = jnp.where(lanes == 0, high, jnp.where(lanes == 1, low, 0.0)).astype(HALFS)
    info = dot(info, pick0, "tn")[: CHUNK_ROWS - WIDTH].astype(HALFS)
    heads = chunk_ref.shape[0]
    for head in range(heads):
        if head % (heads // 2) == 0:
            group = head // (heads // 2)
            weight_loads[group].wait()
            part = dot(emb_ref[...], weight_ref[group]).T
        first = (head % (heads // 2)) * WIDTH
        chunk_ref[head, :WIDTH, :] = part[first : first + WIDTH].astype(HALFS)
        chunk_ref[head, WIDTH:, :] = info


def dilated_body(phase_ref, chunk_ref, query_ref, far_ref, rows_ref, local_ref):
    blocks = chunk_ref.shape[0]
    total = jnp.zeros((WIDTH, query_ref.shape[1]), FLOATS)
    target = 8 * iota((query_ref.shape[1], 128), 0) + phase_ref[0]
    for block in range(blocks):
        lanes = slice(block * 128, (block + 1) * 128)
        part = chunk_ref[block, :WIDTH, :]
        info = chunk_ref[block, WIDTH:, :].astype(FLOATS)
        local = ((info[0:1] - 1.0) * 128.0 + info[1:2]).astype(jnp.int32)
        rows_ref[:, lanes] = part
        local_ref[:, lanes] = jnp.broadcast_to(local, (8, 128))
        total = total + dot(part, hot(target == local), "nt")
    query_ref[...] = total[:HEAD_SIZE].astype(HALFS)
    for copy in range(far_ref.shape[0]):
        far_ref[copy] = total[HEAD_SIZE:].astype(HALFS)


def near_body(phase_ref, rows_ref, local_ref, grad_ref, place_ref, near_ref):
    seg = grad_ref.shape[2]
    local = local_ref[0:1, :]
    dilated = (iota((1, seg), 1) & 7) == phase_ref[0]
    for slide in range(grad_ref.shape[0]):
        spots = slice(slide * seg, (slide + 1) * seg)
        order = hot(local == iota((seg, local.shape[1]), 0) + slide * seg)
        parts = dot(rows_ref[...], order, "nt").astype(HALFS)
        place_ref[:, spots] = parts
        query = parts[:HEAD_SIZE]
        key = parts[HEAD_SIZE : 2 * HEAD_SIZE]
        value = parts[2 * HEAD_SIZE :]
        grad = grad_ref[slide]
        score = dot(key, query, "tn") * SCALE
        top = jnp.max(score, axis=0, keepdims=True)
        prob = jnp.exp(score - top)
        norm = 1.0 / jnp.sum(prob, axis=0, keepdims=True)
        prob = prob * jnp.where(dilated, 0.0, norm)
        dprob = dot(value, grad, "tn")
        delta = jnp.sum(prob * dprob, axis=0, keepdims=True)
        dscore = (prob * (dprob - delta)).astype(HALFS)
        near_ref[:HEAD_SIZE, spots] = dot(key, dscore) * SCALE
        near_ref[HEAD_SIZE : 2 * HEAD_SIZE, spots] = dot(query, dscore, "nt") * SCALE
        near_ref[2 * HEAD_SIZE :, spots] = dot(grad, prob.astype(HALFS), "nt")


def pick_body(phase_ref, grad_ref, out_ref):
    seg = grad_ref.shape[2]
    for pair in range(grad_ref.shape[0] // 2):
        grad = jnp.zeros((HEAD_SIZE, 128), FLOATS)
        for b in range(2):
            target = 8 * (iota((seg, 128), 1) - 64 * b) + phase_ref[0]
            grad = grad + dot(grad_ref[2 * pair + b], hot(iota((seg, 128), 0) == target))
        out_ref[:, pair * 128 : (pair + 1) * 128] = grad.astype(HALFS)


def far_body(query_ref, grad_ref, place_ref, far_ref, out_ref, dscore_ref, prob_ref):
    n = far_ref.shape[0]
    near = place_ref.shape[1] // 2
    seg = near // 2
    for pair in range(2):
        lanes = slice(pair * 128, (pair + 1) * 128)
        spots = slice(pair * near, (pair + 1) * near)
        query = query_ref[:, lanes]
        grad = grad_ref[:, lanes]
        key = jnp.concatenate(
            [place_ref[HEAD_SIZE : 2 * HEAD_SIZE, spots]]
            + [far_ref[k, :HEAD_SIZE, lanes] for k in range(n)],
            axis=1,
        )
        value = jnp.concatenate(
            [place_ref[2 * HEAD_SIZE :, spots]]
            + [far_ref[k, HEAD_SIZE:, lanes] for k in range(n)],
            axis=1,
        )
        size = key.shape[1]
        column = iota((128, size), 1)
        slide_of_key = jnp.where(column < near, column // seg, (column & 127) >> 6)
        same = slide_of_key == iota((128, size), 0) >> 6
        score = jnp.where(same, dot(query, key, "tn") * SCALE, -1e30)
        top = jnp.max(score, axis=1, keepdims=True)
        prob = jnp.exp(score - top)
        prob = prob * (1.0 / jnp.sum(prob, axis=1, keepdims=True))
        dprob = dot(grad, value, "tn")
        delta = jnp.sum(prob * dprob, axis=1, keepdims=True)
        dscore = (prob * (dprob - delta)).astype(HALFS)
        prob = prob.astype(HALFS)
        dkey = dot(query, dscore[:, near:]) * SCALE
        dvalue = dot(grad, prob[:, near:])
        for k in range(n):
            part = slice(k * 128, (k + 1) * 128)
            out_ref[k, :HEAD_SIZE, lanes] = dkey[:, part].astype(HALFS)
            out_ref[k, HEAD_SIZE:, lanes] = dvalue[:, part].astype(HALFS)
        dscore_ref[pair] = dscore
        prob_ref[pair] = prob[:, :near]


def sum_body(
    query_ref,
    grad_ref,
    place_ref,
    far_ref,
    dscore_ref,
    prob_ref,
    near_ref,
    dquery_ref,
    sum_ref,
):
    near = place_ref.shape[1] // 2
    sum_ref[:HEAD_SIZE, :] = near_ref[:HEAD_SIZE, :].astype(HALFS)
    for pair in range(2):
        lanes = slice(pair * 128, (pair + 1) * 128)
        spots = slice(pair * near, (pair + 1) * near)
        query = query_ref[:, lanes]
        grad = grad_ref[:, lanes]
        key = jnp.concatenate(
            [place_ref[HEAD_SIZE : 2 * HEAD_SIZE, spots]]
            + [far_ref[k, :HEAD_SIZE, lanes] for k in range(far_ref.shape[0])],
            axis=1,
        )
        dscore = dscore_ref[pair]
        dquery_ref[:, lanes] = (dot(key, dscore, "nt") * SCALE).astype(HALFS)
        dkey = dot(query, dscore[:, :near]) * SCALE
        dvalue = dot(grad, prob_ref[pair])
        middle = slice(HEAD_SIZE, 2 * HEAD_SIZE)
        sum_ref[middle, spots] = (near_ref[middle, spots] + dkey).astype(HALFS)
        last = slice(2 * HEAD_SIZE, WIDTH)
        sum_ref[last, spots] = (near_ref[last, spots] + dvalue).astype(HALFS)


def unplace_body(local_ref, sum_ref, out_ref):
    block = 512
    for start in range(0, out_ref.shape[1], block):
        lanes = slice(start, start + block)
        order = hot(local_ref[0:1, lanes] == iota((sum_ref.shape[1], block), 0))
        out_ref[:, lanes] = dot(sum_ref[...], order)


def finish_body(phase_ref, local_ref, main_ref, dquery_ref, far_ref, chunk_ref, rows_ref):
    far = far_ref[0].astype(FLOATS)
    for k in range(1, far_ref.shape[0]):
        far = far + far_ref[k].astype(FLOATS)
    sparse = jnp.concatenate([dquery_ref[...], far.astype(HALFS)], axis=0)
    local = local_ref[0:1, :]
    count = dquery_ref.shape[1]
    order = hot(local == 8 * iota((count, local.shape[1]), 0) + phase_ref[0])
    rows = (main_ref[...] + dot(sparse, order)).astype(HALFS)
    rows_ref[...] = rows
    for block in range(chunk_ref.shape[0] // WIDTH):
        chunk_ref[block * WIDTH : (block + 1) * WIDTH, :] = rows[
            :, block * 128 : (block + 1) * 128
        ]


def qkv_grad_body(core_ref, grad_ref, rows_ref, keep_ref, give_ref, all_ref):
    block = keep_ref.shape[1]
    part = dot(grad_ref[...], rows_ref[...]).T
    all_ref[...] = jnp.concatenate([part, jnp.zeros_like(part[:, : 256 - WIDTH])], axis=1)
    for chip in range(keep_ref.shape[0]):
        mine = pl.multiple_of((2 * chip + core_ref[0]) * block, block)
        other = pl.multiple_of((2 * chip + 1 - core_ref[0]) * block, block)
        keep_ref[chip] = all_ref[pl.ds(mine, block), :]
        give_ref[chip] = all_ref[pl.ds(other, block), :].astype(HALFS)


def merge_body(grad_ref, other_grad_ref, keep_ref, other_keep_ref, out_ref):
    rows, size = out_ref.shape[1] * 2 // 3, 128
    grad = jnp.concatenate([grad_ref[...], other_grad_ref[...]], axis=1)
    part = dot(grad, jnp.concatenate([keep_ref[...], other_keep_ref[...]], axis=0))
    part = part.astype(HALFS)
    columns = part.shape[0] // rows
    for block in range(out_ref.shape[0] // columns):
        left = block // 2 * 3 * size
        first = left if block % 2 == 0 else left + 2 * size
        other = left + size if block % 2 == 0 else left + size + 64
        for column in range(columns):
            here = part[column * rows : (column + 1) * rows]
            spot = block * columns + column
            out_ref[spot, :rows, :] = here[:, first : first + size]
            rest = here[:, other : other + 64]
            out_ref[spot, rows:, :] = jnp.concatenate(
                [rest[: rows // 2], rest[rows // 2 :]], axis=1
            )


def merge_qkv_body(chip_ref, keep_ref, given_ref, own_ref, *piece_refs):
    chips = keep_ref.shape[0]
    for k in range(chips):
        block = (chip_ref[0] + k) & (chips - 1)
        part = keep_ref[block] + given_ref[block].astype(FLOATS)
        if k == 0:
            own_ref[...] = part
        else:
            piece_refs[k - 1][...] = part.astype(HALFS)


def last_body(chip_ref, parts_ref, own_ref, *refs):
    piece_refs, embed_ref, qkv_ref = refs[:-2], refs[-2], refs[-1]
    total = parts_ref[0].astype(FLOATS)
    for k in range(1, parts_ref.shape[0]):
        total = total + parts_ref[k].astype(FLOATS)
    rest = jnp.concatenate([total[48:, :64], total[48:, 64:]], axis=0)
    even = jnp.concatenate([total[:48], rest], axis=1)
    odd = jnp.concatenate([rest, total[:48]], axis=1)
    embed_ref[...] = jnp.where((chip_ref[0] & 1) == 0, even, odd)
    qkv = own_ref[...]
    for ref in piece_refs:
        qkv = qkv + ref[...].astype(FLOATS)
    qkv_ref[...] = qkv.T[:WIDTH]


def load_body(_, *refs):
    count, sems = len(refs) // 2, refs[-1]
    loads = [
        pltpu.make_async_copy(refs[k], refs[count + k], sems.at[k]) for k in range(count)
    ]
    for load in loads:
        load.start()
    for load in loads:
        load.wait()


def load(after, *values):
    return call(
        load_body,
        [resident(value.shape) for value in values],
        [after, *values],
        anywhere=range(len(values) + 1),
        scratch_shapes=[pltpu.SemaphoreType.DMA((len(values),))],
    )


def back_body(rows_ref, weight_ref, pick_ref, grad_ref, back_ref):
    half = back_ref.shape[1]
    grad = dot(weight_ref[...], rows_ref[...]).astype(HALFS)
    grad_ref[...] = grad
    step = 128
    for start in range(0, pick_ref.shape[0], step):
        pick = pick_ref[start : start + step, :]
        both = interleave(dot(pick, grad[:half], "nt"), dot(pick, grad[half:], "nt"))
        back_ref[2 * start : 2 * (start + step), :] = both.astype(HALFS)


def collect_body(recv_ref, base_ref, out_ref):
    total, half = recv_ref.shape
    base, mask = base_ref[:, 0:1], base_ref[:, 1:2]
    rows = iota((base.shape[0], total), 1) & mask
    out_ref[:, :half] = dot(hot(rows == base), recv_ref[...]).astype(HALFS)
    out_ref[:, half:] = dot(hot(rows == base + 4), recv_ref[...]).astype(HALFS)


def per_device(tile_features, embed_weight, qkv_weight, positions, out_grad):
    n_slide = lax.axis_size("slide")
    n_tile = lax.axis_size("tile")
    devices = n_slide * n_tile
    every = ("slide", "tile")
    slots = tile_features.shape[0]
    slides, seg = out_grad.shape[0], out_grad.shape[1]
    wide = embed_weight.shape[1]
    half = wide // 2
    rows = slides * seg
    share = rows // n_tile
    row_here = lax.axis_index("slide")
    col_here = lax.axis_index("tile")
    phase = (col_here % n_slide).astype(jnp.int32).reshape(1)
    odd = (col_here % 2).astype(jnp.int32).reshape(1)
    core = row_here % 2
    tiles = tile_features.shape[1]
    packed = (tiles - 256) // 2

    with jax.named_scope("dispatch"):
        sent = call(
            dispatch_body,
            resident((devices * 8, packed)),
            [positions] + [tile_features] * 3,
            blocks={
                1: pl.BlockSpec((slots, packed), lambda i: (0, 0)),
                2: pl.BlockSpec((slots, packed), lambda i: (0, 1)),
                3: pl.BlockSpec((slots, 256), lambda i: (0, (tiles - 256) // 256)),
            },
            grid=(1,),
        )
        base = call(slots_body, resident((slots, 128), jnp.int32), [positions])
        arrived = lax.all_to_all(
            sent.reshape(devices, 8, packed), every, 0, 0, tiled=True
        ).reshape(devices * 8, packed)
    with jax.named_scope("project"):
        emb_rows, tile_rows, chunks, pick = call(
            project_body,
            [
                shaped((share, wide)),
                shaped((share, tiles)),
                resident((n_tile, CHUNK_ROWS, 128)),
                shaped((devices * 4, 128)),
            ],
            [odd, *stay(arrived), embed_weight, qkv_weight],
            smem=(0,),
            anywhere=(2, 3),
            scratch_shapes=[
                pltpu.VMEM(embed_weight.shape, HALFS),
                pltpu.VMEM((2, wide, qkv_weight.shape[1] // 2), HALFS),
                pltpu.SemaphoreType.DMA,
                pltpu.SemaphoreType.DMA((2,)),
            ],
        )
        chunks = lax.all_to_all(chunks, "tile", 0, 0, tiled=True)
    with jax.named_scope("swap_tiles"):
        swap = [(i, i ^ 1) for i in range(n_slide)]
        chips = n_slide // 2
        narrow = tiles // n_slide
        split = tile_rows.reshape(share, chips, 2, narrow)
        keep_cols = lax.dynamic_index_in_dim(split, core, 2, False).reshape(share, tiles // 2)
        give_cols = lax.dynamic_index_in_dim(split, 1 - core, 2, False).reshape(share, tiles // 2)
        got_cols = lax.ppermute(give_cols, "slide", swap)
    with jax.named_scope("dilated"):
        few = rows // n_slide
        query, far, head_rows, local = call(
            dilated_body,
            [
                resident((HEAD_SIZE, few)),
                resident((n_slide, 2 * HEAD_SIZE, few)),
                shaped((WIDTH, rows)),
                resident((8, rows), jnp.int32),
            ],
            [phase, *stay(chunks)],
            smem=(0,),
        )
        far = lax.all_to_all(far, "slide", 0, 0, tiled=True)
    with jax.named_scope("near"):
        grads = out_grad.transpose(0, 2, 1)
        dilated_grads = call(pick_body, resident((HEAD_SIZE, few)), [phase, grads], smem=(0,))
        placed, near = call(
            near_body,
            [resident((WIDTH, rows)), resident((WIDTH, rows), FLOATS)],
            [phase, head_rows, *stay(local), grads],
            smem=(0,),
            cost_estimate=pl.CostEstimate(
                flops=8_000_000_000, bytes_accessed=8_000_000, transcendentals=1 << 20
            ),
        )
    with jax.named_scope("far"):
        far_grads, dscores, probs = call(
            far_body,
            [
                resident((n_slide, 2 * HEAD_SIZE, few)),
                shaped((2, 128, rows)),
                shaped((2, 128, rows // 2)),
            ],
            stay(query, dilated_grads, placed, far),
        )
        far_grads = lax.all_to_all(far_grads, "slide", 0, 0, tiled=True)
    with jax.named_scope("unplace"):
        dquery, summed = call(
            sum_body,
            [resident((HEAD_SIZE, few)), resident((WIDTH, rows))],
            [*stay(query, dilated_grads, placed, far), dscores, probs, *stay(near)],
        )
        main = call(
            unplace_body,
            resident((WIDTH, rows), FLOATS),
            stay(local, summed),
            cost_estimate=pl.CostEstimate(
                flops=4_000_000_000, bytes_accessed=4_000_000, transcendentals=0
            ),
        )
        back_chunks, d_rows = call(
            finish_body,
            [resident((n_tile * WIDTH, 128)), shaped((WIDTH, rows))],
            [phase, *stay(local, main, dquery, far_grads)],
            smem=(0,),
        )
        back_rows = lax.all_to_all(
            back_chunks.reshape(n_tile, WIDTH, 128), "tile", 0, 0, tiled=True
        ).reshape(n_tile * WIDTH, 128)
    with jax.named_scope("qkv_grad"):
        all_rows = lax.all_gather(emb_rows, "tile", axis=0, tiled=True)
        block = wide // n_slide
        keep_qkv, give_qkv = call(
            qkv_grad_body,
            [shaped((chips, block, 256), FLOATS), shaped((chips, block, 256))],
            [core.astype(jnp.int32).reshape(1), d_rows, all_rows],
            smem=(0,),
            scratch_shapes=[pltpu.VMEM((wide, 256), FLOATS)],
        )
        chip = (row_here // 2).astype(jnp.int32).reshape(1)
        given_qkv = lax.ppermute(give_qkv, "slide", swap)
        own_qkv, *pieces = call(
            merge_qkv_body,
            [shaped((block, 256), FLOATS)] + [shaped((block, 256))] * (chips - 1),
            [chip, keep_qkv, given_qkv],
            smem=(0,),
        )
        pieces = [
            lax.ppermute(
                pieces[k - 1], "slide", [(i, (i + 2 * k) % n_slide) for i in range(n_slide)]
            )
            for k in range(1, chips)
        ]
    with jax.named_scope("tiles_grad"):
        (weight_here,) = load(d_rows, qkv_weight)
        grad_rows, back = call(
            back_body,
            [shaped((wide, share)), shaped((devices * 8, half))],
            [*stay(back_rows, weight_here), pick],
        )
        back = lax.all_to_all(
            back.reshape(devices, 8, half), every, 0, 0, tiled=True
        ).reshape(devices * 8, half)
        other_rows = lax.ppermute(grad_rows, "slide", swap)
        merged = call(
            merge_body,
            shaped((chips * n_tile, 72, 128)),
            [grad_rows, *stay(other_rows), keep_cols, got_cols],
        )
        merged, back = lax.optimization_barrier((merged, back))
    with jax.named_scope("collect"):
        d_embedded = call(collect_body, shaped((slots, wide)), stay(back, base))
    with jax.named_scope("embed_grad"):
        same_core = [
            [(2 * z + c) * n_tile + t for z in range(chips) for t in range(n_tile)]
            for c in range(2)
        ]
        parts = lax.all_to_all(
            merged, every, 0, 0, axis_index_groups=same_core, tiled=True
        )
        embed_grad, qkv_grad = call(
            last_body,
            [shaped((wide // n_tile, narrow), FLOATS), shaped((WIDTH, wide // n_slide), FLOATS)],
            [chip, *stay(parts), own_qkv, *pieces],
            smem=(0,),
        )
        embed_grad, qkv_grad = embed_grad.T, qkv_grad.T
    with jax.named_scope("feature_grad"):
        feature_grad = lax.dot_general(
            d_embedded, embed_weight, (((1,), (1,)), ((), ())), preferred_element_type=FLOATS
        ).astype(HALFS)
    return feature_grad, embed_grad, qkv_grad


def solution(mesh):
    placed = (P(("slide", "tile"), None), P(), P(), P(("slide", "tile")), P(None, "slide", "tile"))
    return jax.shard_map(
        per_device,
        mesh=mesh,
        in_specs=placed,
        out_specs=(P(("slide", "tile"), None), P("slide", "tile"), P("slide", "tile")),
        check_vma=False,
    )
```

```python
import functools

import jax
import jax.numpy as jnp
from jax import lax
from jax.experimental import pallas as pl
from jax.experimental.pallas import tpu as pltpu
from jax.sharding import PartitionSpec as P

HEAD_SIZE = 48
WIDTH = 3 * HEAD_SIZE
CHUNK_ROWS = 152
FLOATS = jnp.float32
HALFS = jnp.bfloat16
SCALE = HEAD_SIZE ** (-0.5)
VMEM = pltpu.CompilerParams(vmem_limit_bytes=56 * 1024 * 1024)


def iota(shape, dim):
    return lax.broadcasted_iota(jnp.int32, shape, dim)


def hot(cond):
    return jnp.where(cond, 1.0, 0.0).astype(HALFS)


def dot(a, b, dims="nn"):
    contract = (0 if dims[0] == "t" else 1, 1 if dims[1] == "t" else 0)
    return lax.dot_general(
        a, b, (((contract[0],), (contract[1],)), ((), ())), preferred_element_type=FLOATS
    )


def whole(memory=pltpu.VMEM):
    return pl.BlockSpec(memory_space=memory)


def call(body, outs, args, smem=(), anywhere=(), blocks=None, **kw):
    specs = [whole(pltpu.SMEM if i in smem else pltpu.VMEM) for i in range(len(args))]
    for i in anywhere:
        specs[i] = whole(pl.ANY)
    for i, block in (blocks or {}).items():
        specs[i] = block
    out_specs = jax.tree.map(lambda _: whole(), outs)
    return pl.pallas_call(
        body,
        out_shape=outs,
        in_specs=specs,
        out_specs=out_specs,
        compiler_params=VMEM,
        **kw,
    )(*args)


def shaped(shape, dtype=HALFS):
    return jax.ShapeDtypeStruct(shape, dtype)


def resident(shape, dtype=HALFS):
    return pltpu.VMEM(shape, dtype)


def stay(*values):
    return [pltpu.with_memory_space_constraint(value, pltpu.VMEM) for value in values]


def place(pos_ref):
    slots = pos_ref.shape[0]
    pos = pos_ref[...].reshape(1, slots)
    live = pos >= 0
    few = jnp.sum(jnp.where(live, 1, 0), axis=1, keepdims=True) <= 64
    pos = jnp.where(live, pos, 0)
    member = ((pos & 4095) >> 9 == iota((8, slots), 0)) & live
    upper = hot(iota((slots, slots), 0) < iota((slots, slots), 1))
    ranks = dot(hot(member), upper)
    rank = jnp.sum(jnp.where(member, ranks, 0.0), axis=0, keepdims=True).astype(jnp.int32)
    dest = ((pos & 4095) >> 9) * 128 + jnp.where(few, rank * 16, (rank & 15) * 8)
    dest = jnp.where(live, dest, -16)
    sub = jnp.where(few, 0, rank >> 4)
    mask = jnp.where(few, -9, -1)
    return pos, few, dest, sub, mask


def interleave(first, second):
    step, half = first.shape
    upper = (iota((step, half), 0) & 7) < 4
    even = jnp.where(upper, first, pltpu.roll(second, 4, 0))
    odd = jnp.where(upper, pltpu.roll(first, step - 4, 0), second)
    both = jnp.stack(
        [even.reshape(step // 8, 8, half), odd.reshape(step // 8, 8, half)], axis=1
    )
    return both.reshape(2 * step, half)


def dispatch_body(pos_ref, left_ref, right_ref, rest_ref, send_ref):
    slots, half = left_ref.shape
    rest = rest_ref.shape[1]
    pos, few, dest, sub, mask = place(pos_ref)
    dest, mask = dest >> 1, jnp.where(few, -5, -1)
    local = ((pos >> 12) << 9) + (pos & 511)
    lane = iota((128, slots), 0) - 4 * sub
    notes = jnp.where(
        lane == 0,
        (local >> 7) + 1,
        jnp.where(lane == 1, local & 127, jnp.where((lane == 2) & few, 1, 0)),
    )
    notes = notes.astype(FLOATS).astype(HALFS)
    last = [jnp.where(sub == k, dest + 3, -16) for k in range(3)]
    step = 128
    for start in range(0, send_ref.shape[0] // 2, step):
        rows = (iota((step, slots), 0) + start) & mask
        whole_rows = hot(rows == dest + sub)
        tail = rest_ref[...]
        first = jnp.concatenate(
            [dot(hot(rows == last[k]), tail) for k in range(2)]
            + [dot(hot(rows == dest + 3), notes, "nt")],
            axis=1,
        )
        first = first + dot(whole_rows, left_ref[...])
        second = dot(whole_rows, right_ref[...])
        second = jnp.concatenate(
            [second[:, :rest] + dot(hot(rows == last[2]), tail), second[:, rest:]], axis=1
        )
        both = interleave(first, second)
        send_ref[2 * start : 2 * (start + step), :] = both.astype(HALFS)


def slots_body(pos_ref, base_ref):
    slots = pos_ref.shape[0]
    _, _, dest, sub, mask = place(pos_ref)
    same = iota((slots, slots), 0) == iota((slots, slots), 1)
    base = jnp.sum(jnp.where(same, dest + sub, 0), axis=1, keepdims=True)
    base_ref[...] = jnp.where(iota(base_ref.shape, 1) == 0, base, mask)


def project_body(
    odd_ref,
    recv_ref,
    embed_hbm_ref,
    weight_hbm_ref,
    emb_ref,
    tiles_ref,
    chunk_ref,
    pick_ref,
    embed_ref,
    weight_ref,
    embed_sem,
    weight_sem,
):
    embed_load = pltpu.make_async_copy(embed_hbm_ref, embed_ref, embed_sem)
    embed_load.start()
    columns = weight_ref.shape[2]
    weight_loads = [
        pltpu.make_async_copy(
            weight_hbm_ref.at[:, k * columns : (k + 1) * columns], weight_ref.at[k], weight_sem.at[k]
        )
        for k in range(2)
    ]
    for one in weight_loads:
        one.start()
    total = recv_ref.shape[0]
    senders = total // 8
    sel = hot(iota((senders, total), 1) == 8 * iota((senders, total), 0) + 3)
    half = recv_ref.shape[1]
    notes = dot(sel, recv_ref[:, half - 128 :])
    lane = iota((senders, 128), 1)
    lower = hot(iota((senders, senders), 0) > iota((senders, senders), 1))
    shared = (notes > 0.5) & (lane == 2)
    order = dot(lower, hot(shared)).astype(jnp.int32)
    other = shared & ((order & 1) != odd_ref[0])
    to_first = hot((iota((128, 128), 0) == 2) & (iota((128, 128), 1) == 0))
    other = dot(hot(other), to_first) > 0.5
    valid = (notes > 0.5) & ((lane & 3) == 0) & (lane < 12) & jnp.logical_not(other)
    cum = dot(lower, hot(valid))
    ones = jnp.where(valid, 1.0, 0.0)
    first = jnp.sum(jnp.where(lane == 0, ones, 0.0), axis=0, keepdims=True)
    first = jnp.sum(first, axis=1, keepdims=True)
    second = jnp.sum(jnp.where(lane == 4, ones, 0.0), axis=0, keepdims=True)
    second = jnp.sum(second, axis=1, keepdims=True)
    shift = jnp.where(lane >= 4, first, 0.0) + jnp.where(lane >= 8, second, 0.0)
    index = jnp.where(valid, cum + shift, -1.0)
    repeat = hot(iota((total, senders), 0) >> 3 == iota((total, senders), 1))
    index_all = dot(repeat, index.astype(HALFS))
    notes_all = dot(repeat, notes.astype(HALFS))
    turn = iota((total, 128), 0) & 7
    lanes = iota((total, 128), 1)
    slot = turn & 3
    here = 4 * jnp.where(slot < 3, slot, jnp.where(turn == 3, 0, 2))
    mine = lanes == here
    mine_low = lanes == here + 1
    spot = jnp.sum(jnp.where(mine, index_all + 1.0, 0.0), axis=1, keepdims=True) - 1.0
    middle = jnp.where((lanes == 4) & (turn == 3), index_all + 1.0, 0.0)
    middle = jnp.sum(middle, axis=1, keepdims=True) - 1.0
    high = jnp.sum(jnp.where(mine, notes_all, 0.0), axis=1, keepdims=True)
    low = jnp.sum(jnp.where(mine_low, notes_all, 0.0), axis=1, keepdims=True)
    match = spot.astype(jnp.int32) == lanes
    pick0 = hot(match & (turn < 3))
    pick1 = hot(match & (turn > 3) & (turn < 7))
    pick_rest = hot(match & (slot == 3))
    pick_middle = hot(middle.astype(jnp.int32) == lanes)
    slots_only = jnp.where(match & (slot < 3), 1.0, 0.0).reshape(senders // 2, 2, 8, 128)
    upper = iota((senders // 2, 8, 128), 1) < 4
    slots_only = jnp.where(upper, slots_only[:, 0], pltpu.roll(slots_only[:, 1], 4, 1))
    pick_ref[...] = slots_only.reshape(total // 2, 128).astype(HALFS)
    tiles_ref[:, :half] = dot(pick0, recv_ref[...], "tn").astype(HALFS)
    tiles_ref[:, half : 2 * half] = dot(pick1, recv_ref[...], "tn").astype(HALFS)
    rest = tiles_ref.shape[1] - 2 * half
    tail = dot(pick_rest, recv_ref[:, :rest], "tn")
    tail = tail + dot(pick_middle, recv_ref[:, rest : 2 * rest], "tn")
    tiles_ref[:, 2 * half :] = tail.astype(HALFS)
    embed_load.wait()
    emb_ref[...] = dot(tiles_ref[...], embed_ref[...]).astype(HALFS)
    info = jnp.where(lanes == 0, high, jnp.where(lanes == 1, low, 0.0)).astype(HALFS)
    info = dot(info, pick0, "tn")[: CHUNK_ROWS - WIDTH].astype(HALFS)
    heads = chunk_ref.shape[0]
    for head in range(heads):
        if head % (heads // 2) == 0:
            group = head // (heads // 2)
            weight_loads[group].wait()
            part = dot(emb_ref[...], weight_ref[group]).T
        first = (head % (heads // 2)) * WIDTH
        chunk_ref[head, :WIDTH, :] = part[first : first + WIDTH].astype(HALFS)
        chunk_ref[head, WIDTH:, :] = info


def dilated_body(phase_ref, chunk_ref, query_ref, far_ref, rows_ref, local_ref):
    blocks = chunk_ref.shape[0]
    total = jnp.zeros((WIDTH, query_ref.shape[1]), FLOATS)
    target = 8 * iota((query_ref.shape[1], 128), 0) + phase_ref[0]
    for block in range(blocks):
        lanes = slice(block * 128, (block + 1) * 128)
        part = chunk_ref[block, :WIDTH, :]
        info = chunk_ref[block, WIDTH:, :].astype(FLOATS)
        local = ((info[0:1] - 1.0) * 128.0 + info[1:2]).astype(jnp.int32)
        rows_ref[:, lanes] = part
        local_ref[:, lanes] = jnp.broadcast_to(local, (8, 128))
        total = total + dot(part, hot(target == local), "nt")
    query_ref[...] = total[:HEAD_SIZE].astype(HALFS)
    for copy in range(far_ref.shape[0]):
        far_ref[copy] = total[HEAD_SIZE:].astype(HALFS)


def near_attend(parts, grad, dilated):
    query = parts[:HEAD_SIZE]
    key = parts[HEAD_SIZE : 2 * HEAD_SIZE]
    value = parts[2 * HEAD_SIZE :]
    score = dot(key, query, "tn") * SCALE
    top = jnp.max(score, axis=0, keepdims=True)
    prob = jnp.exp(score - top)
    norm = 1.0 / jnp.sum(prob, axis=0, keepdims=True)
    prob = prob * jnp.where(dilated, 0.0, norm)
    dprob = dot(value, grad, "tn")
    delta = jnp.sum(prob * dprob, axis=0, keepdims=True)
    dscore = (prob * (dprob - delta)).astype(HALFS)
    return (
        dot(key, dscore) * SCALE,
        dot(query, dscore, "nt") * SCALE,
        dot(grad, prob.astype(HALFS), "nt"),
    )


def near_body(phase_ref, rows_ref, local_ref, grad_ref, place_ref, near_ref):
    seg = grad_ref.shape[2]
    local = local_ref[0:1, :]
    dilated = (iota((1, seg), 1) & 7) == phase_ref[0]
    for slide in range(grad_ref.shape[0]):
        spots = slice(slide * seg, (slide + 1) * seg)
        order = hot(local == iota((seg, local.shape[1]), 0) + slide * seg)
        parts = dot(rows_ref[...], order, "nt").astype(HALFS)
        place_ref[:, spots] = parts
        if slide * seg < near_ref.shape[1]:
            grads = near_attend(parts, grad_ref[slide], dilated)
            for k in range(3):
                near_ref[k * HEAD_SIZE : (k + 1) * HEAD_SIZE, spots] = grads[k]


def pick_body(phase_ref, grad_ref, out_ref):
    seg = grad_ref.shape[2]
    for pair in range(grad_ref.shape[0] // 2):
        grad = jnp.zeros((HEAD_SIZE, 128), FLOATS)
        for b in range(2):
            target = 8 * (iota((seg, 128), 1) - 64 * b) + phase_ref[0]
            grad = grad + dot(grad_ref[2 * pair + b], hot(iota((seg, 128), 0) == target))
        out_ref[:, pair * 128 : (pair + 1) * 128] = grad.astype(HALFS)


def far_body(query_ref, grad_ref, place_ref, far_ref, out_ref, dscore_ref, prob_ref):
    n = far_ref.shape[0]
    near = place_ref.shape[1] // 2
    seg = near // 2
    for pair in range(2):
        lanes = slice(pair * 128, (pair + 1) * 128)
        spots = slice(pair * near, (pair + 1) * near)
        query = query_ref[:, lanes]
        grad = grad_ref[:, lanes]
        key = jnp.concatenate(
            [place_ref[HEAD_SIZE : 2 * HEAD_SIZE, spots]]
            + [far_ref[k, :HEAD_SIZE, lanes] for k in range(n)],
            axis=1,
        )
        value = jnp.concatenate(
            [place_ref[2 * HEAD_SIZE :, spots]]
            + [far_ref[k, HEAD_SIZE:, lanes] for k in range(n)],
            axis=1,
        )
        size = key.shape[1]
        column = iota((128, size), 1)
        slide_of_key = jnp.where(column < near, column // seg, (column & 127) >> 6)
        same = slide_of_key == iota((128, size), 0) >> 6
        score = jnp.where(same, dot(query, key, "tn") * SCALE, -1e30)
        top = jnp.max(score, axis=1, keepdims=True)
        prob = jnp.exp(score - top)
        prob = prob * (1.0 / jnp.sum(prob, axis=1, keepdims=True))
        dprob = dot(grad, value, "tn")
        delta = jnp.sum(prob * dprob, axis=1, keepdims=True)
        dscore = (prob * (dprob - delta)).astype(HALFS)
        prob = prob.astype(HALFS)
        dkey = dot(query, dscore[:, near:]) * SCALE
        dvalue = dot(grad, prob[:, near:])
        for k in range(n):
            part = slice(k * 128, (k + 1) * 128)
            out_ref[k, :HEAD_SIZE, lanes] = dkey[:, part].astype(HALFS)
            out_ref[k, HEAD_SIZE:, lanes] = dvalue[:, part].astype(HALFS)
        dscore_ref[pair] = dscore
        prob_ref[pair] = prob[:, :near]


def sum_body(
    phase_ref,
    all_grad_ref,
    query_ref,
    grad_ref,
    place_ref,
    far_ref,
    dscore_ref,
    prob_ref,
    near_ref,
    dquery_ref,
    sum_ref,
):
    near = place_ref.shape[1] // 2
    seg = near // 2
    dilated = (iota((1, seg), 1) & 7) == phase_ref[0]
    for pair in range(2):
        lanes = slice(pair * 128, (pair + 1) * 128)
        query = query_ref[:, lanes]
        grad = grad_ref[:, lanes]
        key = jnp.concatenate(
            [place_ref[HEAD_SIZE : 2 * HEAD_SIZE, pair * near : (pair + 1) * near]]
            + [far_ref[k, :HEAD_SIZE, lanes] for k in range(far_ref.shape[0])],
            axis=1,
        )
        dscore = dscore_ref[pair]
        dquery_ref[:, lanes] = (dot(key, dscore, "nt") * SCALE).astype(HALFS)
        dkey = dot(query, dscore[:, :near]) * SCALE
        dvalue = dot(grad, prob_ref[pair])
        for b in range(2):
            slide = 2 * pair + b
            spots = slice(slide * seg, (slide + 1) * seg)
            part = slice(b * seg, (b + 1) * seg)
            if pair == 0:
                grads = [near_ref[k * HEAD_SIZE : (k + 1) * HEAD_SIZE, spots] for k in range(3)]
            else:
                grads = near_attend(place_ref[:, spots], all_grad_ref[slide], dilated)
            sum_ref[:HEAD_SIZE, spots] = grads[0].astype(HALFS)
            sum_ref[HEAD_SIZE : 2 * HEAD_SIZE, spots] = (grads[1] + dkey[:, part]).astype(HALFS)
            sum_ref[2 * HEAD_SIZE :, spots] = (grads[2] + dvalue[:, part]).astype(HALFS)


def unplace_body(local_ref, sum_ref, out_ref):
    block = 512
    for start in range(0, out_ref.shape[1], block):
        lanes = slice(start, start + block)
        order = hot(local_ref[0:1, lanes] == iota((sum_ref.shape[1], block), 0))
        out_ref[:, lanes] = dot(sum_ref[...], order)


def finish_body(phase_ref, local_ref, main_ref, dquery_ref, far_ref, chunk_ref, rows_ref):
    far = far_ref[0].astype(FLOATS)
    for k in range(1, far_ref.shape[0]):
        far = far + far_ref[k].astype(FLOATS)
    sparse = jnp.concatenate([dquery_ref[...], far.astype(HALFS)], axis=0)
    local = local_ref[0:1, :]
    count = dquery_ref.shape[1]
    order = hot(local == 8 * iota((count, local.shape[1]), 0) + phase_ref[0])
    rows = (main_ref[...] + dot(sparse, order)).astype(HALFS)
    rows_ref[...] = rows
    for block in range(chunk_ref.shape[0] // WIDTH):
        chunk_ref[block * WIDTH : (block + 1) * WIDTH, :] = rows[
            :, block * 128 : (block + 1) * 128
        ]


def qkv_grad_body(core_ref, grad_ref, rows_ref, keep_ref, give_ref, all_ref):
    block = keep_ref.shape[1]
    part = dot(grad_ref[...], rows_ref[...]).T
    all_ref[...] = jnp.concatenate([part, jnp.zeros_like(part[:, : 256 - WIDTH])], axis=1)
    for chip in range(keep_ref.shape[0]):
        mine = pl.multiple_of((2 * chip + core_ref[0]) * block, block)
        other = pl.multiple_of((2 * chip + 1 - core_ref[0]) * block, block)
        keep_ref[chip] = all_ref[pl.ds(mine, block), :]
        give_ref[chip] = all_ref[pl.ds(other, block), :].astype(HALFS)


def merge_body(grad_ref, other_grad_ref, keep_ref, other_keep_ref, out_ref):
    rows, size = out_ref.shape[1] * 2 // 3, 128
    grad = jnp.concatenate([grad_ref[...], other_grad_ref[...]], axis=1)
    part = dot(grad, jnp.concatenate([keep_ref[...], other_keep_ref[...]], axis=0))
    part = part.astype(HALFS)
    columns = part.shape[0] // rows
    for block in range(out_ref.shape[0] // columns):
        left = block // 2 * 3 * size
        first = left if block % 2 == 0 else left + 2 * size
        other = left + size if block % 2 == 0 else left + size + 64
        for column in range(columns):
            here = part[column * rows : (column + 1) * rows]
            spot = block * columns + column
            out_ref[spot, :rows, :] = here[:, first : first + size]
            rest = here[:, other : other + 64]
            out_ref[spot, rows:, :] = jnp.concatenate(
                [rest[: rows // 2], rest[rows // 2 :]], axis=1
            )


def merge_qkv_body(chip_ref, keep_ref, given_ref, own_ref, *piece_refs):
    chips = keep_ref.shape[0]
    for k in range(chips):
        block = (chip_ref[0] + k) & (chips - 1)
        part = keep_ref[block] + given_ref[block].astype(FLOATS)
        if k == 0:
            own_ref[...] = part
        else:
            piece_refs[k - 1][...] = part.astype(HALFS)


def last_body(chip_ref, parts_ref, own_ref, *refs):
    piece_refs, embed_ref, qkv_ref = refs[:-2], refs[-2], refs[-1]
    total = parts_ref[0].astype(FLOATS)
    for k in range(1, parts_ref.shape[0]):
        total = total + parts_ref[k].astype(FLOATS)
    rest = jnp.concatenate([total[48:, :64], total[48:, 64:]], axis=0)
    even = jnp.concatenate([total[:48], rest], axis=1)
    odd = jnp.concatenate([rest, total[:48]], axis=1)
    embed_ref[...] = jnp.where((chip_ref[0] & 1) == 0, even, odd)
    qkv = own_ref[...]
    for ref in piece_refs:
        qkv = qkv + ref[...].astype(FLOATS)
    qkv_ref[...] = qkv.T[:WIDTH]


def load_body(_, *refs):
    count, sems = len(refs) // 2, refs[-1]
    loads = [
        pltpu.make_async_copy(refs[k], refs[count + k], sems.at[k]) for k in range(count)
    ]
    for load in loads:
        load.start()
    for load in loads:
        load.wait()


def load(after, *values):
    return call(
        load_body,
        [resident(value.shape) for value in values],
        [after, *values],
        anywhere=range(len(values) + 1),
        scratch_shapes=[pltpu.SemaphoreType.DMA((len(values),))],
    )


def back_body(rows_ref, weight_ref, pick_ref, grad_ref, back_ref):
    half = back_ref.shape[1]
    grad = dot(weight_ref[...], rows_ref[...]).astype(HALFS)
    grad_ref[...] = grad
    step = 128
    for start in range(0, pick_ref.shape[0], step):
        pick = pick_ref[start : start + step, :]
        both = interleave(dot(pick, grad[:half], "nt"), dot(pick, grad[half:], "nt"))
        back_ref[2 * start : 2 * (start + step), :] = both.astype(HALFS)


def collect_body(recv_ref, base_ref, out_ref):
    total, half = recv_ref.shape
    base, mask = base_ref[:, 0:1], base_ref[:, 1:2]
    rows = iota((base.shape[0], total), 1) & mask
    out_ref[:, :half] = dot(hot(rows == base), recv_ref[...]).astype(HALFS)
    out_ref[:, half:] = dot(hot(rows == base + 4), recv_ref[...]).astype(HALFS)


def per_device(tile_features, embed_weight, qkv_weight, positions, out_grad):
    n_slide = lax.axis_size("slide")
    n_tile = lax.axis_size("tile")
    devices = n_slide * n_tile
    every = ("slide", "tile")
    slots = tile_features.shape[0]
    slides, seg = out_grad.shape[0], out_grad.shape[1]
    wide = embed_weight.shape[1]
    half = wide // 2
    rows = slides * seg
    share = rows // n_tile
    row_here = lax.axis_index("slide")
    col_here = lax.axis_index("tile")
    phase = (col_here % n_slide).astype(jnp.int32).reshape(1)
    odd = (col_here % 2).astype(jnp.int32).reshape(1)
    core = row_here % 2
    tiles = tile_features.shape[1]
    packed = (tiles - 256) // 2

    with jax.named_scope("dispatch"):
        sent = call(
            dispatch_body,
            resident((devices * 8, packed)),
            [positions] + [tile_features] * 3,
            blocks={
                1: pl.BlockSpec((slots, packed), lambda i: (0, 0)),
                2: pl.BlockSpec((slots, packed), lambda i: (0, 1)),
                3: pl.BlockSpec((slots, 256), lambda i: (0, (tiles - 256) // 256)),
            },
            grid=(1,),
        )
        base = call(slots_body, resident((slots, 128), jnp.int32), [positions])
        arrived = lax.all_to_all(
            sent.reshape(devices, 8, packed), every, 0, 0, tiled=True
        ).reshape(devices * 8, packed)
    with jax.named_scope("project"):
        emb_rows, tile_rows, chunks, pick = call(
            project_body,
            [
                shaped((share, wide)),
                shaped((share, tiles)),
                resident((n_tile, CHUNK_ROWS, 128)),
                shaped((devices * 4, 128)),
            ],
            [odd, *stay(arrived), embed_weight, qkv_weight],
            smem=(0,),
            anywhere=(2, 3),
            scratch_shapes=[
                pltpu.VMEM(embed_weight.shape, HALFS),
                pltpu.VMEM((2, wide, qkv_weight.shape[1] // 2), HALFS),
                pltpu.SemaphoreType.DMA,
                pltpu.SemaphoreType.DMA((2,)),
            ],
        )
        chunks = lax.all_to_all(chunks, "tile", 0, 0, tiled=True)
    with jax.named_scope("swap_tiles"):
        swap = [(i, i ^ 1) for i in range(n_slide)]
        chips = n_slide // 2
        narrow = tiles // n_slide
        split = tile_rows.reshape(share, chips, 2, narrow)
        keep_cols = lax.dynamic_index_in_dim(split, core, 2, False).reshape(share, tiles // 2)
        give_cols = lax.dynamic_index_in_dim(split, 1 - core, 2, False).reshape(share, tiles // 2)
        got_cols = lax.ppermute(give_cols, "slide", swap)
    with jax.named_scope("dilated"):
        few = rows // n_slide
        query, far, head_rows, local = call(
            dilated_body,
            [
                resident((HEAD_SIZE, few)),
                resident((n_slide, 2 * HEAD_SIZE, few)),
                shaped((WIDTH, rows)),
                resident((8, rows), jnp.int32),
            ],
            [phase, *stay(chunks)],
            smem=(0,),
        )
        far = lax.all_to_all(far, "slide", 0, 0, tiled=True)
    with jax.named_scope("near"):
        grads = out_grad.transpose(0, 2, 1)
        dilated_grads = call(pick_body, resident((HEAD_SIZE, few)), [phase, grads], smem=(0,))
        placed, near = call(
            near_body,
            [resident((WIDTH, rows)), resident((WIDTH, rows // 2), FLOATS)],
            [phase, head_rows, *stay(local), grads],
            smem=(0,),
            cost_estimate=pl.CostEstimate(
                flops=8_000_000_000, bytes_accessed=8_000_000, transcendentals=1 << 20
            ),
        )
    with jax.named_scope("far"):
        far_grads, dscores, probs = call(
            far_body,
            [
                resident((n_slide, 2 * HEAD_SIZE, few)),
                shaped((2, 128, rows)),
                shaped((2, 128, rows // 2)),
            ],
            stay(query, dilated_grads, placed, far),
        )
        far_grads = lax.all_to_all(far_grads, "slide", 0, 0, tiled=True)
    with jax.named_scope("unplace"):
        dquery, summed = call(
            sum_body,
            [resident((HEAD_SIZE, few)), resident((WIDTH, rows))],
            [
                phase,
                grads,
                *stay(query, dilated_grads, placed, far),
                dscores,
                probs,
                *stay(near),
            ],
            smem=(0,),
        )
        main = call(
            unplace_body,
            resident((WIDTH, rows), FLOATS),
            stay(local, summed),
            cost_estimate=pl.CostEstimate(
                flops=4_000_000_000, bytes_accessed=4_000_000, transcendentals=0
            ),
        )
        back_chunks, d_rows = call(
            finish_body,
            [resident((n_tile * WIDTH, 128)), shaped((WIDTH, rows))],
            [phase, *stay(local, main, dquery, far_grads)],
            smem=(0,),
        )
        back_rows = lax.all_to_all(
            back_chunks.reshape(n_tile, WIDTH, 128), "tile", 0, 0, tiled=True
        ).reshape(n_tile * WIDTH, 128)
    with jax.named_scope("qkv_grad"):
        all_rows = lax.all_gather(emb_rows, "tile", axis=0, tiled=True)
        block = wide // n_slide
        keep_qkv, give_qkv = call(
            qkv_grad_body,
            [shaped((chips, block, 256), FLOATS), shaped((chips, block, 256))],
            [core.astype(jnp.int32).reshape(1), d_rows, all_rows],
            smem=(0,),
            scratch_shapes=[pltpu.VMEM((wide, 256), FLOATS)],
        )
        chip = (row_here // 2).astype(jnp.int32).reshape(1)
        given_qkv = lax.ppermute(give_qkv, "slide", swap)
        own_qkv, *pieces = call(
            merge_qkv_body,
            [shaped((block, 256), FLOATS)] + [shaped((block, 256))] * (chips - 1),
            [chip, keep_qkv, given_qkv],
            smem=(0,),
        )
        pieces = [
            lax.ppermute(
                pieces[k - 1], "slide", [(i, (i + 2 * k) % n_slide) for i in range(n_slide)]
            )
            for k in range(1, chips)
        ]
    with jax.named_scope("tiles_grad"):
        (weight_here,) = load(d_rows, qkv_weight)
        grad_rows, back = call(
            back_body,
            [shaped((wide, share)), shaped((devices * 8, half))],
            [*stay(back_rows, weight_here), pick],
        )
        back = lax.all_to_all(
            back.reshape(devices, 8, half), every, 0, 0, tiled=True
        ).reshape(devices * 8, half)
        other_rows = lax.ppermute(grad_rows, "slide", swap)
        merged = call(
            merge_body,
            shaped((chips * n_tile, 72, 128)),
            [grad_rows, *stay(other_rows), keep_cols, got_cols],
        )
        merged, back = lax.optimization_barrier((merged, back))
    with jax.named_scope("collect"):
        d_embedded = call(collect_body, shaped((slots, wide)), stay(back, base))
    with jax.named_scope("embed_grad"):
        same_core = [
            [(2 * z + c) * n_tile + t for z in range(chips) for t in range(n_tile)]
            for c in range(2)
        ]
        parts = lax.all_to_all(
            merged, every, 0, 0, axis_index_groups=same_core, tiled=True
        )
        embed_grad, qkv_grad = call(
            last_body,
            [shaped((wide // n_tile, narrow), FLOATS), shaped((WIDTH, wide // n_slide), FLOATS)],
            [chip, *stay(parts), own_qkv, *pieces],
            smem=(0,),
        )
        embed_grad, qkv_grad = embed_grad.T, qkv_grad.T
    with jax.named_scope("feature_grad"):
        feature_grad = lax.dot_general(
            d_embedded, embed_weight, (((1,), (1,)), ((), ())), preferred_element_type=FLOATS
        ).astype(HALFS)
    return feature_grad, embed_grad, qkv_grad


def solution(mesh):
    placed = (P(("slide", "tile"), None), P(), P(), P(("slide", "tile")), P(None, "slide", "tile"))
    return jax.shard_map(
        per_device,
        mesh=mesh,
        in_specs=placed,
        out_specs=(P(("slide", "tile"), None), P("slide", "tile"), P("slide", "tile")),
        check_vma=False,
    )
```

```python
import functools

import jax
import jax.numpy as jnp
from jax import lax
from jax.experimental import pallas as pl
from jax.experimental.pallas import tpu as pltpu
from jax.sharding import PartitionSpec as P

HEAD_SIZE = 48
WIDTH = 3 * HEAD_SIZE
CHUNK_ROWS = 152
FLOATS = jnp.float32
HALFS = jnp.bfloat16
SCALE = HEAD_SIZE ** (-0.5)
VMEM = pltpu.CompilerParams(vmem_limit_bytes=56 * 1024 * 1024)


def iota(shape, dim):
    return lax.broadcasted_iota(jnp.int32, shape, dim)


def hot(cond):
    return jnp.where(cond, 1.0, 0.0).astype(HALFS)


def dot(a, b, dims="nn"):
    contract = (0 if dims[0] == "t" else 1, 1 if dims[1] == "t" else 0)
    return lax.dot_general(
        a, b, (((contract[0],), (contract[1],)), ((), ())), preferred_element_type=FLOATS
    )


def whole(memory=pltpu.VMEM):
    return pl.BlockSpec(memory_space=memory)


def call(body, outs, args, smem=(), anywhere=(), blocks=None, **kw):
    specs = [whole(pltpu.SMEM if i in smem else pltpu.VMEM) for i in range(len(args))]
    for i in anywhere:
        specs[i] = whole(pl.ANY)
    for i, block in (blocks or {}).items():
        specs[i] = block
    out_specs = jax.tree.map(lambda _: whole(), outs)
    return pl.pallas_call(
        body,
        out_shape=outs,
        in_specs=specs,
        out_specs=out_specs,
        compiler_params=VMEM,
        **kw,
    )(*args)


def shaped(shape, dtype=HALFS):
    return jax.ShapeDtypeStruct(shape, dtype)


def resident(shape, dtype=HALFS):
    return pltpu.VMEM(shape, dtype)


def stay(*values):
    return [pltpu.with_memory_space_constraint(value, pltpu.VMEM) for value in values]


def place(pos_ref):
    slots = pos_ref.shape[0]
    pos = pos_ref[...].reshape(1, slots)
    live = pos >= 0
    few = jnp.sum(jnp.where(live, 1, 0), axis=1, keepdims=True) <= 64
    pos = jnp.where(live, pos, 0)
    member = ((pos & 4095) >> 9 == iota((8, slots), 0)) & live
    upper = hot(iota((slots, slots), 0) < iota((slots, slots), 1))
    ranks = dot(hot(member), upper)
    rank = jnp.sum(jnp.where(member, ranks, 0.0), axis=0, keepdims=True).astype(jnp.int32)
    dest = ((pos & 4095) >> 9) * 128 + jnp.where(few, rank * 16, (rank & 15) * 8)
    dest = jnp.where(live, dest, -16)
    sub = jnp.where(few, 0, rank >> 4)
    mask = jnp.where(few, -9, -1)
    return pos, few, dest, sub, mask


def interleave(first, second):
    step, half = first.shape
    upper = (iota((step, half), 0) & 7) < 4
    even = jnp.where(upper, first, pltpu.roll(second, 4, 0))
    odd = jnp.where(upper, pltpu.roll(first, step - 4, 0), second)
    both = jnp.stack(
        [even.reshape(step // 8, 8, half), odd.reshape(step // 8, 8, half)], axis=1
    )
    return both.reshape(2 * step, half)


def dispatch_body(pos_ref, left_ref, right_ref, rest_ref, send_ref):
    slots, half = left_ref.shape
    rest = rest_ref.shape[1]
    pos, few, dest, sub, mask = place(pos_ref)
    dest, mask = dest >> 1, jnp.where(few, -5, -1)
    local = ((pos >> 12) << 9) + (pos & 511)
    lane = iota((128, slots), 0) - 4 * sub
    notes = jnp.where(
        lane == 0,
        (local >> 7) + 1,
        jnp.where(lane == 1, local & 127, jnp.where((lane == 2) & few, 1, 0)),
    )
    notes = notes.astype(FLOATS).astype(HALFS)
    last = [jnp.where(sub == k, dest + 3, -16) for k in range(3)]
    step = 128
    for start in range(0, send_ref.shape[0] // 2, step):
        rows = (iota((step, slots), 0) + start) & mask
        whole_rows = hot(rows == dest + sub)
        tail = rest_ref[...]
        first = jnp.concatenate(
            [dot(hot(rows == last[k]), tail) for k in range(2)]
            + [dot(hot(rows == dest + 3), notes, "nt")],
            axis=1,
        )
        first = first + dot(whole_rows, left_ref[...])
        second = dot(whole_rows, right_ref[...])
        second = jnp.concatenate(
            [second[:, :rest] + dot(hot(rows == last[2]), tail), second[:, rest:]], axis=1
        )
        both = interleave(first, second)
        send_ref[2 * start : 2 * (start + step), :] = both.astype(HALFS)


def slots_body(pos_ref, base_ref):
    slots = pos_ref.shape[0]
    _, _, dest, sub, mask = place(pos_ref)
    same = iota((slots, slots), 0) == iota((slots, slots), 1)
    base = jnp.sum(jnp.where(same, dest + sub, 0), axis=1, keepdims=True)
    base_ref[...] = jnp.where(iota(base_ref.shape, 1) == 0, base, mask)


def project_body(
    odd_ref,
    recv_ref,
    embed_hbm_ref,
    weight_hbm_ref,
    emb_ref,
    tiles_ref,
    chunk_ref,
    pick_ref,
    embed_ref,
    weight_ref,
    embed_sem,
    weight_sem,
):
    embed_load = pltpu.make_async_copy(embed_hbm_ref, embed_ref, embed_sem)
    embed_load.start()
    columns = weight_ref.shape[2]
    weight_loads = [
        pltpu.make_async_copy(
            weight_hbm_ref.at[:, k * columns : (k + 1) * columns], weight_ref.at[k], weight_sem.at[k]
        )
        for k in range(2)
    ]
    for one in weight_loads:
        one.start()
    total = recv_ref.shape[0]
    senders = total // 8
    sel = hot(iota((senders, total), 1) == 8 * iota((senders, total), 0) + 3)
    half = recv_ref.shape[1]
    notes = dot(sel, recv_ref[:, half - 128 :])
    lane = iota((senders, 128), 1)
    lower = hot(iota((senders, senders), 0) > iota((senders, senders), 1))
    shared = (notes > 0.5) & (lane == 2)
    order = dot(lower, hot(shared)).astype(jnp.int32)
    other = shared & ((order & 1) != odd_ref[0])
    to_first = hot((iota((128, 128), 0) == 2) & (iota((128, 128), 1) == 0))
    other = dot(hot(other), to_first) > 0.5
    valid = (notes > 0.5) & ((lane & 3) == 0) & (lane < 12) & jnp.logical_not(other)
    cum = dot(lower, hot(valid))
    ones = jnp.where(valid, 1.0, 0.0)
    first = jnp.sum(jnp.where(lane == 0, ones, 0.0), axis=0, keepdims=True)
    first = jnp.sum(first, axis=1, keepdims=True)
    second = jnp.sum(jnp.where(lane == 4, ones, 0.0), axis=0, keepdims=True)
    second = jnp.sum(second, axis=1, keepdims=True)
    shift = jnp.where(lane >= 4, first, 0.0) + jnp.where(lane >= 8, second, 0.0)
    index = jnp.where(valid, cum + shift, -1.0)
    repeat = hot(iota((total, senders), 0) >> 3 == iota((total, senders), 1))
    index_all = dot(repeat, index.astype(HALFS))
    notes_all = dot(repeat, notes.astype(HALFS))
    turn = iota((total, 128), 0) & 7
    lanes = iota((total, 128), 1)
    slot = turn & 3
    here = 4 * jnp.where(slot < 3, slot, jnp.where(turn == 3, 0, 2))
    mine = lanes == here
    mine_low = lanes == here + 1
    spot = jnp.sum(jnp.where(mine, index_all + 1.0, 0.0), axis=1, keepdims=True) - 1.0
    middle = jnp.where((lanes == 4) & (turn == 3), index_all + 1.0, 0.0)
    middle = jnp.sum(middle, axis=1, keepdims=True) - 1.0
    high = jnp.sum(jnp.where(mine, notes_all, 0.0), axis=1, keepdims=True)
    low = jnp.sum(jnp.where(mine_low, notes_all, 0.0), axis=1, keepdims=True)
    match = spot.astype(jnp.int32) == lanes
    pick0 = hot(match & (turn < 3))
    pick1 = hot(match & (turn > 3) & (turn < 7))
    pick_rest = hot(match & (slot == 3))
    pick_middle = hot(middle.astype(jnp.int32) == lanes)
    slots_only = jnp.where(match & (slot < 3), 1.0, 0.0).reshape(senders // 2, 2, 8, 128)
    upper = iota((senders // 2, 8, 128), 1) < 4
    slots_only = jnp.where(upper, slots_only[:, 0], pltpu.roll(slots_only[:, 1], 4, 1))
    pick_ref[...] = slots_only.reshape(total // 2, 128).astype(HALFS)
    tiles_ref[:, :half] = dot(pick0, recv_ref[...], "tn").astype(HALFS)
    tiles_ref[:, half : 2 * half] = dot(pick1, recv_ref[...], "tn").astype(HALFS)
    rest = tiles_ref.shape[1] - 2 * half
    tail = dot(pick_rest, recv_ref[:, :rest], "tn")
    tail = tail + dot(pick_middle, recv_ref[:, rest : 2 * rest], "tn")
    tiles_ref[:, 2 * half :] = tail.astype(HALFS)
    embed_load.wait()
    emb_ref[...] = dot(tiles_ref[...], embed_ref[...]).astype(HALFS)
    info = jnp.where(lanes == 0, high, jnp.where(lanes == 1, low, 0.0)).astype(HALFS)
    info = dot(info, pick0, "tn")[: CHUNK_ROWS - WIDTH].astype(HALFS)
    heads = chunk_ref.shape[0]
    for head in range(heads):
        if head % (heads // 2) == 0:
            group = head // (heads // 2)
            weight_loads[group].wait()
            part = dot(emb_ref[...], weight_ref[group]).T
        first = (head % (heads // 2)) * WIDTH
        chunk_ref[head, :WIDTH, :] = part[first : first + WIDTH].astype(HALFS)
        chunk_ref[head, WIDTH:, :] = info


def dilated_body(phase_ref, chunk_ref, query_ref, far_ref, rows_ref, local_ref):
    blocks = chunk_ref.shape[0]
    total = jnp.zeros((WIDTH, query_ref.shape[1]), FLOATS)
    target = 8 * iota((query_ref.shape[1], 128), 0) + phase_ref[0]
    for block in range(blocks):
        lanes = slice(block * 128, (block + 1) * 128)
        part = chunk_ref[block, :WIDTH, :]
        info = chunk_ref[block, WIDTH:, :].astype(FLOATS)
        local = ((info[0:1] - 1.0) * 128.0 + info[1:2]).astype(jnp.int32)
        rows_ref[:, lanes] = part
        local_ref[:, lanes] = jnp.broadcast_to(local, (8, 128))
        total = total + dot(part, hot(target == local), "nt")
    query_ref[...] = total[:HEAD_SIZE].astype(HALFS)
    for copy in range(far_ref.shape[0]):
        far_ref[copy] = total[HEAD_SIZE:].astype(HALFS)


def near_attend(parts, grad, dilated):
    query = parts[:HEAD_SIZE]
    key = parts[HEAD_SIZE : 2 * HEAD_SIZE]
    value = parts[2 * HEAD_SIZE :]
    score = dot(key, query, "tn") * SCALE
    top = jnp.max(score, axis=0, keepdims=True)
    prob = jnp.exp(score - top)
    norm = 1.0 / jnp.sum(prob, axis=0, keepdims=True)
    prob = prob * jnp.where(dilated, 0.0, norm)
    dprob = dot(value, grad, "tn")
    delta = jnp.sum(prob * dprob, axis=0, keepdims=True)
    dscore = (prob * (dprob - delta)).astype(HALFS)
    return (
        dot(key, dscore) * SCALE,
        dot(query, dscore, "nt") * SCALE,
        dot(grad, prob.astype(HALFS), "nt"),
    )


def near_body(
    phase_ref,
    rows_ref,
    local_ref,
    grad_ref,
    query_ref,
    dilated_grad_ref,
    place_ref,
    near_ref,
    score_ref,
    dprob_ref,
):
    seg = grad_ref.shape[2]
    local = local_ref[0:1, :]
    dilated = (iota((1, seg), 1) & 7) == phase_ref[0]
    for slide in range(grad_ref.shape[0]):
        spots = slice(slide * seg, (slide + 1) * seg)
        order = hot(local == iota((seg, local.shape[1]), 0) + slide * seg)
        parts = dot(rows_ref[...], order, "nt").astype(HALFS)
        place_ref[:, spots] = parts
        if slide * seg < near_ref.shape[1]:
            grads = near_attend(parts, grad_ref[slide], dilated)
            for k in range(3):
                near_ref[k * HEAD_SIZE : (k + 1) * HEAD_SIZE, spots] = grads[k]
        pair, b = slide // 2, slide % 2
        lanes = slice(pair * 128, (pair + 1) * 128)
        part = slice(b * seg, (b + 1) * seg)
        same = iota((128, seg), 0) >> 6 == b
        key, value = parts[HEAD_SIZE : 2 * HEAD_SIZE], parts[2 * HEAD_SIZE :]
        score = dot(query_ref[:, lanes], key, "tn") * SCALE
        score_ref[pair, :, part] = jnp.where(same, score, -1e30)
        dprob_ref[pair, :, part] = dot(dilated_grad_ref[:, lanes], value, "tn")


def pick_body(phase_ref, grad_ref, out_ref):
    seg = grad_ref.shape[2]
    for pair in range(grad_ref.shape[0] // 2):
        grad = jnp.zeros((HEAD_SIZE, 128), FLOATS)
        for b in range(2):
            target = 8 * (iota((seg, 128), 1) - 64 * b) + phase_ref[0]
            grad = grad + dot(grad_ref[2 * pair + b], hot(iota((seg, 128), 0) == target))
        out_ref[:, pair * 128 : (pair + 1) * 128] = grad.astype(HALFS)


def far_body(
    query_ref, grad_ref, score_ref, dprob_ref, far_ref, out_ref, dscore_ref, prob_ref
):
    n = far_ref.shape[0]
    near = score_ref.shape[2]
    for pair in range(2):
        lanes = slice(pair * 128, (pair + 1) * 128)
        query = query_ref[:, lanes]
        grad = grad_ref[:, lanes]
        key = jnp.concatenate([far_ref[k, :HEAD_SIZE, lanes] for k in range(n)], axis=1)
        value = jnp.concatenate([far_ref[k, HEAD_SIZE:, lanes] for k in range(n)], axis=1)
        size = key.shape[1]
        same = (iota((128, size), 1) & 127) >> 6 == iota((128, size), 0) >> 6
        score = jnp.where(same, dot(query, key, "tn") * SCALE, -1e30)
        score = jnp.concatenate([score_ref[pair], score], axis=1)
        top = jnp.max(score, axis=1, keepdims=True)
        prob = jnp.exp(score - top)
        prob = prob * (1.0 / jnp.sum(prob, axis=1, keepdims=True))
        dprob = jnp.concatenate([dprob_ref[pair], dot(grad, value, "tn")], axis=1)
        delta = jnp.sum(prob * dprob, axis=1, keepdims=True)
        dscore = (prob * (dprob - delta)).astype(HALFS)
        prob = prob.astype(HALFS)
        dkey = dot(query, dscore[:, near:]) * SCALE
        dvalue = dot(grad, prob[:, near:])
        for k in range(n):
            part = slice(k * 128, (k + 1) * 128)
            out_ref[k, :HEAD_SIZE, lanes] = dkey[:, part].astype(HALFS)
            out_ref[k, HEAD_SIZE:, lanes] = dvalue[:, part].astype(HALFS)
        dscore_ref[pair] = dscore
        prob_ref[pair] = prob[:, :near]


def sum_body(
    phase_ref,
    all_grad_ref,
    query_ref,
    grad_ref,
    place_ref,
    far_ref,
    dscore_ref,
    prob_ref,
    near_ref,
    dquery_ref,
    sum_ref,
):
    near = place_ref.shape[1] // 2
    seg = near // 2
    dilated = (iota((1, seg), 1) & 7) == phase_ref[0]
    for pair in range(2):
        lanes = slice(pair * 128, (pair + 1) * 128)
        query = query_ref[:, lanes]
        grad = grad_ref[:, lanes]
        key = jnp.concatenate(
            [place_ref[HEAD_SIZE : 2 * HEAD_SIZE, pair * near : (pair + 1) * near]]
            + [far_ref[k, :HEAD_SIZE, lanes] for k in range(far_ref.shape[0])],
            axis=1,
        )
        dscore = dscore_ref[pair]
        dquery_ref[:, lanes] = (dot(key, dscore, "nt") * SCALE).astype(HALFS)
        dkey = dot(query, dscore[:, :near]) * SCALE
        dvalue = dot(grad, prob_ref[pair])
        for b in range(2):
            slide = 2 * pair + b
            spots = slice(slide * seg, (slide + 1) * seg)
            part = slice(b * seg, (b + 1) * seg)
            if pair == 0:
                grads = [near_ref[k * HEAD_SIZE : (k + 1) * HEAD_SIZE, spots] for k in range(3)]
            else:
                grads = near_attend(place_ref[:, spots], all_grad_ref[slide], dilated)
            sum_ref[:HEAD_SIZE, spots] = grads[0].astype(HALFS)
            sum_ref[HEAD_SIZE : 2 * HEAD_SIZE, spots] = (grads[1] + dkey[:, part]).astype(HALFS)
            sum_ref[2 * HEAD_SIZE :, spots] = (grads[2] + dvalue[:, part]).astype(HALFS)


def unplace_body(local_ref, sum_ref, out_ref):
    block = 512
    for start in range(0, out_ref.shape[1], block):
        lanes = slice(start, start + block)
        order = hot(local_ref[0:1, lanes] == iota((sum_ref.shape[1], block), 0))
        out_ref[:, lanes] = dot(sum_ref[...], order)


def finish_body(phase_ref, local_ref, main_ref, dquery_ref, far_ref, chunk_ref, rows_ref):
    far = far_ref[0].astype(FLOATS)
    for k in range(1, far_ref.shape[0]):
        far = far + far_ref[k].astype(FLOATS)
    sparse = jnp.concatenate([dquery_ref[...], far.astype(HALFS)], axis=0)
    local = local_ref[0:1, :]
    count = dquery_ref.shape[1]
    order = hot(local == 8 * iota((count, local.shape[1]), 0) + phase_ref[0])
    rows = (main_ref[...] + dot(sparse, order)).astype(HALFS)
    rows_ref[...] = rows
    for block in range(chunk_ref.shape[0] // WIDTH):
        chunk_ref[block * WIDTH : (block + 1) * WIDTH, :] = rows[
            :, block * 128 : (block + 1) * 128
        ]


def qkv_grad_body(core_ref, grad_ref, rows_ref, keep_ref, give_ref, all_ref):
    block = keep_ref.shape[1]
    part = dot(grad_ref[...], rows_ref[...]).T
    all_ref[...] = jnp.concatenate([part, jnp.zeros_like(part[:, : 256 - WIDTH])], axis=1)
    for chip in range(keep_ref.shape[0]):
        mine = pl.multiple_of((2 * chip + core_ref[0]) * block, block)
        other = pl.multiple_of((2 * chip + 1 - core_ref[0]) * block, block)
        keep_ref[chip] = all_ref[pl.ds(mine, block), :]
        give_ref[chip] = all_ref[pl.ds(other, block), :].astype(HALFS)


def merge_body(grad_ref, other_grad_ref, keep_ref, other_keep_ref, out_ref):
    rows, size = out_ref.shape[1] * 2 // 3, 128
    grad = jnp.concatenate([grad_ref[...], other_grad_ref[...]], axis=1)
    part = dot(grad, jnp.concatenate([keep_ref[...], other_keep_ref[...]], axis=0))
    part = part.astype(HALFS)
    columns = part.shape[0] // rows
    for block in range(out_ref.shape[0] // columns):
        left = block // 2 * 3 * size
        first = left if block % 2 == 0 else left + 2 * size
        other = left + size if block % 2 == 0 else left + size + 64
        for column in range(columns):
            here = part[column * rows : (column + 1) * rows]
            spot = block * columns + column
            out_ref[spot, :rows, :] = here[:, first : first + size]
            rest = here[:, other : other + 64]
            out_ref[spot, rows:, :] = jnp.concatenate(
                [rest[: rows // 2], rest[rows // 2 :]], axis=1
            )


def merge_qkv_body(chip_ref, keep_ref, given_ref, own_ref, *piece_refs):
    chips = keep_ref.shape[0]
    for k in range(chips):
        block = (chip_ref[0] + k) & (chips - 1)
        part = keep_ref[block] + given_ref[block].astype(FLOATS)
        if k == 0:
            own_ref[...] = part
        else:
            piece_refs[k - 1][...] = part.astype(HALFS)


def last_body(chip_ref, parts_ref, own_ref, *refs):
    piece_refs, embed_ref, qkv_ref = refs[:-2], refs[-2], refs[-1]
    total = parts_ref[0].astype(FLOATS)
    for k in range(1, parts_ref.shape[0]):
        total = total + parts_ref[k].astype(FLOATS)
    rest = jnp.concatenate([total[48:, :64], total[48:, 64:]], axis=0)
    even = jnp.concatenate([total[:48], rest], axis=1)
    odd = jnp.concatenate([rest, total[:48]], axis=1)
    embed_ref[...] = jnp.where((chip_ref[0] & 1) == 0, even, odd)
    qkv = own_ref[...]
    for ref in piece_refs:
        qkv = qkv + ref[...].astype(FLOATS)
    qkv_ref[...] = qkv.T[:WIDTH]


def load_body(_, *refs):
    count, sems = len(refs) // 2, refs[-1]
    loads = [
        pltpu.make_async_copy(refs[k], refs[count + k], sems.at[k]) for k in range(count)
    ]
    for load in loads:
        load.start()
    for load in loads:
        load.wait()


def load(after, *values):
    return call(
        load_body,
        [resident(value.shape) for value in values],
        [after, *values],
        anywhere=range(len(values) + 1),
        scratch_shapes=[pltpu.SemaphoreType.DMA((len(values),))],
    )


def back_body(rows_ref, weight_ref, pick_ref, grad_ref, back_ref):
    half = back_ref.shape[1]
    grad = dot(weight_ref[...], rows_ref[...]).astype(HALFS)
    grad_ref[...] = grad
    step = 128
    for start in range(0, pick_ref.shape[0], step):
        pick = pick_ref[start : start + step, :]
        both = interleave(dot(pick, grad[:half], "nt"), dot(pick, grad[half:], "nt"))
        back_ref[2 * start : 2 * (start + step), :] = both.astype(HALFS)


def collect_body(recv_ref, base_ref, out_ref):
    total, half = recv_ref.shape
    base, mask = base_ref[:, 0:1], base_ref[:, 1:2]
    rows = iota((base.shape[0], total), 1) & mask
    out_ref[:, :half] = dot(hot(rows == base), recv_ref[...]).astype(HALFS)
    out_ref[:, half:] = dot(hot(rows == base + 4), recv_ref[...]).astype(HALFS)


def per_device(tile_features, embed_weight, qkv_weight, positions, out_grad):
    n_slide = lax.axis_size("slide")
    n_tile = lax.axis_size("tile")
    devices = n_slide * n_tile
    every = ("slide", "tile")
    slots = tile_features.shape[0]
    slides, seg = out_grad.shape[0], out_grad.shape[1]
    wide = embed_weight.shape[1]
    half = wide // 2
    rows = slides * seg
    share = rows // n_tile
    row_here = lax.axis_index("slide")
    col_here = lax.axis_index("tile")
    phase = (col_here % n_slide).astype(jnp.int32).reshape(1)
    odd = (col_here % 2).astype(jnp.int32).reshape(1)
    core = row_here % 2
    tiles = tile_features.shape[1]
    packed = (tiles - 256) // 2

    with jax.named_scope("dispatch"):
        sent = call(
            dispatch_body,
            resident((devices * 8, packed)),
            [positions] + [tile_features] * 3,
            blocks={
                1: pl.BlockSpec((slots, packed), lambda i: (0, 0)),
                2: pl.BlockSpec((slots, packed), lambda i: (0, 1)),
                3: pl.BlockSpec((slots, 256), lambda i: (0, (tiles - 256) // 256)),
            },
            grid=(1,),
        )
        base = call(slots_body, resident((slots, 128), jnp.int32), [positions])
        arrived = lax.all_to_all(
            sent.reshape(devices, 8, packed), every, 0, 0, tiled=True
        ).reshape(devices * 8, packed)
    with jax.named_scope("project"):
        emb_rows, tile_rows, chunks, pick = call(
            project_body,
            [
                shaped((share, wide)),
                shaped((share, tiles)),
                resident((n_tile, CHUNK_ROWS, 128)),
                shaped((devices * 4, 128)),
            ],
            [odd, *stay(arrived), embed_weight, qkv_weight],
            smem=(0,),
            anywhere=(2, 3),
            scratch_shapes=[
                pltpu.VMEM(embed_weight.shape, HALFS),
                pltpu.VMEM((2, wide, qkv_weight.shape[1] // 2), HALFS),
                pltpu.SemaphoreType.DMA,
                pltpu.SemaphoreType.DMA((2,)),
            ],
        )
        chunks = lax.all_to_all(chunks, "tile", 0, 0, tiled=True)
    with jax.named_scope("swap_tiles"):
        swap = [(i, i ^ 1) for i in range(n_slide)]
        chips = n_slide // 2
        narrow = tiles // n_slide
        split = tile_rows.reshape(share, chips, 2, narrow)
        keep_cols = lax.dynamic_index_in_dim(split, core, 2, False).reshape(share, tiles // 2)
        give_cols = lax.dynamic_index_in_dim(split, 1 - core, 2, False).reshape(share, tiles // 2)
        got_cols = lax.ppermute(give_cols, "slide", swap)
    with jax.named_scope("dilated"):
        few = rows // n_slide
        query, far, head_rows, local = call(
            dilated_body,
            [
                resident((HEAD_SIZE, few)),
                resident((n_slide, 2 * HEAD_SIZE, few)),
                shaped((WIDTH, rows)),
                resident((8, rows), jnp.int32),
            ],
            [phase, *stay(chunks)],
            smem=(0,),
        )
        far = lax.all_to_all(far, "slide", 0, 0, tiled=True)
    with jax.named_scope("near"):
        grads = out_grad.transpose(0, 2, 1)
        dilated_grads = call(pick_body, resident((HEAD_SIZE, few)), [phase, grads], smem=(0,))
        placed, near, near_scores, near_dprobs = call(
            near_body,
            [resident((WIDTH, rows)), shaped((WIDTH, rows // 2), FLOATS)]
            + [resident((2, 128, rows // 2), FLOATS)] * 2,
            [phase, head_rows, *stay(local), grads, *stay(query, dilated_grads)],
            smem=(0,),
            cost_estimate=pl.CostEstimate(
                flops=8_000_000_000, bytes_accessed=8_000_000, transcendentals=1 << 20
            ),
        )
    with jax.named_scope("far"):
        far_grads, dscores, probs = call(
            far_body,
            [
                resident((n_slide, 2 * HEAD_SIZE, few)),
                shaped((2, 128, rows)),
                shaped((2, 128, rows // 2)),
            ],
            stay(query, dilated_grads, near_scores, near_dprobs, far),
        )
        far_grads = lax.all_to_all(far_grads, "slide", 0, 0, tiled=True)
    with jax.named_scope("unplace"):
        dquery, summed = call(
            sum_body,
            [resident((HEAD_SIZE, few)), resident((WIDTH, rows))],
            [
                phase,
                grads,
                *stay(query, dilated_grads, placed, far),
                dscores,
                probs,
                near,
            ],
            smem=(0,),
        )
        main = call(
            unplace_body,
            resident((WIDTH, rows), FLOATS),
            stay(local, summed),
            cost_estimate=pl.CostEstimate(
                flops=4_000_000_000, bytes_accessed=4_000_000, transcendentals=0
            ),
        )
        back_chunks, d_rows = call(
            finish_body,
            [resident((n_tile * WIDTH, 128)), shaped((WIDTH, rows))],
            [phase, *stay(local, main, dquery, far_grads)],
            smem=(0,),
        )
        back_rows = lax.all_to_all(
            back_chunks.reshape(n_tile, WIDTH, 128), "tile", 0, 0, tiled=True
        ).reshape(n_tile * WIDTH, 128)
    with jax.named_scope("qkv_grad"):
        all_rows = lax.all_gather(emb_rows, "tile", axis=0, tiled=True)
        block = wide // n_slide
        keep_qkv, give_qkv = call(
            qkv_grad_body,
            [shaped((chips, block, 256), FLOATS), shaped((chips, block, 256))],
            [core.astype(jnp.int32).reshape(1), d_rows, all_rows],
            smem=(0,),
            scratch_shapes=[pltpu.VMEM((wide, 256), FLOATS)],
        )
        chip = (row_here // 2).astype(jnp.int32).reshape(1)
        given_qkv = lax.ppermute(give_qkv, "slide", swap)
        own_qkv, *pieces = call(
            merge_qkv_body,
            [shaped((block, 256), FLOATS)] + [shaped((block, 256))] * (chips - 1),
            [chip, keep_qkv, given_qkv],
            smem=(0,),
        )
        pieces = [
            lax.ppermute(
                pieces[k - 1], "slide", [(i, (i + 2 * k) % n_slide) for i in range(n_slide)]
            )
            for k in range(1, chips)
        ]
    with jax.named_scope("tiles_grad"):
        (weight_here,) = load(d_rows, qkv_weight)
        grad_rows, back = call(
            back_body,
            [shaped((wide, share)), shaped((devices * 8, half))],
            [*stay(back_rows, weight_here), pick],
        )
        back = lax.all_to_all(
            back.reshape(devices, 8, half), every, 0, 0, tiled=True
        ).reshape(devices * 8, half)
        other_rows = lax.ppermute(grad_rows, "slide", swap)
        merged = call(
            merge_body,
            shaped((chips * n_tile, 72, 128)),
            [grad_rows, *stay(other_rows), keep_cols, got_cols],
        )
        merged, back = lax.optimization_barrier((merged, back))
    with jax.named_scope("collect"):
        d_embedded = call(collect_body, shaped((slots, wide)), stay(back, base))
    with jax.named_scope("embed_grad"):
        same_core = [
            [(2 * z + c) * n_tile + t for z in range(chips) for t in range(n_tile)]
            for c in range(2)
        ]
        parts = lax.all_to_all(
            merged, every, 0, 0, axis_index_groups=same_core, tiled=True
        )
        embed_grad, qkv_grad = call(
            last_body,
            [shaped((wide // n_tile, narrow), FLOATS), shaped((WIDTH, wide // n_slide), FLOATS)],
            [chip, *stay(parts), own_qkv, *pieces],
            smem=(0,),
        )
        embed_grad, qkv_grad = embed_grad.T, qkv_grad.T
    with jax.named_scope("feature_grad"):
        feature_grad = lax.dot_general(
            d_embedded, embed_weight, (((1,), (1,)), ((), ())), preferred_element_type=FLOATS
        ).astype(HALFS)
    return feature_grad, embed_grad, qkv_grad


def solution(mesh):
    placed = (P(("slide", "tile"), None), P(), P(), P(("slide", "tile")), P(None, "slide", "tile"))
    return jax.shard_map(
        per_device,
        mesh=mesh,
        in_specs=placed,
        out_specs=(P(("slide", "tile"), None), P("slide", "tile"), P("slide", "tile")),
        check_vma=False,
    )
```
